32 devices in a mesh: bx: 4 (over y, x), by: 2 (over core), bz: 4 (over z).
Axes of the slice: x: 2, y: 2, z: 4, core: 2. Of those that a mesh axis runs over, the one named last changes fastest.
Arguments:
- counts: bfloat16 [64, 64, 128, 128], P(('bx', 'by', 'bz')), may hold values from 0.099609375 to 10
- row_split: bfloat16 [64, 64, 128, 256], P(('bx', 'by', 'bz')), may hold values from 0 to 0.03125
- col_split: bfloat16 [64, 64, 128, 256], P(('bx', 'by', 'bz')), may hold values from 0 to 0.03125
- efficiency: bfloat16 [64, 128, 128], replicated, may hold values from 0.5 to 1.5
- lorentz: float32 [3600], replicated, may hold values from 0.3 to 3
- angles: int32 [64], P(('bx', 'by', 'bz')), may hold values from 0 to 3599
- tile_owner: int32 [4096, 1], P(('bx', 'by', 'bz')), may hold values from 0 to 31; in each aligned block of 128 rows (0 to 127, 128 to 255, ...) at most 16 rows name the same one
- tile_box: int32 [4096], P(('bx', 'by', 'bz')), may hold values from 0 to 511
Outputs:
- intensity: float32 [8, 8, 4, 64, 256], P('bx', 'by', 'bz')
The draws below stay inside these ranges and needn't reach their ends.
Inputs may be any that keep to these rules, and one draw needn't show every extreme that they name: `tile_owner`: among the 128 tiles of one device, no owner is named more than 16 times, a bound that some block reaches.
All inputs are finite; a program needn't handle non-finite values.
Results may differ from the reference program's by a relative error of at most 0.0003.
Values sent between devices are 32-bit elements; how exact they have to be, the bound alone decides.
No kernel may reach another device: no remote copies, remote signals or barrier semaphores. Data moves between devices by JAX's collectives and lax.ppermute only.
A program may use at most 128 MiB of HBM per device.

```python
import math
import jax
import jax.numpy as jnp
import numpy as np
from jax import lax

PIX = 128
VX = 8
VY = 8
VZ = 4
VOX = 256
GX = 8
GY = 8
GZ = 4
BOXX = 4
BOXY = 4
BOXZ = 4
BOX_BRICK = 64
TILE_FRAME = 64
NANG = 3600
FRAMES = 64
TILE_DEV = 128
TILES = 4096
LX = 2
LY = 4
LZ = 1
BOX_DEV = 512
CAP = 16
N_BY = 2
N_BZ = 4
DEVICES = 32


def place_ends(values, stream_key, low, largest):
    longest = values.shape.index(max(values.shape))
    spots = []
    for shift in (0, 1):
        where = [jax.random.randint(jax.random.fold_in(stream_key, axis), (), 0, length) for axis, length in enumerate(values.shape)]
        where[longest] = (where[longest] + shift) % values.shape[longest]
        spots.append(tuple(where))
    return values.at[spots[0]].set(low).at[spots[1]].set(largest)


def block_levels(rng, extent, cuts, smallest, top_value):
    gain, own = 1.0, jax.random.fold_in(rng, 6)
    for axis_at, blocks in cuts:
        steps = jnp.exp(jax.random.uniform(jax.random.fold_in(own, axis_at), (blocks,), jnp.float32, smallest / len(cuts), top_value / len(cuts)))
        gain = gain * jnp.repeat(steps, extent[axis_at] // blocks).reshape([-1 if axis == axis_at else 1 for axis in range(len(extent))])
    return gain


def deal_out(stream_key, own, number, rows, amount, top, limit, skew):
    ranking = jax.random.permutation(stream_key, amount)
    packed, usual = portions_of(amount, rows * top, limit, skew, True), portions_of(amount, rows * top, limit, skew, False)
    places = jnp.arange(amount)

    def named(lengths, rotation):
        used = int((lengths > 0).sum())
        fixed = max(1, used // 4)
        passed = fixed + (places - fixed + rotation * (used - fixed)) % max(1, amount - fixed)
        return jnp.zeros((amount,), jnp.int32).at[ranking[jnp.where(places < fixed, places, passed)]].set(jnp.asarray(lengths, jnp.int32))

    lengths = jnp.where(number % 4 == 0, named(packed, number // 4), named(usual, number - number // 4 - 1))
    mixed = jax.random.permutation(jax.random.fold_in(own, 3), amount)
    donor, receiver = mixed[0:amount // 2 * 2:2], mixed[1:amount // 2 * 2:2]
    slack = jnp.minimum(lengths[donor] - 1, limit - lengths[receiver]) // 2
    slack = jnp.where((donor == ranking[0]) | (receiver == ranking[0]) | (lengths[receiver] == 0), 0, jnp.maximum(slack, 0))
    passed = jax.random.randint(jax.random.fold_in(own, 4), (amount // 2,), 0, 1 << 20) % (slack + 1)
    lengths = lengths.at[donor].add(-passed).at[receiver].add(passed)
    labels = jnp.searchsorted(jnp.cumsum(lengths), jnp.arange(rows * top), side="right").astype(jnp.int32)
    table = labels.reshape(top, rows).T
    table = table[jax.random.permutation(jax.random.fold_in(own, 1), rows)]
    rotation = jax.random.randint(jax.random.fold_in(own, 2), (rows, 1), 0, top)
    return jnp.take_along_axis(table, (jnp.arange(top)[None, :] + rotation) % top, axis=1)


def portions_of(count, total, bound, skew, full):
    weights = [(1 << 20) // math.isqrt(grade ** skew) + 1 for grade in range(1, count + 1)]
    largest = bound if full else min(bound, max(-(-total // count), total * weights[0] // sum(weights)))
    least = 1 if total - largest >= count - 1 else 0
    given, spare = [largest] + [least] * (count - 1), total - largest - least * (count - 1)
    while spare > 0:
        candidates = [i for i in range(1, count) if given[i] < largest] or [i for i in range(1, count) if given[i] < bound]
        pool, left = sum([weights[i] for i in candidates]), spare
        for i in candidates:
            extra = min(bound - given[i], max(1, left * weights[i] // pool), spare)
            given[i] = given[i] + extra
            spare = spare - extra
    return np.array(given)


def setup_inputs(seed: int = 0) -> dict:
    streams_of = jax.random.split(jax.random.key(seed), 9)
    counts = jnp.clip(jnp.exp(math.log(10.0) - 4.609084 * jax.random.uniform(streams_of[0], (FRAMES, TILE_FRAME, PIX, PIX), jnp.float32) ** block_levels(streams_of[0], (FRAMES, TILE_FRAME, PIX, PIX), ((0, 32),), -0.2, 0.2)), 0.099609375, 10.0).astype(jnp.bfloat16)
    row_split = jnp.clip(0.03125 * jax.random.uniform(streams_of[1], (FRAMES, TILE_FRAME, PIX, VOX), jnp.float32) ** block_levels(streams_of[1], (FRAMES, TILE_FRAME, PIX, VOX), ((0, 32),), -0.2, 0.2), 0.0, 0.03125).astype(jnp.bfloat16)
    col_split = jnp.clip(0.03125 * jax.random.uniform(streams_of[2], (FRAMES, TILE_FRAME, PIX, VOX), jnp.float32) ** block_levels(streams_of[2], (FRAMES, TILE_FRAME, PIX, VOX), ((0, 32),), -0.2, 0.2), 0.0, 0.03125).astype(jnp.bfloat16)
    efficiency = jnp.clip(1.0 + 0.1 * jax.random.normal(streams_of[3], (TILE_FRAME, PIX, PIX), jnp.float32), 0.5, 1.5).astype(jnp.bfloat16)
    lorentz = jnp.clip(jnp.exp(jax.random.uniform(streams_of[4], (NANG,), jnp.float32, math.log(0.3), math.log(3.0))), 0.3, 3.0)
    angles = place_ends(jax.random.randint(streams_of[5], (FRAMES,), 0, NANG), jax.random.fold_in(streams_of[5], 1), 0, NANG - 1).astype(jnp.int32)
    tile_owner_keys = jax.random.split(jax.random.fold_in(streams_of[6], 1), TILES // TILE_DEV)
    tile_owner_turns = jax.random.permutation(jax.random.fold_in(streams_of[6], 3), TILES // TILE_DEV)
    tile_owner = jax.vmap(lambda own, number: deal_out(jax.random.fold_in(streams_of[6], 2), own, number, TILE_DEV, DEVICES, 1, CAP, 2))(tile_owner_keys, tile_owner_turns).reshape((TILES, 1))
    tile_box = place_ends(jax.random.randint(streams_of[7], (TILES,), 0, BOX_DEV), jax.random.fold_in(streams_of[7], 1), 0, BOX_DEV - 1).astype(jnp.int32)
    return dict(counts=counts, row_split=row_split, col_split=col_split, efficiency=efficiency, lorentz=lorentz, angles=angles, tile_owner=tile_owner, tile_box=tile_box)


def contributions(item, efficiency):
    frame_counts, frame_rows, frame_cols, frame_factor = item
    cols = frame_cols.astype(jnp.float32)
    rows = frame_rows.astype(jnp.float32)
    counted = jnp.einsum("tpq,tqv->tpv", frame_counts.astype(jnp.float32), cols)
    value = jnp.sum(rows * counted, axis=1) * frame_factor
    seen = jnp.einsum("tpq,tqv->tpv", efficiency.astype(jnp.float32), cols)
    weight = jnp.sum(rows * seen, axis=1)
    return jnp.stack([value, weight], axis=1)


def reference(counts, row_split, col_split, efficiency, lorentz, angles, tile_owner, tile_box):
    factor = lorentz[angles]
    payload = lax.map(lambda item: contributions(item, efficiency), (counts, row_split, col_split, factor))
    payload = payload.reshape(-1, 2, VOX)
    owner = tile_owner[:, 0]
    dev_x = owner // (N_BY * N_BZ)
    dev_y = (owner // N_BZ) % N_BY
    dev_z = owner % N_BZ
    brick_local = tile_box // BOX_BRICK
    box_index = tile_box % BOX_BRICK
    part_a = brick_local // (LY * LZ)
    part_b = (brick_local // LZ) % LY
    part_c = brick_local % LZ
    gx_index = dev_x * LX + part_a
    gy_index = dev_y * LY + part_b
    gz_index = dev_z * LZ + part_c
    flat = (((gx_index * GY + gy_index) * GZ + gz_index) * BOX_BRICK + box_index).astype(jnp.int32)
    sums = jax.ops.segment_sum(payload, flat, num_segments=GX * GY * GZ * BOX_BRICK)
    volume = sums.reshape(GX, GY, GZ, BOXX, BOXY, BOXZ, 2, VX, VY, VZ)
    volume = 0.5 * (volume + jnp.flip(volume, (0, 3, 7)))
    volume = 0.5 * (volume + jnp.flip(volume, (1, 4, 8)))
    volume = 0.5 * (volume + jnp.flip(volume, (2, 5, 9)))
    result = volume[:, :, :, :, :, :, 0] / jnp.maximum(volume[:, :, :, :, :, :, 1], 1.0)
    return result.reshape(GX, GY, GZ, BOX_BRICK, VOX)
```

```python
import functools

import jax
import jax.numpy as jnp
from jax import lax
from jax.experimental import pallas as pl
from jax.experimental.pallas import tpu as pltpu
from jax.sharding import PartitionSpec as P

VOX = 256
LANES = 128
GX = 8
GY = 8
GZ = 4
BOX_BRICK = 64
FLIP_VOX = (0b11100000, 0b00011100, 0b00000011)
FLIP_BOX = (0b110000, 0b001100, 0b000011)
AXES = ("bx", "by", "bz")
CHUNKS = 2
POSITIONS = 8
VMEM_LIMIT = 40 * 1024 * 1024


class Plan:
    def __init__(self, mesh):
        self.sx, self.sy, self.sz = (mesh.shape[name] for name in AXES)
        self.devices = self.sx * self.sy * self.sz
        lx, ly, lz = GX // self.sx, GY // self.sy, GZ // self.sz
        self.boxes = lx * ly * lz * BOX_BRICK
        self.share = self.boxes // 8
        self.flip_dev = ((self.sx - 1) * self.sy * self.sz, (self.sy - 1) * self.sz, self.sz - 1)
        self.half = (self.sx * self.sy * self.sz // 2, self.sy * self.sz // 2, self.sz // 2)
        self.flip_local = (
            (lx - 1) * ly * lz * BOX_BRICK + FLIP_BOX[0],
            (ly - 1) * lz * BOX_BRICK + FLIP_BOX[1],
            (lz - 1) * BOX_BRICK + FLIP_BOX[2],
        )

    def upper(self, device):
        return [(device & half) != 0 for half in self.half]

    def here(self):
        return (lax.axis_index("bx") * self.sy + lax.axis_index("by")) * self.sz + lax.axis_index("bz")


def masked(flags, masks):
    total = jnp.where(flags[0], masks[0], 0)
    for flag, mask in zip(flags[1:], masks[1:]):
        total = total ^ jnp.where(flag, mask, 0)
    return total


def lane_gather(values, index):
    return jnp.take_along_axis(values, index, axis=1, mode="promise_in_bounds")


def destination(plan, owner, box):
    upper = plan.upper(owner)
    local = box ^ masked(upper, plan.flip_local)
    part = local // plan.share
    row = local % plan.share
    holder = owner ^ masked(upper, plan.flip_dev)
    holder = holder ^ masked([(part & bit) != 0 for bit in (4, 2, 1)], plan.flip_dev)
    return holder * plan.share + row


def accumulate_kernel(plan, chunk, first, angles, lorentz, owner, box, counts, rows, cols, seen, out):
    frames, group = counts.shape[0], counts.shape[1]
    span = out.shape[0] // frames if not first else (out.shape[0] - 8) // frames
    step = pl.program_id(0)
    lanes = lax.broadcasted_iota(jnp.int32, (group, LANES), 1)
    for f in range(frames):
        factor = lorentz[angles[f]]
        value_rows, weight_rows = [], []
        for p in range(group):
            spread = rows[f, p].astype(jnp.float32)
            pixels = jnp.concatenate([counts[f, p], seen[p]], axis=0)
            both = jnp.dot(pixels, cols[f, p], preferred_element_type=jnp.float32)
            half = both.shape[0] // 2
            value_rows.append(jnp.sum(spread * both[:half], axis=0, keepdims=True))
            weight_rows.append(jnp.sum(spread * both[half:], axis=0, keepdims=True))
        value = jnp.concatenate(value_rows, axis=0) * factor
        weight = jnp.concatenate(weight_rows, axis=0)
        tile = f * (span * CHUNKS) + chunk * span + step * group
        upper = plan.upper(owner[pl.ds(pl.multiple_of(tile, group), group), :])
        mask = jnp.broadcast_to(masked(upper, FLIP_VOX), (group, LANES))
        index = lanes ^ (mask & (LANES - 1))
        swap = (mask & LANES) != 0
        pieces = []
        for item in (value, weight):
            low, high = item[:, :LANES], item[:, LANES:]
            pieces.append(lane_gather(jnp.where(swap, high, low), index))
            pieces.append(lane_gather(jnp.where(swap, low, high), index))
        place = pl.multiple_of(f * span + step * group, group)
        out[pl.ds(place, group), :] = jnp.concatenate(pieces, axis=1)
    if first:

        @pl.when(step == 0)
        def _():
            tiles = owner.shape[0]
            across = lax.broadcasted_iota(jnp.int32, (tiles, tiles), 1)
            down = lax.broadcasted_iota(jnp.int32, (tiles, tiles), 0)
            packed = frames * span
            tile = (across % packed) // span * (span * CHUNKS) + across // packed * span + across % span
            owner_row = jnp.sum(jnp.where(tile == down, owner[...], 0), axis=0, keepdims=True)
            box_rows = lane_gather(jnp.broadcast_to(box[...], (8, tiles)), tile[:8])
            ids = destination(plan, jnp.broadcast_to(owner_row, (8, tiles)), box_rows)
            start = frames * span
            out[start : start + 8, :] = jnp.zeros((8, out.shape[1]), jnp.float32)
            out[start : start + 8, :tiles] = ids.astype(jnp.float32)


def accumulate(plan, chunk, counts, row_split, col_split, efficiency, lorentz, angles, owner, box):
    frames, positions, pixels, _ = counts.shape
    span = positions // CHUNKS
    steps = span // POSITIONS
    first = chunk == 0
    out_rows = frames * span + (8 if first else 0)
    tiles = frames * positions
    at = lambda i: (0, chunk * steps + i, 0, 0)
    whole = lambda i: (0, 0)
    return pl.pallas_call(
        functools.partial(accumulate_kernel, plan, chunk, first),
        grid=(steps,),
        in_specs=[
            pl.BlockSpec(memory_space=pltpu.SMEM),
            pl.BlockSpec(memory_space=pltpu.SMEM),
            pl.BlockSpec((tiles, 1), whole),
            pl.BlockSpec((1, tiles), whole),
            pl.BlockSpec((frames, POSITIONS, pixels, pixels), at),
            pl.BlockSpec((frames, POSITIONS, pixels, VOX), at),
            pl.BlockSpec((frames, POSITIONS, pixels, VOX), at),
            pl.BlockSpec((POSITIONS, pixels, pixels), lambda i: (chunk * steps + i, 0, 0)),
        ],
        out_specs=pl.BlockSpec((out_rows, 2 * VOX), whole),
        out_shape=jax.ShapeDtypeStruct((out_rows, 2 * VOX), jnp.float32),
        compiler_params=pltpu.CompilerParams(vmem_limit_bytes=VMEM_LIMIT),
        cost_estimate=pl.CostEstimate(
            flops=4 * frames * span * pixels * pixels * VOX,
            bytes_accessed=span * pixels * (frames * 2 * (pixels + 2 * VOX) + 2 * pixels),
            transcendentals=0,
        ),
        name="tile_sums",
    )(angles, lorentz, owner, box, counts, row_split, col_split, efficiency)


def scatter_kernel(plan, sources, *refs):
    payloads, outs = refs[: sources * CHUNKS], refs[sources * CHUNKS :]
    packed = payloads[CHUNKS - 1].shape[0]
    tiles = packed * CHUNKS
    offset = plan.here() * plan.share
    part = plan.sz * plan.share
    for at in range(0, sources, 2):
        ids, data = [], []
        for source in range(at, min(at + 2, sources)):
            chunks = payloads[source * CHUNKS : (source + 1) * CHUNKS]
            ids.append(chunks[0][packed : packed + 1, :tiles].astype(jnp.int32) ^ offset)
            data += [ref[:packed, :] for ref in chunks]
        ids = jnp.concatenate(ids, axis=1)
        data = jnp.concatenate(data, axis=0)
        high = data.astype(jnp.bfloat16)
        low = (data - high.astype(jnp.float32)).astype(jnp.bfloat16)
        for number, out in enumerate(outs):
            boxes = lax.broadcasted_iota(jnp.int32, (part, ids.shape[1]), 0) + number * part
            pick = (boxes == ids).astype(jnp.float32).astype(jnp.bfloat16)
            total = jnp.dot(pick, high, preferred_element_type=jnp.float32)
            total = total + jnp.dot(pick, low, preferred_element_type=jnp.float32)
            if at == 0:
                out[...] = total
            else:
                out[...] += total


def split_kernel(count, *refs):
    inputs, outs = refs[:count], refs[count:]
    share = outs[0].shape[0]
    for number, out in enumerate(outs):
        span = slice(number * share, (number + 1) * share)
        total = inputs[0][span, :]
        for ref in inputs[1:]:
            total = total + ref[span, :]
        out[...] = total


def intensity_kernel(*refs):
    inputs, out = refs[:-1], refs[-1]
    total = inputs[0][...]
    for ref in inputs[1:]:
        total = total + ref[...]
    total = total * 0.125
    out[...] = total[:, :VOX] / jnp.maximum(total[:, VOX:], 1.0)


def unfold_kernel(plan, *refs):
    inputs, out = refs[:-1], refs[-1]
    upper = plan.upper(plan.here())
    own = masked(upper, (4, 2, 1))
    local = masked(upper, plan.flip_local)
    mask = masked(upper, FLIP_VOX)
    index = lax.broadcasted_iota(jnp.int32, (8, LANES), 1) ^ (mask & (LANES - 1))
    turn = lax.broadcasted_iota(jnp.int32, (8, LANES), 0) ^ (local & 7)
    swap = (mask & LANES) != 0
    for relative, ref in enumerate(inputs):
        base = (relative ^ own) * plan.share
        for group in range(plan.share // 8):
            rows = ref[group * 8 : group * 8 + 8, :]
            low, high = rows[:, :LANES], rows[:, LANES:]
            pieces = []
            for item in (jnp.where(swap, high, low), jnp.where(swap, low, high)):
                item = jnp.take_along_axis(item, turn, axis=0, mode="promise_in_bounds")
                pieces.append(lane_gather(item, index))
            place = (base + group * 8) ^ (local & ~7)
            out[pl.ds(pl.multiple_of(place, 8), 8), :] = jnp.concatenate(pieces, axis=1)


def small_call(kernel, shapes, name, *arrays):
    return pl.pallas_call(
        kernel,
        out_shape=[jax.ShapeDtypeStruct(shape, jnp.float32) for shape in shapes],
        compiler_params=pltpu.CompilerParams(vmem_limit_bytes=VMEM_LIMIT),
        name=name,
    )(*arrays)


def shards(plan, counts, row_split, col_split, efficiency, lorentz, angles, tile_owner, tile_box):
    def send(array, mask):
        pairs = [(i, i ^ mask) for i in range(plan.devices)]
        return lax.ppermute(array, AXES, pairs)

    row = plan.sy * plan.sz
    box = tile_box.reshape(1, -1)
    payloads = [[] for _ in range(plan.sx)]
    for chunk in range(CHUNKS):
        own = accumulate(plan, chunk, counts, row_split, col_split, efficiency, lorentz, angles, tile_owner, box)
        for source in range(plan.sx):
            payloads[source].append(own if source == 0 else send(own, source * row))
    flat = [array for chunks in payloads for array in chunks]
    width = 2 * VOX
    sums = small_call(
        functools.partial(scatter_kernel, plan, plan.sx),
        [(plan.sz * plan.share, width)] * plan.sy,
        "box_sums",
        *flat,
    )
    arrived = [sums[0]] + [send(sums[i], i * plan.sz) for i in range(1, plan.sy)]
    parts = small_call(
        functools.partial(split_kernel, plan.sy),
        [(plan.share, width)] * plan.sz,
        "core_sums",
        *arrived,
    )
    arrived = [parts[0]] + [send(parts[i], i) for i in range(1, plan.sz)]
    (own,) = small_call(intensity_kernel, [(plan.share, VOX)], "intensity", *arrived)
    flip_x, flip_y, flip_z = plan.flip_dev
    near = [own, send(own, flip_z), send(own, flip_x), send(own, flip_x ^ flip_z)]
    far = [send(array, flip_y) for array in near]
    ordered = [near[0], near[1], far[0], far[1], near[2], near[3], far[2], far[3]]
    (result,) = small_call(
        functools.partial(unfold_kernel, plan), [(plan.boxes, VOX)], "unfold", *ordered
    )
    return result.reshape(GX // plan.sx, GY // plan.sy, GZ // plan.sz, BOX_BRICK, VOX)


def solution(mesh):
    return jax.shard_map(
        functools.partial(shards, Plan(mesh)),
        mesh=mesh,
        in_specs=(
            P(AXES, None, None, None),
            P(AXES, None, None, None),
            P(AXES, None, None, None),
            P(),
            P(),
            P(AXES),
            P(AXES, None),
            P(AXES),
        ),
        out_specs=P("bx", "by", "bz", None, None),
        check_vma=False,
    )
```

```python
import functools

import jax
import jax.numpy as jnp
from jax import lax
from jax.experimental import pallas as pl
from jax.experimental.pallas import tpu as pltpu
from jax.sharding import PartitionSpec as P

VOX = 256
LANES = 128
GX = 8
GY = 8
GZ = 4
BOX_BRICK = 64
FLIP_VOX = (0b11100000, 0b00011100, 0b00000011)
FLIP_BOX = (0b110000, 0b001100, 0b000011)
AXES = ("bx", "by", "bz")
POSITIONS = 8
TILE_LIMIT = 56 * 1024 * 1024
VMEM_LIMIT = 24 * 1024 * 1024


class Plan:
    def __init__(self, mesh):
        self.sx, self.sy, self.sz = (mesh.shape[name] for name in AXES)
        self.devices = self.sx * self.sy * self.sz
        lx, ly, lz = GX // self.sx, GY // self.sy, GZ // self.sz
        self.boxes = lx * ly * lz * BOX_BRICK
        self.share = self.boxes // 8
        self.flip_dev = ((self.sx - 1) * self.sy * self.sz, (self.sy - 1) * self.sz, self.sz - 1)
        self.half = (self.sx * self.sy * self.sz // 2, self.sy * self.sz // 2, self.sz // 2)
        self.flip_local = (
            (lx - 1) * ly * lz * BOX_BRICK + FLIP_BOX[0],
            (ly - 1) * lz * BOX_BRICK + FLIP_BOX[1],
            (lz - 1) * BOX_BRICK + FLIP_BOX[2],
        )

    def upper(self, device):
        return [(device & half) != 0 for half in self.half]

    def orbit(self):
        x, y, z = self.flip_dev
        return [a ^ b ^ c for a in (0, x) for b in (0, y) for c in (0, z)]

    def here(self):
        return (lax.axis_index("bx") * self.sy + lax.axis_index("by")) * self.sz + lax.axis_index("bz")


def masked(flags, masks):
    total = jnp.where(flags[0], masks[0], 0)
    for flag, mask in zip(flags[1:], masks[1:]):
        total = total ^ jnp.where(flag, mask, 0)
    return total


def lane_gather(values, index):
    return jnp.take_along_axis(values, index, axis=1, mode="promise_in_bounds")


def destination(plan, owner, box):
    upper = plan.upper(owner)
    local = box ^ masked(upper, plan.flip_local)
    part = local // plan.share
    row = local % plan.share
    holder = owner ^ masked(upper, plan.flip_dev)
    holder = holder ^ masked([(part & bit) != 0 for bit in (4, 2, 1)], plan.flip_dev)
    return holder * plan.share + row


def accumulate_kernel(plan, angles, lorentz, owner, box, counts, rows, cols, seen, out, *scratch):
    arrays, sems = scratch[:4], scratch[4]
    frames, positions = counts.shape[0], counts.shape[1]
    blocks = positions // POSITIONS

    def copies(block):
        span = pl.ds(block * POSITIONS, POSITIONS)
        views = [(ref.at[:, span], held.at[:, span]) for ref, held in zip((counts, rows, cols), arrays)]
        views.append((seen.at[span], arrays[3].at[span]))
        return [pltpu.make_async_copy(src, dst, sems.at[block, i]) for i, (src, dst) in enumerate(views)]

    for block in range(blocks):
        for copy in copies(block):
            copy.start()

    tiles = frames * positions
    across = lax.broadcasted_iota(jnp.int32, (tiles, tiles), 1)
    down = lax.broadcasted_iota(jnp.int32, (tiles, tiles), 0)
    owner_row = jnp.sum(jnp.where(across == down, owner[...], 0), axis=0, keepdims=True)
    ids = destination(plan, owner_row, box[...])
    out[tiles : tiles + 8, :] = jnp.zeros((8, out.shape[1]), jnp.float32)
    out[tiles : tiles + 8, :tiles] = jnp.broadcast_to(ids.astype(jnp.float32), (8, tiles))

    @pl.loop(0, blocks)
    def _(block):
        for copy in copies(block):
            copy.wait()
        lanes = lax.broadcasted_iota(jnp.int32, (POSITIONS, LANES), 1)
        for f in range(frames):
            factor = lorentz[angles[f]]
            value_rows, weight_rows = [], []
            for p in range(POSITIONS):
                at = block * POSITIONS + p
                held_counts, held_rows, held_cols, held_seen = arrays
                spread = held_rows[f, at].astype(jnp.float32)
                pixels = jnp.concatenate([held_counts[f, at], held_seen[at]], axis=0)
                both = jnp.dot(pixels, held_cols[f, at], preferred_element_type=jnp.float32)
                half = both.shape[0] // 2
                value_rows.append(jnp.sum(spread * both[:half], axis=0, keepdims=True))
                weight_rows.append(jnp.sum(spread * both[half:], axis=0, keepdims=True))
            value = jnp.concatenate(value_rows, axis=0) * factor
            weight = jnp.concatenate(weight_rows, axis=0)
            place = pl.ds(pl.multiple_of(f * positions + block * POSITIONS, POSITIONS), POSITIONS)
            mask = jnp.broadcast_to(masked(plan.upper(owner[place, :]), FLIP_VOX), (POSITIONS, LANES))
            index = lanes ^ (mask & (LANES - 1))
            swap = (mask & LANES) != 0
            pieces = []
            for item in (value, weight):
                low, high = item[:, :LANES], item[:, LANES:]
                pieces.append(lane_gather(jnp.where(swap, high, low), index))
                pieces.append(lane_gather(jnp.where(swap, low, high), index))
            out[place, :] = jnp.concatenate(pieces, axis=1)


def accumulate(plan, counts, row_split, col_split, efficiency, lorentz, angles, owner, box):
    frames, positions, pixels, _ = counts.shape
    tiles = frames * positions
    arrays = (counts, row_split, col_split, efficiency)
    return pl.pallas_call(
        functools.partial(accumulate_kernel, plan),
        in_specs=[pl.BlockSpec(memory_space=pltpu.SMEM)] * 2
        + [pl.BlockSpec(memory_space=pltpu.VMEM)] * 2
        + [pl.BlockSpec(memory_space=pl.ANY)] * 4,
        out_specs=pl.BlockSpec(memory_space=pltpu.VMEM),
        out_shape=jax.ShapeDtypeStruct((tiles + 8, 2 * VOX), jnp.float32),
        scratch_shapes=[pltpu.VMEM(array.shape, array.dtype) for array in arrays]
        + [pltpu.SemaphoreType.DMA((positions // POSITIONS, 4))],
        compiler_params=pltpu.CompilerParams(vmem_limit_bytes=TILE_LIMIT),
        cost_estimate=pl.CostEstimate(
            flops=4 * tiles * pixels * pixels * VOX,
            bytes_accessed=sum(array.size * 2 for array in arrays),
            transcendentals=0,
        ),
        name="tile_sums",
    )(angles, lorentz, owner, box, *arrays)


def scatter_kernel(plan, offset_of, payload, out):
    tiles = LANES
    packed = tiles + 8
    sources = payload.shape[0] // packed
    offset = offset_of()
    for at in range(0, sources, 2):
        starts = [source * packed for source in range(at, min(at + 2, sources))]
        ids = [payload[start + tiles : start + tiles + 1, :tiles].astype(jnp.int32) - offset for start in starts]
        ids = jnp.concatenate(ids, axis=1)
        data = jnp.concatenate([payload[start : start + tiles, :] for start in starts], axis=0)
        high = data.astype(jnp.bfloat16)
        low = (data - high.astype(jnp.float32)).astype(jnp.bfloat16)
        boxes = lax.broadcasted_iota(jnp.int32, (out.shape[0], ids.shape[1]), 0)
        pick = (boxes == ids).astype(jnp.float32).astype(jnp.bfloat16)
        total = jnp.dot(pick, high, preferred_element_type=jnp.float32)
        total = total + jnp.dot(pick, low, preferred_element_type=jnp.float32)
        if at == 0:
            out[...] = total
        else:
            out[...] += total


def intensity_kernel(*refs):
    inputs, out = refs[:-1], refs[-1]
    total = inputs[0][...]
    for ref in inputs[1:]:
        total = total + ref[...]
    total = total * 0.125
    out[...] = total[:, :VOX] / jnp.maximum(total[:, VOX:], 1.0)


def unfold_kernel(plan, parts, out):
    upper = plan.upper(plan.here())
    local = masked(upper, plan.flip_local)
    mask = masked(upper, FLIP_VOX)
    index = lax.broadcasted_iota(jnp.int32, (8, LANES), 1) ^ (mask & (LANES - 1))
    turn = lax.broadcasted_iota(jnp.int32, (8, LANES), 0) ^ (local & 7)
    swap = (mask & LANES) != 0
    for start in range(0, plan.boxes, 8):
        rows = parts[start : start + 8, :]
        low, high = rows[:, :LANES], rows[:, LANES:]
        pieces = []
        for item in (jnp.where(swap, high, low), jnp.where(swap, low, high)):
            item = jnp.take_along_axis(item, turn, axis=0, mode="promise_in_bounds")
            pieces.append(lane_gather(item, index))
        place = start ^ (local & ~7)
        out[pl.ds(pl.multiple_of(place, 8), 8), :] = jnp.concatenate(pieces, axis=1)


def small_call(kernel, shapes, name, *arrays):
    return pl.pallas_call(
        kernel,
        out_shape=[jax.ShapeDtypeStruct(shape, jnp.float32) for shape in shapes],
        compiler_params=pltpu.CompilerParams(vmem_limit_bytes=VMEM_LIMIT),
        name=name,
    )(*arrays)


def shards(plan, counts, row_split, col_split, efficiency, lorentz, angles, tile_owner, tile_box):
    box = tile_box.reshape(1, -1)
    own = accumulate(plan, counts, row_split, col_split, efficiency, lorentz, angles, tile_owner, box)
    payload = lax.all_gather(own, ("bx", "by"), axis=0, tiled=True)
    column = lambda: (plan.here() // plan.sz) * plan.sz * plan.share
    (sums,) = small_call(
        functools.partial(scatter_kernel, plan, column), [(plan.sz * plan.share, 2 * VOX)], "box_sums", payload
    )
    total = lax.psum_scatter(sums, "bz", scatter_dimension=0, tiled=True)
    (part,) = small_call(intensity_kernel, [(plan.share, VOX)], "intensity", total)
    groups = [
        [base ^ mask for mask in plan.orbit()]
        for base in range(plan.devices)
        if not any(base & half for half in plan.half)
    ]
    parts = lax.all_gather(part, AXES, axis=0, tiled=True, axis_index_groups=groups)
    (result,) = small_call(functools.partial(unfold_kernel, plan), [(plan.boxes, VOX)], "unfold", parts)
    return result.reshape(GX // plan.sx, GY // plan.sy, GZ // plan.sz, BOX_BRICK, VOX)


def solution(mesh):
    return jax.shard_map(
        functools.partial(shards, Plan(mesh)),
        mesh=mesh,
        in_specs=(
            P(AXES, None, None, None),
            P(AXES, None, None, None),
            P(AXES, None, None, None),
            P(),
            P(),
            P(AXES),
            P(AXES, None),
            P(AXES),
        ),
        out_specs=P("bx", "by", "bz", None, None),
        check_vma=False,
    )
```

```python
import functools

import jax
import jax.numpy as jnp
from jax import lax
from jax.experimental import pallas as pl
from jax.experimental.pallas import tpu as pltpu
from jax.sharding import PartitionSpec as P

VOX = 256
LANES = 128
GX = 8
GY = 8
GZ = 4
BOX_BRICK = 64
FLIP_VOX = (0b11100000, 0b00011100, 0b00000011)
FLIP_BOX = (0b110000, 0b001100, 0b000011)
AXES = ("bx", "by", "bz")
POSITIONS = 8
TILE_LIMIT = 56 * 1024 * 1024
VMEM_LIMIT = 24 * 1024 * 1024


class Plan:
    def __init__(self, mesh):
        self.sx, self.sy, self.sz = (mesh.shape[name] for name in AXES)
        self.devices = self.sx * self.sy * self.sz
        lx, ly, lz = GX // self.sx, GY // self.sy, GZ // self.sz
        self.boxes = lx * ly * lz * BOX_BRICK
        self.share = self.boxes // 8
        self.flip_dev = ((self.sx - 1) * self.sy * self.sz, (self.sy - 1) * self.sz, self.sz - 1)
        self.half = (self.sx * self.sy * self.sz // 2, self.sy * self.sz // 2, self.sz // 2)
        self.flip_local = (
            (lx - 1) * ly * lz * BOX_BRICK + FLIP_BOX[0],
            (ly - 1) * lz * BOX_BRICK + FLIP_BOX[1],
            (lz - 1) * BOX_BRICK + FLIP_BOX[2],
        )

    def upper(self, device):
        return [(device & half) != 0 for half in self.half]

    def stages(self):
        along_y = [self.sz << bit for bit in range(self.sy.bit_length() - 1)]
        return along_y + [1 << bit for bit in range(self.sz.bit_length() - 1)]

    def stage_order(self, place):
        stages = self.stages()
        kept = place & ~((self.sy * self.sz - 1) * self.share)
        for number, mask in enumerate(stages):
            bit = self.share << (len(stages) - 1 - number)
            kept = kept | jnp.where((place & (mask * self.share)) != 0, bit, 0)
        return kept

    def here(self):
        return (lax.axis_index("bx") * self.sy + lax.axis_index("by")) * self.sz + lax.axis_index("bz")


def masked(flags, masks):
    total = jnp.where(flags[0], masks[0], 0)
    for flag, mask in zip(flags[1:], masks[1:]):
        total = total ^ jnp.where(flag, mask, 0)
    return total


def lane_gather(values, index):
    return jnp.take_along_axis(values, index, axis=1, mode="promise_in_bounds")


def destination(plan, owner, box):
    upper = plan.upper(owner)
    local = box ^ masked(upper, plan.flip_local)
    part = local // plan.share
    row = local % plan.share
    holder = owner ^ masked(upper, plan.flip_dev)
    holder = holder ^ masked([(part & bit) != 0 for bit in (4, 2, 1)], plan.flip_dev)
    return holder * plan.share + row


def accumulate_kernel(plan, angles, lorentz, owner, box, counts, rows, cols, seen, out, *scratch):
    arrays, sems, turned = scratch[:4], scratch[4], scratch[5]
    frames, positions = counts.shape[0], counts.shape[1]
    blocks = positions // POSITIONS

    def copies(block):
        span = pl.ds(block * POSITIONS, POSITIONS)
        views = [(ref.at[:, span], held.at[:, span]) for ref, held in zip((counts, rows, cols), arrays)]
        views.append((seen.at[span], arrays[3].at[span]))
        return [pltpu.make_async_copy(src, dst, sems.at[block, i]) for i, (src, dst) in enumerate(views)]

    for block in range(blocks):
        for copy in copies(block):
            copy.start()

    tiles = frames * positions
    across = lax.broadcasted_iota(jnp.int32, (tiles, tiles), 1)
    down = lax.broadcasted_iota(jnp.int32, (tiles, tiles), 0)
    flips = masked(plan.upper(owner[...]), FLIP_VOX)
    turned[...] = jnp.sum(jnp.where(across == down, flips, 0), axis=1, keepdims=True)
    ids = destination(plan, owner[...], box[...])
    out[tiles : tiles + 8, :] = jnp.zeros((8, out.shape[1]), jnp.float32)
    out[tiles : tiles + 8, :tiles] = jnp.broadcast_to(ids.astype(jnp.float32), (8, tiles))

    @pl.loop(0, blocks)
    def _(block):
        for copy in copies(block):
            copy.wait()
        held_counts, held_rows, held_cols, held_seen = arrays
        lanes = lax.broadcasted_iota(jnp.int32, (POSITIONS, LANES), 1)
        value_rows = [[] for _ in range(frames)]
        weight_rows = [[] for _ in range(frames)]
        for p in range(POSITIONS):
            at = block * POSITIONS + p
            cols_all = jnp.concatenate([held_cols[f, at] for f in range(frames)], axis=1)
            seen_all = jnp.dot(held_seen[at], cols_all, preferred_element_type=jnp.float32)
            for f in range(frames):
                spread = held_rows[f, at].astype(jnp.float32)
                counted = jnp.dot(held_counts[f, at], held_cols[f, at], preferred_element_type=jnp.float32)
                value_rows[f].append(jnp.sum(spread * counted, axis=0, keepdims=True))
                observed = seen_all[:, f * VOX : (f + 1) * VOX]
                weight_rows[f].append(jnp.sum(spread * observed, axis=0, keepdims=True))
        for f in range(frames):
            value = jnp.concatenate(value_rows[f], axis=0) * lorentz[angles[f]]
            weight = jnp.concatenate(weight_rows[f], axis=0)
            place = pl.ds(pl.multiple_of(f * positions + block * POSITIONS, POSITIONS), POSITIONS)
            mask = jnp.broadcast_to(turned[place, :], (POSITIONS, LANES))
            index = lanes ^ (mask & (LANES - 1))
            swap = (mask & LANES) != 0
            pieces = []
            for item in (value, weight):
                low, high = item[:, :LANES], item[:, LANES:]
                pieces.append(lane_gather(jnp.where(swap, high, low), index))
                pieces.append(lane_gather(jnp.where(swap, low, high), index))
            out[place, :] = jnp.concatenate(pieces, axis=1)


def accumulate(plan, counts, row_split, col_split, efficiency, lorentz, angles, owner, box):
    frames, positions, pixels, _ = counts.shape
    tiles = frames * positions
    arrays = (counts, row_split, col_split, efficiency)
    return pl.pallas_call(
        functools.partial(accumulate_kernel, plan),
        in_specs=[pl.BlockSpec(memory_space=pltpu.SMEM)] * 2
        + [pl.BlockSpec(memory_space=pltpu.VMEM)] * 2
        + [pl.BlockSpec(memory_space=pl.ANY)] * 4,
        out_specs=pl.BlockSpec(memory_space=pltpu.VMEM),
        out_shape=jax.ShapeDtypeStruct((tiles + 8, 2 * VOX), jnp.float32),
        scratch_shapes=[pltpu.VMEM(array.shape, array.dtype) for array in arrays]
        + [pltpu.SemaphoreType.DMA((positions // POSITIONS, 4)), pltpu.VMEM((tiles, 1), jnp.int32)],
        compiler_params=pltpu.CompilerParams(vmem_limit_bytes=TILE_LIMIT),
        cost_estimate=pl.CostEstimate(
            flops=4 * tiles * pixels * pixels * VOX,
            bytes_accessed=sum(array.size * 2 for array in arrays),
            transcendentals=0,
        ),
        name="tile_sums",
    )(angles, lorentz, owner, box, *arrays)


def scatter_kernel(plan, payload_a, payload_b, *outs):
    tiles = LANES
    packed = tiles + 8
    offset = plan.here() * plan.share
    blocks = [ref.at[pl.ds(start, packed)] for ref in (payload_a, payload_b) for start in range(0, ref.shape[0], packed)]
    for at in range(0, len(blocks), 2):
        pair = blocks[at : at + 2]
        ids = jnp.concatenate([ref[tiles : tiles + 1, :tiles] for ref in pair], axis=1)
        ids = plan.stage_order(ids.astype(jnp.int32) ^ offset)
        data = jnp.concatenate([ref[:tiles, :] for ref in pair], axis=0)
        high = data.astype(jnp.bfloat16)
        low = (data - high.astype(jnp.float32)).astype(jnp.bfloat16)
        start = 0
        for out in outs:
            boxes = lax.broadcasted_iota(jnp.int32, (out.shape[0], ids.shape[1]), 0) + start
            start += out.shape[0]
            pick = (boxes == ids).astype(jnp.float32).astype(jnp.bfloat16)
            total = jnp.dot(pick, high, preferred_element_type=jnp.float32)
            total = total + jnp.dot(pick, low, preferred_element_type=jnp.float32)
            if at == 0:
                out[...] = total
            else:
                out[...] += total


def join_kernel(first, second, out):
    half = first.shape[0]
    out[:half, :] = first[...]
    out[half:, :] = second[...]


def halve_kernel(first, second, keep, give):
    half = keep.shape[0]
    keep[...] = first[:half, :] + second[:half, :]
    give[...] = first[half:, :] + second[half:, :]


def intensity_kernel(*refs):
    inputs, out = refs[:-1], refs[-1]
    total = inputs[0][...]
    for ref in inputs[1:]:
        total = total + ref[...]
    total = total * 0.125
    out[...] = total[:, :VOX] / jnp.maximum(total[:, VOX:], 1.0)


def unfold_kernel(plan, near, far, out):
    upper = plan.upper(plan.here())
    own = masked(upper, (4, 2, 1))
    local = masked(upper, plan.flip_local)
    mask = masked(upper, FLIP_VOX)
    index = lax.broadcasted_iota(jnp.int32, (8, LANES), 1) ^ (mask & (LANES - 1))
    turn = lax.broadcasted_iota(jnp.int32, (8, LANES), 0) ^ (local & 7)
    swap = (mask & LANES) != 0
    odd = lax.axis_index("by") & 1
    orders = ((0, 1, 4, 5), (0, 4, 1, 5))
    for ref, other in ((near, 0), (far, 1)):
        for place in range(4):
            codes = [orders[other][place], orders[1 - other][place]]
            code = jnp.where(odd == 0, codes[0], codes[1]) + 2 * other
            base = (code ^ own) * plan.share
            for group in range(0, plan.share, 8):
                start = place * plan.share + group
                rows = ref[start : start + 8, :]
                low, high = rows[:, :LANES], rows[:, LANES:]
                pieces = []
                for item in (jnp.where(swap, high, low), jnp.where(swap, low, high)):
                    item = jnp.take_along_axis(item, turn, axis=0, mode="promise_in_bounds")
                    pieces.append(lane_gather(item, index))
                target = (base + group) ^ (local & ~7)
                out[pl.ds(pl.multiple_of(target, 8), 8), :] = jnp.concatenate(pieces, axis=1)


def small_call(kernel, shapes, name, *arrays):
    return pl.pallas_call(
        kernel,
        out_shape=[jax.ShapeDtypeStruct(shape, jnp.float32) for shape in shapes],
        compiler_params=pltpu.CompilerParams(vmem_limit_bytes=VMEM_LIMIT),
        name=name,
    )(*arrays)


def shards(plan, counts, row_split, col_split, efficiency, lorentz, angles, tile_owner, tile_box):
    def swap(array, even, odd):
        pairs = [(i, i ^ (odd if i // plan.sz % 2 else even)) for i in range(plan.devices)]
        return lax.ppermute(array, AXES, pairs)

    def join(first, second):
        rows, width = first.shape
        return small_call(join_kernel, [(2 * rows, width)], "join", first, second)[0]

    row = plan.sy * plan.sz
    owner = tile_owner.reshape(1, -1)
    box = tile_box.reshape(1, -1)
    own = accumulate(plan, counts, row_split, col_split, efficiency, lorentz, angles, owner, box)
    pair = join(own, swap(own, row, 2 * row))
    other = swap(pair, 2 * row, row)
    shape = (row * plan.share // 2, 2 * VOX)
    keep, give = small_call(functools.partial(scatter_kernel, plan), [shape] * 2, "box_sums", pair, other)
    for mask in plan.stages()[:-1]:
        shape = (keep.shape[0] // 2, 2 * VOX)
        keep, give = small_call(halve_kernel, [shape] * 2, "halve", keep, swap(give, mask, mask))
    last = swap(give, plan.stages()[-1], plan.stages()[-1])
    (part,) = small_call(intensity_kernel, [(plan.share, VOX)], "intensity", keep, last)
    flip_x, flip_y, flip_z = plan.flip_dev
    pair = join(part, swap(part, flip_z, flip_x))
    near = join(pair, swap(pair, flip_x, flip_z))
    far = swap(near, flip_y, flip_y)
    (result,) = small_call(functools.partial(unfold_kernel, plan), [(plan.boxes, VOX)], "unfold", near, far)
    return result.reshape(GX // plan.sx, GY // plan.sy, GZ // plan.sz, BOX_BRICK, VOX)


def solution(mesh):
    return jax.shard_map(
        functools.partial(shards, Plan(mesh)),
        mesh=mesh,
        in_specs=(
            P(AXES, None, None, None),
            P(AXES, None, None, None),
            P(AXES, None, None, None),
            P(),
            P(),
            P(AXES),
            P(AXES, None),
            P(AXES),
        ),
        out_specs=P("bx", "by", "bz", None, None),
        check_vma=False,
    )
```

```python
import functools

import jax
import jax.numpy as jnp
from jax import lax
from jax.experimental import pallas as pl
from jax.experimental.pallas import tpu as pltpu
from jax.sharding import PartitionSpec as P

VOX = 256
LANES = 128
GX = 8
GY = 8
GZ = 4
BOX_BRICK = 64
FLIP_VOX = (0b11100000, 0b00011100, 0b00000011)
FLIP_BOX = (0b110000, 0b001100, 0b000011)
AXES = ("bx", "by", "bz")
POSITIONS = 8
TILE_LIMIT = 56 * 1024 * 1024
VMEM_LIMIT = 24 * 1024 * 1024


class Plan:
    def __init__(self, mesh):
        self.sx, self.sy, self.sz = (mesh.shape[name] for name in AXES)
        self.devices = self.sx * self.sy * self.sz
        lx, ly, lz = GX // self.sx, GY // self.sy, GZ // self.sz
        self.boxes = lx * ly * lz * BOX_BRICK
        self.share = self.boxes // 8
        self.flip_dev = ((self.sx - 1) * self.sy * self.sz, (self.sy - 1) * self.sz, self.sz - 1)
        self.half = (self.sx * self.sy * self.sz // 2, self.sy * self.sz // 2, self.sz // 2)
        self.flip_local = (
            (lx - 1) * ly * lz * BOX_BRICK + FLIP_BOX[0],
            (ly - 1) * lz * BOX_BRICK + FLIP_BOX[1],
            (lz - 1) * BOX_BRICK + FLIP_BOX[2],
        )

    def upper(self, device):
        return [(device & half) != 0 for half in self.half]

    def here(self):
        return (lax.axis_index("bx") * self.sy + lax.axis_index("by")) * self.sz + lax.axis_index("bz")


def masked(flags, masks):
    total = jnp.where(flags[0], masks[0], 0)
    for flag, mask in zip(flags[1:], masks[1:]):
        total = total ^ jnp.where(flag, mask, 0)
    return total


def lane_gather(values, index):
    return jnp.take_along_axis(values, index, axis=1, mode="promise_in_bounds")


def destination(plan, owner, box):
    upper = plan.upper(owner)
    local = box ^ masked(upper, plan.flip_local)
    part = local // plan.share
    row = local % plan.share
    holder = owner ^ masked(upper, plan.flip_dev)
    holder = holder ^ masked([(part & bit) != 0 for bit in (4, 2, 1)], plan.flip_dev)
    return holder * plan.share + row


def accumulate_kernel(plan, angles, lorentz, owner, box, counts, rows, cols, seen, out, *scratch):
    arrays, sems, turned = scratch[:4], scratch[4], scratch[5]
    frames, positions = counts.shape[0], counts.shape[1]
    blocks = positions // POSITIONS

    def copies(block):
        span = pl.ds(block * POSITIONS, POSITIONS)
        views = [(ref.at[:, span], held.at[:, span]) for ref, held in zip((counts, rows, cols), arrays)]
        views.append((seen.at[span], arrays[3].at[span]))
        return [pltpu.make_async_copy(src, dst, sems.at[block, i]) for i, (src, dst) in enumerate(views)]

    for block in range(blocks):
        for copy in copies(block):
            copy.start()

    tiles = frames * positions
    across = lax.broadcasted_iota(jnp.int32, (tiles, tiles), 1)
    down = lax.broadcasted_iota(jnp.int32, (tiles, tiles), 0)
    flips = masked(plan.upper(owner[...]), FLIP_VOX)
    turned[...] = jnp.sum(jnp.where(across == down, flips, 0), axis=1, keepdims=True)
    ids = destination(plan, owner[...], box[...])
    packed = tiles + 8
    for copy in range(plan.sx):
        start = copy * packed + tiles
        out[start : start + 8, :] = jnp.zeros((8, out.shape[1]), jnp.float32)
        out[start : start + 8, :tiles] = jnp.broadcast_to(ids.astype(jnp.float32), (8, tiles))

    @pl.loop(0, blocks)
    def _(block):
        for copy in copies(block):
            copy.wait()
        held_counts, held_rows, held_cols, held_seen = arrays
        lanes = lax.broadcasted_iota(jnp.int32, (POSITIONS, LANES), 1)
        value_rows = [[] for _ in range(frames)]
        weight_rows = [[] for _ in range(frames)]
        for p in range(POSITIONS):
            at = block * POSITIONS + p
            cols_all = jnp.concatenate([held_cols[f, at] for f in range(frames)], axis=1)
            seen_all = jnp.dot(held_seen[at], cols_all, preferred_element_type=jnp.float32)
            for f in range(frames):
                spread = held_rows[f, at].astype(jnp.float32)
                counted = jnp.dot(held_counts[f, at], held_cols[f, at], preferred_element_type=jnp.float32)
                value_rows[f].append(jnp.sum(spread * counted, axis=0, keepdims=True))
                observed = seen_all[:, f * VOX : (f + 1) * VOX]
                weight_rows[f].append(jnp.sum(spread * observed, axis=0, keepdims=True))
        for f in range(frames):
            value = jnp.concatenate(value_rows[f], axis=0) * lorentz[angles[f]]
            weight = jnp.concatenate(weight_rows[f], axis=0)
            place = pl.ds(pl.multiple_of(f * positions + block * POSITIONS, POSITIONS), POSITIONS)
            mask = jnp.broadcast_to(turned[place, :], (POSITIONS, LANES))
            index = lanes ^ (mask & (LANES - 1))
            swap = (mask & LANES) != 0
            pieces = []
            for item in (value, weight):
                low, high = item[:, :LANES], item[:, LANES:]
                pieces.append(lane_gather(jnp.where(swap, high, low), index))
                pieces.append(lane_gather(jnp.where(swap, low, high), index))
            turned_rows = jnp.concatenate(pieces, axis=1)
            for copy in range(plan.sx):
                target = copy * packed + f * positions + block * POSITIONS
                out[pl.ds(pl.multiple_of(target, POSITIONS), POSITIONS), :] = turned_rows


def accumulate(plan, counts, row_split, col_split, efficiency, lorentz, angles, owner, box):
    frames, positions, pixels, _ = counts.shape
    tiles = frames * positions
    arrays = (counts, row_split, col_split, efficiency)
    return pl.pallas_call(
        functools.partial(accumulate_kernel, plan),
        in_specs=[pl.BlockSpec(memory_space=pltpu.SMEM)] * 2
        + [pl.BlockSpec(memory_space=pltpu.VMEM)] * 2
        + [pl.BlockSpec(memory_space=pl.ANY)] * 4,
        out_specs=pl.BlockSpec(memory_space=pltpu.VMEM),
        out_shape=jax.ShapeDtypeStruct((plan.sx * (tiles + 8), 2 * VOX), jnp.float32),
        scratch_shapes=[pltpu.VMEM(array.shape, array.dtype) for array in arrays]
        + [pltpu.SemaphoreType.DMA((positions // POSITIONS, 4)), pltpu.VMEM((tiles, 1), jnp.int32)],
        compiler_params=pltpu.CompilerParams(vmem_limit_bytes=TILE_LIMIT),
        cost_estimate=pl.CostEstimate(
            flops=4 * tiles * pixels * pixels * VOX,
            bytes_accessed=sum(array.size * 2 for array in arrays),
            transcendentals=0,
        ),
        name="tile_sums",
    )(angles, lorentz, owner, box, *arrays)


def scatter_kernel(plan, payload, *outs):
    tiles = LANES
    packed = tiles + 8
    offset = plan.here() // plan.sz * (plan.sz * plan.share)
    blocks = [payload.at[pl.ds(start, packed)] for start in range(0, payload.shape[0], packed)]
    for at in range(0, len(blocks), 2):
        pair = blocks[at : at + 2]
        ids = jnp.concatenate([ref[tiles : tiles + 1, :tiles] for ref in pair], axis=1)
        ids = ids.astype(jnp.int32) ^ offset
        data = jnp.concatenate([ref[:tiles, :] for ref in pair], axis=0)
        high = data.astype(jnp.bfloat16)
        low = (data - high.astype(jnp.float32)).astype(jnp.bfloat16)
        start = 0
        for out in outs:
            boxes = lax.broadcasted_iota(jnp.int32, (out.shape[0], ids.shape[1]), 0) + start
            start += out.shape[0]
            pick = (boxes == ids).astype(jnp.float32).astype(jnp.bfloat16)
            total = jnp.dot(pick, high, preferred_element_type=jnp.float32)
            total = total + jnp.dot(pick, low, preferred_element_type=jnp.float32)
            if at == 0:
                out[...] = total
            else:
                out[...] += total


def add_kernel(*refs):
    inputs, out = refs[:-1], refs[-1]
    total = inputs[0][...]
    for ref in inputs[1:]:
        total = total + ref[...]
    out[...] = total


def intensity_kernel(copies, parts, out):
    share = out.shape[0] // copies
    total = parts[:share, :]
    for start in range(share, parts.shape[0], share):
        total = total + parts[start : start + share, :]
    total = total * 0.125
    result = total[:, :VOX] / jnp.maximum(total[:, VOX:], 1.0)
    for start in range(0, out.shape[0], share):
        out[start : start + share, :] = result


def unfold_kernel(plan, near, far, out):
    upper = plan.upper(plan.here())
    own = masked(upper, (4, 2, 1))
    local = masked(upper, plan.flip_local)
    mask = masked(upper, FLIP_VOX)
    index = lax.broadcasted_iota(jnp.int32, (8, LANES), 1) ^ (mask & (LANES - 1))
    turn = lax.broadcasted_iota(jnp.int32, (8, LANES), 0) ^ (local & 7)
    swap = (mask & LANES) != 0
    for ref, other in ((near, 0), (far, 2)):
        for place, code in enumerate((0, 1, 4, 5)):
            base = (code ^ (own & 2) ^ other) * plan.share
            for group in range(0, plan.share, 8):
                start = place * plan.share + group
                rows = ref[start : start + 8, :]
                low, high = rows[:, :LANES], rows[:, LANES:]
                pieces = []
                for item in (jnp.where(swap, high, low), jnp.where(swap, low, high)):
                    item = jnp.take_along_axis(item, turn, axis=0, mode="promise_in_bounds")
                    pieces.append(lane_gather(item, index))
                target = (base + group) ^ (local & ~7)
                out[pl.ds(pl.multiple_of(target, 8), 8), :] = jnp.concatenate(pieces, axis=1)


def small_call(kernel, shapes, name, *arrays):
    return pl.pallas_call(
        kernel,
        out_shape=[jax.ShapeDtypeStruct(shape, jnp.float32) for shape in shapes],
        compiler_params=pltpu.CompilerParams(vmem_limit_bytes=VMEM_LIMIT),
        name=name,
    )(*arrays)


def shards(plan, counts, row_split, col_split, efficiency, lorentz, angles, tile_owner, tile_box):
    def swap(array, mask):
        return lax.ppermute(array, AXES, [(i, i ^ mask) for i in range(plan.devices)])

    width = 2 * VOX
    owner = tile_owner.reshape(1, -1)
    box = tile_box.reshape(1, -1)
    own = accumulate(plan, counts, row_split, col_split, efficiency, lorentz, angles, owner, box)
    payload = lax.all_to_all(own, "bx", split_axis=0, concat_axis=0, tiled=True)
    column = (plan.sz * plan.share, width)
    sums = small_call(functools.partial(scatter_kernel, plan), [column] * plan.sy, "box_sums", payload)
    arrived = [sums[0]] + [swap(sums[i], i * plan.sz) for i in range(1, plan.sy)]
    (total,) = small_call(add_kernel, [column], "core_sums", *arrived)
    parts = lax.all_to_all(total, "bz", split_axis=0, concat_axis=0, tiled=True)
    flip_x, flip_y, flip_z = plan.flip_dev
    kernel = functools.partial(intensity_kernel, 4)
    (part,) = small_call(kernel, [(4 * plan.share, VOX)], "intensity", parts)
    groups = [
        [base ^ mask for mask in (0, flip_z, flip_x, flip_x ^ flip_z)]
        for base in range(plan.devices)
        if not base & (plan.half[0] | plan.half[2])
    ]
    near = lax.all_to_all(part, AXES, split_axis=0, concat_axis=0, tiled=True, axis_index_groups=groups)
    far = swap(near, flip_y)
    (result,) = small_call(functools.partial(unfold_kernel, plan), [(plan.boxes, VOX)], "unfold", near, far)
    return result.reshape(GX // plan.sx, GY // plan.sy, GZ // plan.sz, BOX_BRICK, VOX)


def solution(mesh):
    return jax.shard_map(
        functools.partial(shards, Plan(mesh)),
        mesh=mesh,
        in_specs=(
            P(AXES, None, None, None),
            P(AXES, None, None, None),
            P(AXES, None, None, None),
            P(),
            P(),
            P(AXES),
            P(AXES, None),
            P(AXES),
        ),
        out_specs=P("bx", "by", "bz", None, None),
        check_vma=False,
    )
```

```python
import functools

import jax
import jax.numpy as jnp
from jax import lax
from jax.experimental import pallas as pl
from jax.experimental.pallas import tpu as pltpu
from jax.sharding import PartitionSpec as P

VOX = 256
LANES = 128
GX = 8
GY = 8
GZ = 4
BOX_BRICK = 64
FLIP_VOX = (0b11100000, 0b00011100, 0b00000011)
FLIP_BOX = (0b110000, 0b001100, 0b000011)
AXES = ("bx", "by", "bz")
POSITIONS = 8
TILE_LIMIT = 56 * 1024 * 1024
VMEM_LIMIT = 24 * 1024 * 1024
LARGE = 10**10


class Plan:
    def __init__(self, mesh):
        self.sx, self.sy, self.sz = (mesh.shape[name] for name in AXES)
        self.devices = self.sx * self.sy * self.sz
        lx, ly, lz = GX // self.sx, GY // self.sy, GZ // self.sz
        self.boxes = lx * ly * lz * BOX_BRICK
        self.share = self.boxes // 8
        self.flip_dev = ((self.sx - 1) * self.sy * self.sz, (self.sy - 1) * self.sz, self.sz - 1)
        self.half = (self.sx * self.sy * self.sz // 2, self.sy * self.sz // 2, self.sz // 2)
        self.flip_local = (
            (lx - 1) * ly * lz * BOX_BRICK + FLIP_BOX[0],
            (ly - 1) * lz * BOX_BRICK + FLIP_BOX[1],
            (lz - 1) * BOX_BRICK + FLIP_BOX[2],
        )

    def upper(self, device):
        return [(device & half) != 0 for half in self.half]

    def here(self):
        return (lax.axis_index("bx") * self.sy + lax.axis_index("by")) * self.sz + lax.axis_index("bz")


def masked(flags, masks):
    total = jnp.where(flags[0], masks[0], 0)
    for flag, mask in zip(flags[1:], masks[1:]):
        total = total ^ jnp.where(flag, mask, 0)
    return total


def lane_gather(values, index):
    return jnp.take_along_axis(values, index, axis=1, mode="promise_in_bounds")


def destination(plan, owner, box):
    upper = plan.upper(owner)
    local = box ^ masked(upper, plan.flip_local)
    part = local // plan.share
    row = local % plan.share
    holder = owner ^ masked(upper, plan.flip_dev)
    holder = holder ^ masked([(part & bit) != 0 for bit in (4, 2, 1)], plan.flip_dev)
    return holder * plan.share + row


def accumulate_kernel(plan, angles, lorentz, owner, box, counts, rows, cols, seen, value_out, weight_out, *scratch):
    arrays, sems, turned = scratch[:4], scratch[4], scratch[5]
    frames, positions = counts.shape[0], counts.shape[1]
    blocks = positions // POSITIONS

    def copies(block):
        span = pl.ds(block * POSITIONS, POSITIONS)
        views = [(ref.at[:, span], held.at[:, span]) for ref, held in zip((counts, rows, cols), arrays)]
        views.append((seen.at[span], arrays[3].at[span]))
        return [pltpu.make_async_copy(src, dst, sems.at[block, i]) for i, (src, dst) in enumerate(views)]

    for block in range(blocks):
        for copy in copies(block):
            copy.start()

    tiles = frames * positions
    across = lax.broadcasted_iota(jnp.int32, (tiles, tiles), 1)
    down = lax.broadcasted_iota(jnp.int32, (tiles, tiles), 0)
    flips = masked(plan.upper(owner[...]), FLIP_VOX)
    turned[...] = jnp.sum(jnp.where(across == down, flips, 0), axis=1, keepdims=True)
    ids = destination(plan, owner[...], box[...])
    for out in (value_out, weight_out):
        out[tiles : tiles + 8, :] = jnp.zeros((8, VOX), jnp.float32)
        out[tiles : tiles + 8, :tiles] = jnp.broadcast_to(ids.astype(jnp.float32), (8, tiles))

    @pl.loop(0, blocks)
    def _(block):
        for copy in copies(block):
            copy.wait()
        held_counts, held_rows, held_cols, held_seen = arrays
        lanes = lax.broadcasted_iota(jnp.int32, (POSITIONS, LANES), 1)
        value_rows = [[] for _ in range(frames)]
        weight_rows = [[] for _ in range(frames)]
        for p in range(POSITIONS):
            at = block * POSITIONS + p
            cols_all = jnp.concatenate([held_cols[f, at] for f in range(frames)], axis=1)
            seen_all = jnp.dot(held_seen[at], cols_all, preferred_element_type=jnp.float32)
            for f in range(frames):
                spread = held_rows[f, at].astype(jnp.float32)
                counted = jnp.dot(held_counts[f, at], held_cols[f, at], preferred_element_type=jnp.float32)
                value_rows[f].append(jnp.sum(spread * counted, axis=0, keepdims=True))
                observed = seen_all[:, f * VOX : (f + 1) * VOX]
                weight_rows[f].append(jnp.sum(spread * observed, axis=0, keepdims=True))
        for f in range(frames):
            value = jnp.concatenate(value_rows[f], axis=0) * lorentz[angles[f]]
            weight = jnp.concatenate(weight_rows[f], axis=0)
            place = pl.ds(pl.multiple_of(f * positions + block * POSITIONS, POSITIONS), POSITIONS)
            mask = jnp.broadcast_to(turned[place, :], (POSITIONS, LANES))
            index = lanes ^ (mask & (LANES - 1))
            swap = (mask & LANES) != 0
            for item, out in ((value, value_out), (weight, weight_out)):
                low, high = item[:, :LANES], item[:, LANES:]
                out[place, :LANES] = lane_gather(jnp.where(swap, high, low), index)
                out[place, LANES:] = lane_gather(jnp.where(swap, low, high), index)


def accumulate(plan, counts, row_split, col_split, efficiency, lorentz, angles, owner, box):
    frames, positions, pixels, _ = counts.shape
    tiles = frames * positions
    arrays = (counts, row_split, col_split, efficiency)
    return pl.pallas_call(
        functools.partial(accumulate_kernel, plan),
        in_specs=[pl.BlockSpec(memory_space=pltpu.SMEM)] * 2
        + [pl.BlockSpec(memory_space=pltpu.VMEM)] * 2
        + [pl.BlockSpec(memory_space=pl.ANY)] * 4,
        out_specs=[pl.BlockSpec(memory_space=pltpu.VMEM)] * 2,
        out_shape=[jax.ShapeDtypeStruct((tiles + 8, VOX), jnp.float32)] * 2,
        scratch_shapes=[pltpu.VMEM(array.shape, array.dtype) for array in arrays]
        + [pltpu.SemaphoreType.DMA((positions // POSITIONS, 4)), pltpu.VMEM((tiles, 1), jnp.int32)],
        compiler_params=pltpu.CompilerParams(vmem_limit_bytes=TILE_LIMIT),
        cost_estimate=pl.CostEstimate(
            flops=4 * tiles * pixels * pixels * VOX,
            bytes_accessed=sum(array.size * 2 for array in arrays),
            transcendentals=0,
        ),
        name="tile_sums",
    )(angles, lorentz, owner, box, *arrays)


def scatter_kernel(plan, relative, olds, outs, payload, *refs):
    before, after = refs[:olds], refs[len(refs) - outs :]
    tiles = LANES
    half = payload.shape[0] // 2
    offset = plan.here() if relative else plan.here() & ~((plan.sy - 1) * plan.sz)
    ids = [payload[start + tiles : start + tiles + 1, :tiles] for start in (0, half)]
    ids = jnp.concatenate(ids, axis=1).astype(jnp.int32) ^ (offset * plan.share)
    values = jnp.concatenate([payload[:tiles, :], payload[half : half + tiles, :]], axis=0)
    high = values.astype(jnp.bfloat16)
    low = (values - high.astype(jnp.float32)).astype(jnp.bfloat16)
    for number, out in enumerate(after):
        boxes = lax.broadcasted_iota(jnp.int32, (out.shape[0], ids.shape[1]), 0) + number * out.shape[0]
        pick = (boxes == ids).astype(jnp.float32).astype(jnp.bfloat16)
        total = jnp.dot(pick, high, preferred_element_type=jnp.float32)
        total = total + jnp.dot(pick, low, preferred_element_type=jnp.float32)
        out[...] = total + before[number][...] if olds else total


def stage_kernel(first, second, first_out, second_out):
    first_out[...] = first[...]
    second_out[...] = second[...]


def join_kernel(first, second, *rest):
    half, out = first.shape[0], rest[-1]
    out[:half, :] = first[...]
    out[half:, :] = second[...]


def split_kernel(count, *refs):
    inputs, outs = refs[:-count], refs[-count:]
    share = outs[0].shape[0]
    for number, out in enumerate(outs):
        total = None
        for ref in inputs:
            for start in range(number * share, ref.shape[0], count * share):
                rows = ref[start : start + share, :]
                total = rows if total is None else total + rows
        out[...] = total


def total_kernel(*refs):
    inputs, out = refs[:-1], refs[-1]
    total = inputs[0][...]
    for ref in inputs[1:]:
        total = total + ref[...]
    out[...] = total


def intensity_kernel(value, *refs):
    inputs, out = refs[:-1], refs[-1]
    weight = inputs[0][...]
    for ref in inputs[1:]:
        weight = weight + ref[...]
    out[...] = value[...] * 0.125 / jnp.maximum(weight * 0.125, 1.0)


def unfold_kernel(plan, *refs):
    inputs, out = refs[:-1], refs[-1]
    upper = plan.upper(plan.here())
    own = masked(upper, (4, 2, 1))
    local = masked(upper, plan.flip_local)
    mask = masked(upper, FLIP_VOX)
    index = lax.broadcasted_iota(jnp.int32, (8, LANES), 1) ^ (mask & (LANES - 1))
    turn = lax.broadcasted_iota(jnp.int32, (8, LANES), 0) ^ (local & 7)
    swap = (mask & LANES) != 0
    for relative, ref in enumerate(inputs):
        base = (relative ^ own) * plan.share
        for group in range(0, plan.share, 8):
            rows = ref[group : group + 8, :]
            low, high = rows[:, :LANES], rows[:, LANES:]
            target = (base + group) ^ (local & ~7)
            place = pl.ds(pl.multiple_of(target, 8), 8)
            for at, item in enumerate((jnp.where(swap, high, low), jnp.where(swap, low, high))):
                item = jnp.take_along_axis(item, turn, axis=0, mode="promise_in_bounds")
                out[place, at * LANES : (at + 1) * LANES] = lane_gather(item, index)


def small_call(kernel, shapes, name, *arrays, flops=1):
    return pl.pallas_call(
        kernel,
        out_shape=[jax.ShapeDtypeStruct(shape, jnp.float32) for shape in shapes],
        compiler_params=pltpu.CompilerParams(vmem_limit_bytes=VMEM_LIMIT),
        cost_estimate=pl.CostEstimate(flops=flops, bytes_accessed=1, transcendentals=0),
        name=name,
    )(*arrays)


def shards(plan, counts, row_split, col_split, efficiency, lorentz, angles, tile_owner, tile_box):
    def swap(array, even, odd=None):
        odd = even if odd is None else odd
        pairs = [(i, i ^ (odd if i // plan.sz % 2 else even)) for i in range(plan.devices)]
        return lax.ppermute(array, AXES, pairs)

    def join(first, second, *order):
        rows, width = first.shape
        return small_call(join_kernel, [(2 * rows, width)], "join", first, second, *order)[0]

    row = plan.sy * plan.sz
    owner = tile_owner.reshape(1, -1)
    box = tile_box.reshape(1, -1)
    own = accumulate(plan, counts, row_split, col_split, efficiency, lorentz, angles, owner, box)
    arrived = [swap(array, row, 2 * row) for array in own]
    held = small_call(stage_kernel, [array.shape for array in own], "stage", *own, flops=LARGE)
    near = [join(held[0], arrived[0])]
    near.append(join(held[1], arrived[1], near[0]))
    far = [swap(array, 2 * row, row) for array in near]
    def box_sums(payload, relative, olds, *waits, flops=1):
        count = plan.sy if relative else 1
        kernel = functools.partial(scatter_kernel, plan, relative, len(olds), count)
        shapes = [(row * plan.share // count, VOX)] * count
        return small_call(kernel, shapes, "box_sums", payload, *olds, *waits, flops=flops)

    def spread(arrived):
        kernel = functools.partial(split_kernel, plan.sz)
        parts = small_call(kernel, [(plan.share, VOX)] * plan.sz, "core_sums", *arrived)
        return parts, [parts[0]] + [swap(parts[i], i) for i in range(1, plan.sz)]

    sums = [box_sums(near[0], True, []), box_sums(near[1], False, [], flops=LARGE)]
    value = box_sums(far[0], True, sums[0], sums[1][0])
    value = [value[0]] + [swap(value[i], i * plan.sz) for i in range(1, plan.sy)]
    parts, values = spread(value)
    (weight,) = box_sums(far[1], False, sums[1], parts[0], flops=LARGE)
    weight = lax.all_to_all(weight, "by", split_axis=0, concat_axis=0, tiled=True)
    _, weights = spread([weight])
    (value,) = small_call(total_kernel, [(plan.share, VOX)], "value_total", *values, flops=LARGE)
    (own,) = small_call(intensity_kernel, [(plan.share, VOX)], "intensity", value, *weights)
    flip_x, flip_y, flip_z = plan.flip_dev
    near = [own, swap(own, flip_z), swap(own, flip_x), swap(own, flip_x ^ flip_z)]
    far = [swap(array, flip_y) for array in near]
    ordered = [near[0], near[1], far[0], far[1], near[2], near[3], far[2], far[3]]
    (result,) = small_call(functools.partial(unfold_kernel, plan), [(plan.boxes, VOX)], "unfold", *ordered)
    return result.reshape(GX // plan.sx, GY // plan.sy, GZ // plan.sz, BOX_BRICK, VOX)


def solution(mesh):
    return jax.shard_map(
        functools.partial(shards, Plan(mesh)),
        mesh=mesh,
        in_specs=(
            P(AXES, None, None, None),
            P(AXES, None, None, None),
            P(AXES, None, None, None),
            P(),
            P(),
            P(AXES),
            P(AXES, None),
            P(AXES),
        ),
        out_specs=P("bx", "by", "bz", None, None),
        check_vma=False,
    )
```

```python
import functools

import jax
import jax.numpy as jnp
from jax import lax
from jax.experimental import pallas as pl
from jax.experimental.pallas import tpu as pltpu
from jax.sharding import PartitionSpec as P

VOX = 256
LANES = 128
GX = 8
GY = 8
GZ = 4
BOX_BRICK = 64
FLIP_VOX = (0b11100000, 0b00011100, 0b00000011)
FLIP_BOX = (0b110000, 0b001100, 0b000011)
AXES = ("bx", "by", "bz")
POSITIONS = 8
TILE_LIMIT = 56 * 1024 * 1024
VMEM_LIMIT = 24 * 1024 * 1024
LARGE = 10**10


class Plan:
    def __init__(self, mesh):
        self.sx, self.sy, self.sz = (mesh.shape[name] for name in AXES)
        self.devices = self.sx * self.sy * self.sz
        lx, ly, lz = GX // self.sx, GY // self.sy, GZ // self.sz
        self.boxes = lx * ly * lz * BOX_BRICK
        self.share = self.boxes // 8
        self.flip_dev = ((self.sx - 1) * self.sy * self.sz, (self.sy - 1) * self.sz, self.sz - 1)
        self.half = (self.sx * self.sy * self.sz // 2, self.sy * self.sz // 2, self.sz // 2)
        self.flip_local = (
            (lx - 1) * ly * lz * BOX_BRICK + FLIP_BOX[0],
            (ly - 1) * lz * BOX_BRICK + FLIP_BOX[1],
            (lz - 1) * BOX_BRICK + FLIP_BOX[2],
        )

    def upper(self, device):
        return [(device & half) != 0 for half in self.half]

    def here(self):
        return (lax.axis_index("bx") * self.sy + lax.axis_index("by")) * self.sz + lax.axis_index("bz")


def masked(flags, masks):
    total = jnp.where(flags[0], masks[0], 0)
    for flag, mask in zip(flags[1:], masks[1:]):
        total = total ^ jnp.where(flag, mask, 0)
    return total


def lane_gather(values, index):
    return jnp.take_along_axis(values, index, axis=1, mode="promise_in_bounds")


def destination(plan, owner, box):
    upper = plan.upper(owner)
    local = box ^ masked(upper, plan.flip_local)
    part = local // plan.share
    row = local % plan.share
    holder = owner ^ masked(upper, plan.flip_dev)
    holder = holder ^ masked([(part & bit) != 0 for bit in (4, 2, 1)], plan.flip_dev)
    return holder * plan.share + row


def accumulate_kernel(plan, angles, lorentz, owner, box, counts, rows, cols, seen, value_out, weight_out, *scratch):
    arrays, sems, turned = scratch[:4], scratch[4], scratch[5]
    frames, positions = counts.shape[0], counts.shape[1]
    blocks = positions // POSITIONS

    def copies(block):
        span = pl.ds(block * POSITIONS, POSITIONS)
        views = [(ref.at[:, span], held.at[:, span]) for ref, held in zip((counts, rows, cols), arrays)]
        views.append((seen.at[span], arrays[3].at[span]))
        return [pltpu.make_async_copy(src, dst, sems.at[block, i]) for i, (src, dst) in enumerate(views)]

    for block in range(blocks):
        for copy in copies(block):
            copy.start()

    tiles = frames * positions
    across = lax.broadcasted_iota(jnp.int32, (tiles, tiles), 1)
    down = lax.broadcasted_iota(jnp.int32, (tiles, tiles), 0)
    flips = masked(plan.upper(owner[...]), FLIP_VOX)
    turned[...] = jnp.sum(jnp.where(across == down, flips, 0), axis=1, keepdims=True)
    ids = destination(plan, owner[...], box[...])
    for out in (value_out, weight_out):
        out[tiles : tiles + 8, :] = jnp.zeros((8, VOX), jnp.float32)
        out[tiles : tiles + 8, :tiles] = jnp.broadcast_to(ids.astype(jnp.float32), (8, tiles))

    @pl.loop(0, blocks)
    def _(block):
        for copy in copies(block):
            copy.wait()
        held_counts, held_rows, held_cols, held_seen = arrays
        lanes = lax.broadcasted_iota(jnp.int32, (POSITIONS, LANES), 1)
        value_rows = [[] for _ in range(frames)]
        weight_rows = [[] for _ in range(frames)]
        for p in range(POSITIONS):
            at = block * POSITIONS + p
            cols_all = jnp.concatenate([held_cols[f, at] for f in range(frames)], axis=1)
            seen_all = jnp.dot(held_seen[at], cols_all, preferred_element_type=jnp.float32)
            for f in range(frames):
                spread = held_rows[f, at].astype(jnp.float32)
                counted = jnp.dot(held_counts[f, at], held_cols[f, at], preferred_element_type=jnp.float32)
                value_rows[f].append(jnp.sum(spread * counted, axis=0, keepdims=True))
                observed = seen_all[:, f * VOX : (f + 1) * VOX]
                weight_rows[f].append(jnp.sum(spread * observed, axis=0, keepdims=True))
        for f in range(frames):
            value = jnp.concatenate(value_rows[f], axis=0) * lorentz[angles[f]]
            weight = jnp.concatenate(weight_rows[f], axis=0)
            place = pl.ds(pl.multiple_of(f * positions + block * POSITIONS, POSITIONS), POSITIONS)
            mask = jnp.broadcast_to(turned[place, :], (POSITIONS, LANES))
            index = lanes ^ (mask & (LANES - 1))
            swap = (mask & LANES) != 0
            for item, out in ((value, value_out), (weight, weight_out)):
                low, high = item[:, :LANES], item[:, LANES:]
                out[place, :LANES] = lane_gather(jnp.where(swap, high, low), index)
                out[place, LANES:] = lane_gather(jnp.where(swap, low, high), index)


def accumulate(plan, counts, row_split, col_split, efficiency, lorentz, angles, owner, box):
    frames, positions, pixels, _ = counts.shape
    tiles = frames * positions
    arrays = (counts, row_split, col_split, efficiency)
    return pl.pallas_call(
        functools.partial(accumulate_kernel, plan),
        in_specs=[pl.BlockSpec(memory_space=pltpu.SMEM)] * 2
        + [pl.BlockSpec(memory_space=pltpu.VMEM)] * 2
        + [pl.BlockSpec(memory_space=pl.ANY)] * 4,
        out_specs=[pl.BlockSpec(memory_space=pltpu.VMEM)] * 2,
        out_shape=[jax.ShapeDtypeStruct((tiles + 8, VOX), jnp.float32)] * 2,
        scratch_shapes=[pltpu.VMEM(array.shape, array.dtype) for array in arrays]
        + [pltpu.SemaphoreType.DMA((positions // POSITIONS, 4)), pltpu.VMEM((tiles, 1), jnp.int32)],
        compiler_params=pltpu.CompilerParams(vmem_limit_bytes=TILE_LIMIT),
        cost_estimate=pl.CostEstimate(
            flops=4 * tiles * pixels * pixels * VOX,
            bytes_accessed=sum(array.size * 2 for array in arrays),
            transcendentals=0,
        ),
        name="tile_sums",
    )(angles, lorentz, owner, box, *arrays)


def scatter_kernel(plan, relative, olds, outs, payload, *refs):
    before, after = refs[:olds], refs[len(refs) - outs :]
    tiles = LANES
    half = payload.shape[0] // 2
    offset = plan.here() if relative else plan.here() & ~((plan.sy - 1) * plan.sz)
    ids = [payload[start + tiles : start + tiles + 1, :tiles] for start in (0, half)]
    ids = jnp.concatenate(ids, axis=1).astype(jnp.int32) ^ (offset * plan.share)
    values = jnp.concatenate([payload[:tiles, :], payload[half : half + tiles, :]], axis=0)
    high = values.astype(jnp.bfloat16)
    low = (values - high.astype(jnp.float32)).astype(jnp.bfloat16)
    for number, out in enumerate(after):
        boxes = lax.broadcasted_iota(jnp.int32, (out.shape[0], ids.shape[1]), 0) + number * out.shape[0]
        pick = (boxes == ids).astype(jnp.float32).astype(jnp.bfloat16)
        total = jnp.dot(pick, high, preferred_element_type=jnp.float32)
        total = total + jnp.dot(pick, low, preferred_element_type=jnp.float32)
        out[...] = total + before[number][...] if olds else total


def stage_kernel(first, second, first_out, second_out):
    first_out[...] = first[...]
    second_out[...] = second[...]


def join_kernel(first, second, *rest):
    half, out = first.shape[0], rest[-1]
    out[:half, :] = first[...]
    out[half:, :] = second[...]


def split_kernel(count, *refs):
    inputs, outs = refs[:-count], refs[-count:]
    share = outs[0].shape[0]
    for number, out in enumerate(outs):
        total = None
        for ref in inputs:
            for start in range(number * share, ref.shape[0], count * share):
                rows = ref[start : start + share, :]
                total = rows if total is None else total + rows
        out[...] = total


def total_kernel(*refs):
    inputs, out = refs[:-1], refs[-1]
    total = inputs[0][...]
    for ref in inputs[1:]:
        total = total + ref[...]
    out[...] = total


def intensity_kernel(value, *refs):
    inputs, out = refs[:-1], refs[-1]
    weight = inputs[0][...]
    for ref in inputs[1:]:
        weight = weight + ref[...]
    out[...] = value[...] * 0.125 / jnp.maximum(weight * 0.125, 1.0)


def unfold_kernel(plan, *refs):
    inputs, out = refs[:-1], refs[-1]
    upper = plan.upper(plan.here())
    own = masked(upper, (4, 2, 1))
    local = masked(upper, plan.flip_local)
    mask = masked(upper, FLIP_VOX)
    index = lax.broadcasted_iota(jnp.int32, (8, LANES), 1) ^ (mask & (LANES - 1))
    turn = lax.broadcasted_iota(jnp.int32, (8, LANES), 0) ^ (local & 7)
    swap = (mask & LANES) != 0
    for relative, ref in enumerate(inputs):
        base = (relative ^ own) * plan.share
        for group in range(0, plan.share, 8):
            rows = ref[group : group + 8, :]
            low, high = rows[:, :LANES], rows[:, LANES:]
            target = (base + group) ^ (local & ~7)
            place = pl.ds(pl.multiple_of(target, 8), 8)
            for at, item in enumerate((jnp.where(swap, high, low), jnp.where(swap, low, high))):
                item = jnp.take_along_axis(item, turn, axis=0, mode="promise_in_bounds")
                out[place, at * LANES : (at + 1) * LANES] = lane_gather(item, index)


def small_call(kernel, shapes, name, *arrays, flops=1):
    return pl.pallas_call(
        kernel,
        out_shape=[jax.ShapeDtypeStruct(shape, jnp.float32) for shape in shapes],
        compiler_params=pltpu.CompilerParams(vmem_limit_bytes=VMEM_LIMIT),
        cost_estimate=pl.CostEstimate(flops=flops, bytes_accessed=1, transcendentals=0),
        name=name,
    )(*arrays)


def shards(plan, counts, row_split, col_split, efficiency, lorentz, angles, tile_owner, tile_box):
    def swap(array, even, odd=None):
        odd = even if odd is None else odd
        pairs = [(i, i ^ (odd if i // plan.sz % 2 else even)) for i in range(plan.devices)]
        return lax.ppermute(array, AXES, pairs)

    def join(first, second, *order):
        rows, width = first.shape
        return small_call(join_kernel, [(2 * rows, width)], "join", first, second, *order)[0]

    row = plan.sy * plan.sz
    owner = tile_owner.reshape(1, -1)
    box = tile_box.reshape(1, -1)
    own = accumulate(plan, counts, row_split, col_split, efficiency, lorentz, angles, owner, box)
    arrived = [swap(array, row, 2 * row) for array in own]
    held = small_call(stage_kernel, [array.shape for array in own], "stage", *own, flops=LARGE)
    near = [join(held[0], arrived[0])]
    near.append(join(held[1], arrived[1], near[0]))
    far = [swap(array, 2 * row, row) for array in near]
    def box_sums(payload, relative, olds, *waits, flops=1):
        count = plan.sy if relative else 1
        kernel = functools.partial(scatter_kernel, plan, relative, len(olds), count)
        shapes = [(row * plan.share // count, VOX)] * count
        return small_call(kernel, shapes, "box_sums", payload, *olds, *waits, flops=flops)

    def spread(arrived):
        kernel = functools.partial(split_kernel, plan.sz)
        parts = small_call(kernel, [(plan.share, VOX)] * plan.sz, "core_sums", *arrived)
        return parts, [parts[0]] + [swap(parts[i], i) for i in range(1, plan.sz)]

    sums = [box_sums(near[0], True, []), box_sums(near[1], True, [], flops=LARGE)]
    value = box_sums(far[0], True, sums[0], sums[1][0])
    weight = box_sums(far[1], True, sums[1], value[0])
    value = [value[0]] + [swap(value[i], i * plan.sz) for i in range(1, plan.sy)]
    weight = [weight[0]] + [swap(weight[i], i * plan.sz) for i in range(1, plan.sy)]
    parts, values = spread(value)
    _, weights = spread(weight)
    (value,) = small_call(total_kernel, [(plan.share, VOX)], "value_total", *values, flops=LARGE)
    (own,) = small_call(intensity_kernel, [(plan.share, VOX)], "intensity", value, *weights)
    flip_x, flip_y, flip_z = plan.flip_dev
    near = [own, swap(own, flip_z), swap(own, flip_x), swap(own, flip_x ^ flip_z)]
    far = [swap(array, flip_y) for array in near]
    ordered = [near[0], near[1], far[0], far[1], near[2], near[3], far[2], far[3]]
    (result,) = small_call(functools.partial(unfold_kernel, plan), [(plan.boxes, VOX)], "unfold", *ordered)
    return result.reshape(GX // plan.sx, GY // plan.sy, GZ // plan.sz, BOX_BRICK, VOX)


def solution(mesh):
    return jax.shard_map(
        functools.partial(shards, Plan(mesh)),
        mesh=mesh,
        in_specs=(
            P(AXES, None, None, None),
            P(AXES, None, None, None),
            P(AXES, None, None, None),
            P(),
            P(),
            P(AXES),
            P(AXES, None),
            P(AXES),
        ),
        out_specs=P("bx", "by", "bz", None, None),
        check_vma=False,
    )
```

```python
import functools

import jax
import jax.numpy as jnp
from jax import lax
from jax.experimental import pallas as pl
from jax.experimental.pallas import tpu as pltpu
from jax.sharding import PartitionSpec as P

VOX = 256
LANES = 128
GX = 8
GY = 8
GZ = 4
BOX_BRICK = 64
FLIP_VOX = (0b11100000, 0b00011100, 0b00000011)
FLIP_BOX = (0b110000, 0b001100, 0b000011)
AXES = ("bx", "by", "bz")
POSITIONS = 8
LANDED = 4
TILE_LIMIT = 56 * 1024 * 1024
VMEM_LIMIT = 24 * 1024 * 1024
LARGE = 10**10


class Plan:
    def __init__(self, mesh):
        self.sx, self.sy, self.sz = (mesh.shape[name] for name in AXES)
        self.devices = self.sx * self.sy * self.sz
        lx, ly, lz = GX // self.sx, GY // self.sy, GZ // self.sz
        self.boxes = lx * ly * lz * BOX_BRICK
        self.share = self.boxes // 8
        self.flip_dev = ((self.sx - 1) * self.sy * self.sz, (self.sy - 1) * self.sz, self.sz - 1)
        self.half = (self.sx * self.sy * self.sz // 2, self.sy * self.sz // 2, self.sz // 2)
        self.flip_local = (
            (lx - 1) * ly * lz * BOX_BRICK + FLIP_BOX[0],
            (ly - 1) * lz * BOX_BRICK + FLIP_BOX[1],
            (lz - 1) * BOX_BRICK + FLIP_BOX[2],
        )

    def upper(self, device):
        return [(device & half) != 0 for half in self.half]

    def by_stage(self, place):
        bits = self.sz.bit_length() - 1
        moved = place & ~((self.sz - 1) * self.share)
        for bit in range(bits):
            moved = moved | jnp.where((place & (self.share << bit)) != 0, self.share << (bits - 1 - bit), 0)
        return moved

    def here(self):
        return (lax.axis_index("bx") * self.sy + lax.axis_index("by")) * self.sz + lax.axis_index("bz")


def masked(flags, masks):
    total = jnp.where(flags[0], masks[0], 0)
    for flag, mask in zip(flags[1:], masks[1:]):
        total = total ^ jnp.where(flag, mask, 0)
    return total


def lane_gather(values, index):
    return jnp.take_along_axis(values, index, axis=1, mode="promise_in_bounds")


def destination(plan, owner, box):
    upper = plan.upper(owner)
    local = box ^ masked(upper, plan.flip_local)
    part = local // plan.share
    row = local % plan.share
    holder = owner ^ masked(upper, plan.flip_dev)
    holder = holder ^ masked([(part & bit) != 0 for bit in (4, 2, 1)], plan.flip_dev)
    return holder * plan.share + row


def accumulate_kernel(plan, angles, lorentz, owner, box, counts, rows, cols, seen, value_out, weight_out, *scratch):
    arrays, sems, turned = scratch[:4], scratch[4], scratch[5]
    frames, positions = counts.shape[0], counts.shape[1]
    blocks = positions // POSITIONS

    def copies(block):
        span = pl.ds(block * LANDED, LANDED)
        views = [(ref.at[:, span], held.at[:, span]) for ref, held in zip((counts, rows, cols), arrays)]
        views.append((seen.at[span], arrays[3].at[span]))
        return [pltpu.make_async_copy(src, dst, sems.at[block, i]) for i, (src, dst) in enumerate(views)]

    for block in range(positions // LANDED):
        for copy in copies(block):
            copy.start()

    tiles = frames * positions
    across = lax.broadcasted_iota(jnp.int32, (tiles, tiles), 1)
    down = lax.broadcasted_iota(jnp.int32, (tiles, tiles), 0)
    flips = masked(plan.upper(owner[...]), FLIP_VOX)
    turned[...] = jnp.sum(jnp.where(across == down, flips, 0), axis=1, keepdims=True)
    ids = destination(plan, owner[...], box[...])
    for out in (value_out, weight_out):
        out[tiles : tiles + 8, :] = jnp.zeros((8, VOX), jnp.float32)
        out[tiles : tiles + 8, :tiles] = jnp.broadcast_to(ids.astype(jnp.float32), (8, tiles))

    @pl.loop(0, blocks)
    def _(block):
        held_counts, held_rows, held_cols, held_seen = arrays
        lanes = lax.broadcasted_iota(jnp.int32, (POSITIONS, LANES), 1)
        value_rows = [[] for _ in range(frames)]
        weight_rows = [[] for _ in range(frames)]
        for p in range(POSITIONS):
            if p % LANDED == 0:
                for copy in copies(block * (POSITIONS // LANDED) + p // LANDED):
                    copy.wait()
            at = block * POSITIONS + p
            cols_all = jnp.concatenate([held_cols[f, at] for f in range(frames)], axis=1)
            seen_all = jnp.dot(held_seen[at], cols_all, preferred_element_type=jnp.float32)
            for f in range(frames):
                spread = held_rows[f, at].astype(jnp.float32)
                counted = jnp.dot(held_counts[f, at], held_cols[f, at], preferred_element_type=jnp.float32)
                value_rows[f].append(jnp.sum(spread * counted, axis=0, keepdims=True))
                observed = seen_all[:, f * VOX : (f + 1) * VOX]
                weight_rows[f].append(jnp.sum(spread * observed, axis=0, keepdims=True))
        for f in range(frames):
            value = jnp.concatenate(value_rows[f], axis=0) * lorentz[angles[f]]
            weight = jnp.concatenate(weight_rows[f], axis=0)
            place = pl.ds(pl.multiple_of(f * positions + block * POSITIONS, POSITIONS), POSITIONS)
            mask = jnp.broadcast_to(turned[place, :], (POSITIONS, LANES))
            index = lanes ^ (mask & (LANES - 1))
            swap = (mask & LANES) != 0
            for item, out in ((value, value_out), (weight, weight_out)):
                low, high = item[:, :LANES], item[:, LANES:]
                out[place, :LANES] = lane_gather(jnp.where(swap, high, low), index)
                out[place, LANES:] = lane_gather(jnp.where(swap, low, high), index)


def accumulate(plan, counts, row_split, col_split, efficiency, lorentz, angles, owner, box):
    frames, positions, pixels, _ = counts.shape
    tiles = frames * positions
    arrays = (counts, row_split, col_split, efficiency)
    return pl.pallas_call(
        functools.partial(accumulate_kernel, plan),
        in_specs=[pl.BlockSpec(memory_space=pltpu.SMEM)] * 2
        + [pl.BlockSpec(memory_space=pltpu.VMEM)] * 2
        + [pl.BlockSpec(memory_space=pl.ANY)] * 4,
        out_specs=[pl.BlockSpec(memory_space=pltpu.VMEM)] * 2,
        out_shape=[jax.ShapeDtypeStruct((tiles + 8, VOX), jnp.float32)] * 2,
        scratch_shapes=[pltpu.VMEM(array.shape, array.dtype) for array in arrays]
        + [pltpu.SemaphoreType.DMA((positions // LANDED, 4)), pltpu.VMEM((tiles, 1), jnp.int32)],
        compiler_params=pltpu.CompilerParams(vmem_limit_bytes=TILE_LIMIT),
        cost_estimate=pl.CostEstimate(
            flops=4 * tiles * pixels * pixels * VOX,
            bytes_accessed=sum(array.size * 2 for array in arrays),
            transcendentals=0,
        ),
        name="tile_sums",
    )(angles, lorentz, owner, box, *arrays)


def scatter_kernel(plan, olds, outs, payload, *refs):
    before, after = refs[:olds], refs[len(refs) - outs :]
    tiles = LANES
    half = payload.shape[0] // 2
    ids = [payload[start + tiles : start + tiles + 1, :tiles] for start in (0, half)]
    ids = plan.by_stage(jnp.concatenate(ids, axis=1).astype(jnp.int32) ^ (plan.here() * plan.share))
    values = jnp.concatenate([payload[:tiles, :], payload[half : half + tiles, :]], axis=0)
    high = values.astype(jnp.bfloat16)
    low = (values - high.astype(jnp.float32)).astype(jnp.bfloat16)
    for number, out in enumerate(after):
        boxes = lax.broadcasted_iota(jnp.int32, (out.shape[0], ids.shape[1]), 0) + number * out.shape[0]
        pick = (boxes == ids).astype(jnp.float32).astype(jnp.bfloat16)
        total = jnp.dot(pick, high, preferred_element_type=jnp.float32)
        total = total + jnp.dot(pick, low, preferred_element_type=jnp.float32)
        out[...] = total + before[number][...] if olds else total


def stage_kernel(first, second, first_out, second_out):
    first_out[...] = first[...]
    second_out[...] = second[...]


def join_kernel(count, *refs):
    start, out = 0, refs[-1]
    for ref in refs[:count]:
        out[start : start + ref.shape[0], :] = ref[...]
        start += ref.shape[0]


def add_kernel(count, *refs):
    inputs, outs = refs[:count], refs[count:]
    start = 0
    for out in outs:
        span = slice(start, start + out.shape[0])
        total = inputs[0][span, :]
        for ref in inputs[1:]:
            total = total + ref[span, :]
        out[...] = total
        start += out.shape[0]


def both_kernel(value, weight_a, weight_b, keep, *gives):
    rows = keep.shape[0]
    weight = weight_a[...] + weight_b[...]
    keep[:, :VOX] = value[:rows, :]
    keep[:, VOX:] = weight[:rows, :]
    for give in gives:
        span = slice(rows, rows + give.shape[0])
        give[:, :VOX] = value[span, :]
        give[:, VOX:] = weight[span, :]
        rows += give.shape[0]


def intensity_kernel(half, keep, arrived, *refs):
    out = refs[-1]
    rows = out.shape[0]
    total = (keep[half * rows : (half + 1) * rows, :] + arrived[...]) * 0.125
    out[...] = total[:, :VOX] / jnp.maximum(total[:, VOX:], 1.0)


def unfold_kernel(plan, *refs):
    inputs, out = refs[:-1], refs[-1]
    upper = plan.upper(plan.here())
    own = masked(upper, (4, 2, 1))
    local = masked(upper, plan.flip_local)
    mask = masked(upper, FLIP_VOX)
    index = lax.broadcasted_iota(jnp.int32, (8, LANES), 1) ^ (mask & (LANES - 1))
    turn = lax.broadcasted_iota(jnp.int32, (8, LANES), 0) ^ (local & 7)
    swap = (mask & LANES) != 0
    rows_half = plan.share // 2
    for number, ref in enumerate(inputs):
        half, other = number // 2, 2 * (number % 2)
        for place, code in enumerate((0, 1, 4, 5)):
            base = ((code + other) ^ own) * plan.share + half * rows_half
            for group in range(0, rows_half, 8):
                start = place * rows_half + group
                rows = ref[start : start + 8, :]
                low, high = rows[:, :LANES], rows[:, LANES:]
                target = pl.ds(pl.multiple_of((base + group) ^ (local & ~7), 8), 8)
                for at, item in enumerate((jnp.where(swap, high, low), jnp.where(swap, low, high))):
                    item = jnp.take_along_axis(item, turn, axis=0, mode="promise_in_bounds")
                    out[target, at * LANES : (at + 1) * LANES] = lane_gather(item, index)


def small_call(kernel, shapes, name, *arrays, flops=1):
    return pl.pallas_call(
        kernel,
        out_shape=[jax.ShapeDtypeStruct(shape, jnp.float32) for shape in shapes],
        compiler_params=pltpu.CompilerParams(vmem_limit_bytes=VMEM_LIMIT),
        cost_estimate=pl.CostEstimate(flops=flops, bytes_accessed=1, transcendentals=0),
        name=name,
    )(*arrays)


def shards(plan, counts, row_split, col_split, efficiency, lorentz, angles, tile_owner, tile_box):
    def swap(array, even, odd=None):
        odd = even if odd is None else odd
        pairs = [(i, i ^ (odd if i // plan.sz % 2 else even)) for i in range(plan.devices)]
        return lax.ppermute(array, AXES, pairs)

    def join(parts, *waits, flops=1):
        kernel = functools.partial(join_kernel, len(parts))
        shape = (sum(part.shape[0] for part in parts), parts[0].shape[1])
        return small_call(kernel, [shape], "join", *parts, *waits, flops=flops)[0]

    row = plan.sy * plan.sz
    owner = tile_owner.reshape(1, -1)
    box = tile_box.reshape(1, -1)
    own = accumulate(plan, counts, row_split, col_split, efficiency, lorentz, angles, owner, box)
    arrived = [swap(array, row, 2 * row) for array in own]
    held = small_call(stage_kernel, [array.shape for array in own], "stage", *own, flops=LARGE)
    near = [join([held[0], arrived[0]])]
    near.append(join([held[1], arrived[1]], near[0]))
    far = [swap(array, 2 * row, row) for array in near]
    def box_sums(payload, olds, *waits, flops=1):
        kernel = functools.partial(scatter_kernel, plan, len(olds), plan.sy)
        shapes = [(plan.sz * plan.share, VOX)] * plan.sy
        return small_call(kernel, shapes, "box_sums", payload, *olds, *waits, flops=flops)

    def added(arrays, pieces, flops=1):
        shape = (arrays[0].shape[0] // pieces, VOX)
        kernel = functools.partial(add_kernel, len(arrays))
        return small_call(kernel, [shape] * pieces, "added", *arrays, flops=flops)

    sums = [box_sums(near[0], []), box_sums(near[1], [], flops=LARGE)]
    value = box_sums(far[0], sums[0], sums[1][0])
    weight = box_sums(far[1], sums[1], value[0])
    pairs = []
    for parts in (value, weight):
        parts = [parts[0]] + [swap(parts[i], i * plan.sz) for i in range(1, plan.sy)]
        for bit in range(plan.sz.bit_length() - 2):
            keep, give = added(parts, 2)
            parts = [keep, swap(give, 1 << bit)]
        pairs.append(parts)
    (value,) = added(pairs[0], 1, flops=LARGE)
    half = plan.share // 2
    shapes = [(plan.share, 2 * VOX), (half, 2 * VOX), (half, 2 * VOX)]
    keep, *gives = small_call(both_kernel, shapes, "both", value, *pairs[1])
    arrived = [swap(give, plan.sz // 2) for give in gives]
    flip_x, flip_y, flip_z = plan.flip_dev
    orbits, waits = [], []
    for number in range(2):
        kernel = functools.partial(intensity_kernel, number)
        (own,) = small_call(kernel, [(half, VOX)], "intensity", keep, arrived[number], *waits)
        waits = [own]
        orbits.append([own, swap(own, flip_z), swap(own, flip_x), swap(own, flip_x ^ flip_z)])
    first = join(orbits[0], flops=LARGE)
    second = join(orbits[1], first)
    ordered = [first, swap(first, flip_y), second, swap(second, flip_y)]
    (result,) = small_call(functools.partial(unfold_kernel, plan), [(plan.boxes, VOX)], "unfold", *ordered)
    return result.reshape(GX // plan.sx, GY // plan.sy, GZ // plan.sz, BOX_BRICK, VOX)


def solution(mesh):
    return jax.shard_map(
        functools.partial(shards, Plan(mesh)),
        mesh=mesh,
        in_specs=(
            P(AXES, None, None, None),
            P(AXES, None, None, None),
            P(AXES, None, None, None),
            P(),
            P(),
            P(AXES),
            P(AXES, None),
            P(AXES),
        ),
        out_specs=P("bx", "by", "bz", None, None),
        check_vma=False,
    )
```

```python
import functools

import jax
import jax.numpy as jnp
from jax import lax
from jax.experimental import pallas as pl
from jax.experimental.pallas import tpu as pltpu
from jax.sharding import PartitionSpec as P

VOX = 256
LANES = 128
GX = 8
GY = 8
GZ = 4
BOX_BRICK = 64
FLIP_VOX = (0b11100000, 0b00011100, 0b00000011)
FLIP_BOX = (0b110000, 0b001100, 0b000011)
AXES = ("bx", "by", "bz")
POSITIONS = 8
TILE_LIMIT = 56 * 1024 * 1024
VMEM_LIMIT = 24 * 1024 * 1024
LARGE = 10**10
UNFOLD_ORDER = (7, 5, 6, 4, 3, 1, 2, 0)


class Plan:
    def __init__(self, mesh):
        self.sx, self.sy, self.sz = (mesh.shape[name] for name in AXES)
        self.devices = self.sx * self.sy * self.sz
        lx, ly, lz = GX // self.sx, GY // self.sy, GZ // self.sz
        self.boxes = lx * ly * lz * BOX_BRICK
        self.share = self.boxes // 8
        self.flip_dev = ((self.sx - 1) * self.sy * self.sz, (self.sy - 1) * self.sz, self.sz - 1)
        self.half = (self.sx * self.sy * self.sz // 2, self.sy * self.sz // 2, self.sz // 2)
        self.flip_local = (
            (lx - 1) * ly * lz * BOX_BRICK + FLIP_BOX[0],
            (ly - 1) * lz * BOX_BRICK + FLIP_BOX[1],
            (lz - 1) * BOX_BRICK + FLIP_BOX[2],
        )

    def upper(self, device):
        return [(device & half) != 0 for half in self.half]

    def steps(self):
        row = self.sy * self.sz
        return (row, 1), (2 * row, 2)

    def box_row(self, place):
        (gather_a, gather_b), (first, second) = self.steps()
        has = lambda mask: (place & (mask * self.share)) != 0
        other_y = place // (self.sz * self.share) % self.sy
        odd = ((other_y ^ lax.axis_index("by")) & 1) != 0
        part = jnp.where(has(first), jnp.where(odd, 1, 2), 0) + jnp.where(has(second), jnp.where(odd, 2, 1), 0)
        row = (other_y * 4 + part) * self.share + place % self.share
        return jnp.where(has(gather_a) | has(gather_b), -1, row)

    def here(self):
        return (lax.axis_index("bx") * self.sy + lax.axis_index("by")) * self.sz + lax.axis_index("bz")


def masked(flags, masks):
    total = jnp.where(flags[0], masks[0], 0)
    for flag, mask in zip(flags[1:], masks[1:]):
        total = total ^ jnp.where(flag, mask, 0)
    return total


def lane_gather(values, index):
    return jnp.take_along_axis(values, index, axis=1, mode="promise_in_bounds")


def destination(plan, owner, box):
    upper = plan.upper(owner)
    local = box ^ masked(upper, plan.flip_local)
    part = local // plan.share
    row = local % plan.share
    holder = owner ^ masked(upper, plan.flip_dev)
    holder = holder ^ masked([(part & bit) != 0 for bit in (4, 2, 1)], plan.flip_dev)
    return holder * plan.share + row


def accumulate_kernel(plan, angles, lorentz, owner, box, counts, rows, cols, seen, value_out, weight_out, *scratch):
    arrays, sems, turned, partial = scratch[:4], scratch[4], scratch[5], scratch[6]
    frames, positions = counts.shape[0], counts.shape[1]
    blocks = positions // POSITIONS

    def copies(block):
        span = pl.ds(block * POSITIONS, POSITIONS)
        views = [(ref.at[:, span], held.at[:, span]) for ref, held in zip((counts, rows, cols), arrays)]
        views.append((seen.at[span], arrays[3].at[span]))
        return [pltpu.make_async_copy(src, dst, sems.at[block, i]) for i, (src, dst) in enumerate(views)]

    for block in range(blocks):
        for copy in copies(block):
            copy.start()

    tiles = frames * positions
    across = lax.broadcasted_iota(jnp.int32, (tiles, tiles), 1)
    down = lax.broadcasted_iota(jnp.int32, (tiles, tiles), 0)
    flips = masked(plan.upper(owner[...]), FLIP_VOX)
    turned[...] = jnp.sum(jnp.where(across == down, flips, 0), axis=1, keepdims=True)
    ids = destination(plan, owner[...], box[...])
    for out in (value_out, weight_out):
        out[tiles : tiles + 8, :] = jnp.zeros((8, VOX), jnp.float32)
        out[tiles : tiles + 8, :tiles] = jnp.broadcast_to(ids.astype(jnp.float32), (8, tiles))

    @pl.loop(0, blocks)
    def _(block):
        for copy in copies(block):
            copy.wait()
        held_counts, held_rows, held_cols, held_seen = arrays
        lanes = lax.broadcasted_iota(jnp.int32, (POSITIONS, LANES), 1)
        for p in range(POSITIONS):
            at = block * POSITIONS + p
            cols_all = jnp.concatenate([held_cols[f, at] for f in range(frames)], axis=1)
            seen_all = jnp.dot(held_seen[at], cols_all, preferred_element_type=jnp.float32)
            for f in range(frames):
                spread = held_rows[f, at].astype(jnp.float32)
                counted = jnp.dot(held_counts[f, at], held_cols[f, at], preferred_element_type=jnp.float32)
                observed = seen_all[:, f * VOX : (f + 1) * VOX]
                for kind, item in enumerate((counted, observed)):
                    product = jnp.sum((spread * item).reshape(-1, 8, VOX), axis=0)
                    partial[f, kind, 0, p * 8 : (p + 1) * 8, :] = product[:, :LANES]
                    partial[f, kind, 1, p * 8 : (p + 1) * 8, :] = product[:, LANES:]
        for f in range(frames):
            place = pl.ds(pl.multiple_of(f * positions + block * POSITIONS, POSITIONS), POSITIONS)
            mask = jnp.broadcast_to(turned[place, :], (POSITIONS, LANES))
            index = lanes ^ (mask & (LANES - 1))
            swap = (mask & LANES) != 0
            for kind, out in enumerate((value_out, weight_out)):
                low, high = (
                    sum(partial[f, kind, half, pl.ds(row, POSITIONS, stride=8), :] for row in range(8))
                    for half in range(2)
                )
                scale = lorentz[angles[f]] if kind == 0 else 1.0
                out[place, :LANES] = lane_gather(jnp.where(swap, high, low), index) * scale
                out[place, LANES:] = lane_gather(jnp.where(swap, low, high), index) * scale


def accumulate(plan, counts, row_split, col_split, efficiency, lorentz, angles, owner, box):
    frames, positions, pixels, _ = counts.shape
    tiles = frames * positions
    arrays = (counts, row_split, col_split, efficiency)
    return pl.pallas_call(
        functools.partial(accumulate_kernel, plan),
        in_specs=[pl.BlockSpec(memory_space=pltpu.SMEM)] * 2
        + [pl.BlockSpec(memory_space=pltpu.VMEM)] * 2
        + [pl.BlockSpec(memory_space=pl.ANY)] * 4,
        out_specs=[pl.BlockSpec(memory_space=pltpu.VMEM)] * 2,
        out_shape=[jax.ShapeDtypeStruct((tiles + 8, VOX), jnp.float32)] * 2,
        scratch_shapes=[pltpu.VMEM(array.shape, array.dtype) for array in arrays]
        + [
            pltpu.SemaphoreType.DMA((positions // POSITIONS, 4)),
            pltpu.VMEM((tiles, 1), jnp.int32),
            pltpu.VMEM((frames, 2, 2, 8 * POSITIONS, LANES), jnp.float32),
        ],
        compiler_params=pltpu.CompilerParams(vmem_limit_bytes=TILE_LIMIT),
        cost_estimate=pl.CostEstimate(
            flops=4 * tiles * pixels * pixels * VOX,
            bytes_accessed=sum(array.size * 2 for array in arrays),
            transcendentals=0,
        ),
        name="tile_sums",
    )(angles, lorentz, owner, box, *arrays)


def scatter_kernel(plan, olds, outs, payload, *refs):
    before, after = refs[:olds], refs[len(refs) - outs :]
    tiles = LANES
    half = payload.shape[0] // 2
    ids = [payload[start + tiles : start + tiles + 1, :tiles] for start in (0, half)]
    ids = plan.box_row(jnp.concatenate(ids, axis=1).astype(jnp.int32) ^ (plan.here() * plan.share))
    values = jnp.concatenate([payload[:tiles, :], payload[half : half + tiles, :]], axis=0)
    high = values.astype(jnp.bfloat16)
    low = (values - high.astype(jnp.float32)).astype(jnp.bfloat16)
    for number, out in enumerate(after):
        boxes = lax.broadcasted_iota(jnp.int32, (out.shape[0], ids.shape[1]), 0) + number * out.shape[0]
        pick = (boxes == ids).astype(jnp.float32).astype(jnp.bfloat16)
        total = jnp.dot(pick, high, preferred_element_type=jnp.float32)
        total = total + jnp.dot(pick, low, preferred_element_type=jnp.float32)
        out[...] = total + before[number][...] if olds else total


def stage_kernel(first, second, first_out, second_out):
    first_out[...] = first[...]
    second_out[...] = second[...]


def join_kernel(first, second, *rest):
    half, out = first.shape[0], rest[-1]
    out[:half, :] = first[...]
    out[half:, :] = second[...]


def add_kernel(count, *refs):
    inputs, outs = refs[:count], refs[count:]
    start = 0
    for out in outs:
        span = slice(start, start + out.shape[0])
        total = inputs[0][span, :]
        for ref in inputs[1:]:
            total = total + ref[span, :]
        out[...] = total
        start += out.shape[0]


def intensity_kernel(value, *refs):
    inputs, out = refs[:-1], refs[-1]
    weight = inputs[0][...]
    for ref in inputs[1:]:
        weight = weight + ref[...]
    out[...] = value[...] * 0.125 / jnp.maximum(weight * 0.125, 1.0)


def unfold_kernel(plan, *refs):
    inputs, out = refs[:-1], refs[-1]
    upper = plan.upper(plan.here())
    own = masked(upper, (4, 2, 1))
    local = masked(upper, plan.flip_local)
    mask = masked(upper, FLIP_VOX)
    index = lax.broadcasted_iota(jnp.int32, (8, LANES), 1) ^ (mask & (LANES - 1))
    turn = lax.broadcasted_iota(jnp.int32, (8, LANES), 0) ^ (local & 7)
    swap = (mask & LANES) != 0
    for relative, ref in zip(UNFOLD_ORDER, inputs):
        base = (relative ^ own) * plan.share
        for group in range(0, plan.share, 8):
            rows = ref[group : group + 8, :]
            low, high = rows[:, :LANES], rows[:, LANES:]
            target = (base + group) ^ (local & ~7)
            place = pl.ds(pl.multiple_of(target, 8), 8)
            for at, item in enumerate((jnp.where(swap, high, low), jnp.where(swap, low, high))):
                item = jnp.take_along_axis(item, turn, axis=0, mode="promise_in_bounds")
                out[place, at * LANES : (at + 1) * LANES] = lane_gather(item, index)


def small_call(kernel, shapes, name, *arrays, flops=1):
    return pl.pallas_call(
        kernel,
        out_shape=[jax.ShapeDtypeStruct(shape, jnp.float32) for shape in shapes],
        compiler_params=pltpu.CompilerParams(vmem_limit_bytes=VMEM_LIMIT),
        cost_estimate=pl.CostEstimate(flops=flops, bytes_accessed=1, transcendentals=0),
        name=name,
    )(*arrays)


def shards(plan, counts, row_split, col_split, efficiency, lorentz, angles, tile_owner, tile_box):
    def swap(array, even, odd=None):
        odd = even if odd is None else odd
        pairs = [(i, i ^ (odd if i // plan.sz % 2 else even)) for i in range(plan.devices)]
        return lax.ppermute(array, AXES, pairs)

    def join(first, second, *order):
        rows, width = first.shape
        return small_call(join_kernel, [(2 * rows, width)], "join", first, second, *order)[0]

    gather_steps, reduce_steps = plan.steps()
    owner = tile_owner.reshape(1, -1)
    box = tile_box.reshape(1, -1)
    own = accumulate(plan, counts, row_split, col_split, efficiency, lorentz, angles, owner, box)
    arrived = [swap(array, *gather_steps) for array in own]
    held = small_call(stage_kernel, [array.shape for array in own], "stage", *own, flops=LARGE)
    near = [join(held[0], arrived[0])]
    near.append(join(held[1], arrived[1], near[0]))
    far = [swap(array, *gather_steps[::-1]) for array in near]
    def box_sums(payload, olds, *waits, flops=1):
        kernel = functools.partial(scatter_kernel, plan, len(olds), plan.sy)
        shapes = [(4 * plan.share, VOX)] * plan.sy
        return small_call(kernel, shapes, "box_sums", payload, *olds, *waits, flops=flops)

    def added(arrays, pieces, flops=1):
        shape = (arrays[0].shape[0] // pieces, VOX)
        kernel = functools.partial(add_kernel, len(arrays))
        return small_call(kernel, [shape] * pieces, "added", *arrays, flops=flops)

    sums = [box_sums(near[0], []), box_sums(near[1], [], flops=LARGE)]
    value = box_sums(far[0], sums[0], sums[1][0])
    weight = box_sums(far[1], sums[1], value[0])
    pairs = []
    for parts in (value, weight):
        parts = [parts[0]] + [swap(parts[i], i * plan.sz) for i in range(1, plan.sy)]
        for even, odd in (reduce_steps, reduce_steps[::-1]):
            keep, give = added(parts, 2)
            parts = [keep, swap(give, even, odd)]
        pairs.append(parts)
    (value,) = added(pairs[0], 1, flops=LARGE)
    (own,) = small_call(intensity_kernel, [(plan.share, VOX)], "intensity", value, *pairs[1])
    flip_x, flip_y, flip_z = plan.flip_dev
    near = [own, swap(own, flip_z), swap(own, flip_x), swap(own, flip_x ^ flip_z)]
    far = [swap(array, flip_y) for array in near]
    ordered = [array for pair in zip(near, far) for array in pair][::-1]
    (result,) = small_call(functools.partial(unfold_kernel, plan), [(plan.boxes, VOX)], "unfold", *ordered)
    return result.reshape(GX // plan.sx, GY // plan.sy, GZ // plan.sz, BOX_BRICK, VOX)


def solution(mesh):
    return jax.shard_map(
        functools.partial(shards, Plan(mesh)),
        mesh=mesh,
        in_specs=(
            P(AXES, None, None, None),
            P(AXES, None, None, None),
            P(AXES, None, None, None),
            P(),
            P(),
            P(AXES),
            P(AXES, None),
            P(AXES),
        ),
        out_specs=P("bx", "by", "bz", None, None),
        check_vma=False,
    )
```

```python
import functools

import jax
import jax.numpy as jnp
from jax import lax
from jax.experimental import pallas as pl
from jax.experimental.pallas import tpu as pltpu
from jax.sharding import PartitionSpec as P

VOX = 256
LANES = 128
GX = 8
GY = 8
GZ = 4
BOX_BRICK = 64
FLIP_VOX = (0b11100000, 0b00011100, 0b00000011)
FLIP_BOX = (0b110000, 0b001100, 0b000011)
AXES = ("bx", "by", "bz")
POSITIONS = 8
TILE_LIMIT = 56 * 1024 * 1024
VMEM_LIMIT = 24 * 1024 * 1024
LARGE = 10**10
PIXEL_ROWS = 64


class Plan:
    def __init__(self, mesh):
        self.sx, self.sy, self.sz = (mesh.shape[name] for name in AXES)
        self.devices = self.sx * self.sy * self.sz
        lx, ly, lz = GX // self.sx, GY // self.sy, GZ // self.sz
        self.boxes = lx * ly * lz * BOX_BRICK
        self.share = self.boxes // 8
        self.flip_dev = ((self.sx - 1) * self.sy * self.sz, (self.sy - 1) * self.sz, self.sz - 1)
        self.half = (self.sx * self.sy * self.sz // 2, self.sy * self.sz // 2, self.sz // 2)
        self.flip_local = (
            (lx - 1) * ly * lz * BOX_BRICK + FLIP_BOX[0],
            (ly - 1) * lz * BOX_BRICK + FLIP_BOX[1],
            (lz - 1) * BOX_BRICK + FLIP_BOX[2],
        )

    def upper(self, device):
        return [(device & half) != 0 for half in self.half]

    def steps(self):
        row = self.sy * self.sz
        return (row, 1), (2 * row, 2)

    def box_row(self, place):
        (gather_a, gather_b), (first, second) = self.steps()
        has = lambda mask: (place & (mask * self.share)) != 0
        other_y = place // (self.sz * self.share) % self.sy
        odd = ((other_y ^ lax.axis_index("by")) & 1) != 0
        part = jnp.where(has(first), jnp.where(odd, 1, 2), 0) + jnp.where(has(second), jnp.where(odd, 2, 1), 0)
        row = (other_y * 4 + part) * self.share + place % self.share
        return jnp.where(has(gather_a) | has(gather_b), -1, row)

    def here(self):
        return (lax.axis_index("bx") * self.sy + lax.axis_index("by")) * self.sz + lax.axis_index("bz")


def masked(flags, masks):
    total = jnp.where(flags[0], masks[0], 0)
    for flag, mask in zip(flags[1:], masks[1:]):
        total = total ^ jnp.where(flag, mask, 0)
    return total


def lane_gather(values, index):
    return jnp.take_along_axis(values, index, axis=1, mode="promise_in_bounds")


def destination(plan, owner, box):
    upper = plan.upper(owner)
    local = box ^ masked(upper, plan.flip_local)
    part = local // plan.share
    row = local % plan.share
    holder = owner ^ masked(upper, plan.flip_dev)
    holder = holder ^ masked([(part & bit) != 0 for bit in (4, 2, 1)], plan.flip_dev)
    return holder * plan.share + row


def accumulate_kernel(plan, angles, lorentz, owner, box, counts, rows, cols, seen, value_out, weight_out, *scratch):
    arrays, sems, turned, partial = scratch[:4], scratch[4], scratch[5], scratch[6]
    frames, positions = counts.shape[0], counts.shape[1]
    blocks = positions // POSITIONS

    def copies(block):
        span = pl.ds(block * POSITIONS, POSITIONS)
        views = [(ref.at[:, span], held.at[:, span]) for ref, held in zip((counts, rows, cols), arrays)]
        views.append((seen.at[span], arrays[3].at[span]))
        return [pltpu.make_async_copy(src, dst, sems.at[block, i]) for i, (src, dst) in enumerate(views)]

    for block in range(blocks):
        for copy in copies(block):
            copy.start()

    tiles = frames * positions
    across = lax.broadcasted_iota(jnp.int32, (tiles, tiles), 1)
    down = lax.broadcasted_iota(jnp.int32, (tiles, tiles), 0)
    flips = masked(plan.upper(owner[...]), FLIP_VOX)
    turned[...] = jnp.sum(jnp.where(across == down, flips, 0), axis=1, keepdims=True)
    ids = destination(plan, owner[...], box[...])
    for out in (value_out, weight_out):
        out[tiles : tiles + 8, :] = jnp.zeros((8, VOX), jnp.float32)
        out[tiles : tiles + 8, :tiles] = jnp.broadcast_to(ids.astype(jnp.float32), (8, tiles))

    @pl.loop(0, blocks)
    def _(block):
        for copy in copies(block):
            copy.wait()
        held_counts, held_rows, held_cols, held_seen = arrays
        lanes = lax.broadcasted_iota(jnp.int32, (POSITIONS, LANES), 1)
        for p in range(POSITIONS):
            at = block * POSITIONS + p
            for f in range(frames):
                weights = held_cols[f, at]
                for kind in range(2):
                    total = None
                    for start in range(0, held_rows.shape[2], PIXEL_ROWS):
                        span = pl.ds(start, PIXEL_ROWS)
                        pixels = held_seen[at, span, :] if kind else held_counts[f, at, span, :]
                        item = jnp.dot(pixels, weights, preferred_element_type=jnp.float32)
                        item = held_rows[f, at, span, :].astype(jnp.float32) * item
                        item = jnp.sum(item.reshape(-1, 8, VOX), axis=0)
                        total = item if total is None else total + item
                    partial[f, kind, 0, p * 8 : (p + 1) * 8, :] = total[:, :LANES]
                    partial[f, kind, 1, p * 8 : (p + 1) * 8, :] = total[:, LANES:]
        for f in range(frames):
            place = pl.ds(pl.multiple_of(f * positions + block * POSITIONS, POSITIONS), POSITIONS)
            mask = jnp.broadcast_to(turned[place, :], (POSITIONS, LANES))
            index = lanes ^ (mask & (LANES - 1))
            swap = (mask & LANES) != 0
            for kind, out in enumerate((value_out, weight_out)):
                low, high = (
                    sum(partial[f, kind, half, pl.ds(row, POSITIONS, stride=8), :] for row in range(8))
                    for half in range(2)
                )
                scale = lorentz[angles[f]] if kind == 0 else 1.0
                out[place, :LANES] = lane_gather(jnp.where(swap, high, low), index) * scale
                out[place, LANES:] = lane_gather(jnp.where(swap, low, high), index) * scale


def accumulate(plan, counts, row_split, col_split, efficiency, lorentz, angles, owner, box):
    frames, positions, pixels, _ = counts.shape
    tiles = frames * positions
    arrays = (counts, row_split, col_split, efficiency)
    return pl.pallas_call(
        functools.partial(accumulate_kernel, plan),
        in_specs=[pl.BlockSpec(memory_space=pltpu.SMEM)] * 2
        + [pl.BlockSpec(memory_space=pltpu.VMEM)] * 2
        + [pl.BlockSpec(memory_space=pl.ANY)] * 4,
        out_specs=[pl.BlockSpec(memory_space=pltpu.VMEM)] * 2,
        out_shape=[jax.ShapeDtypeStruct((tiles + 8, VOX), jnp.float32)] * 2,
        scratch_shapes=[pltpu.VMEM(array.shape, array.dtype) for array in arrays]
        + [
            pltpu.SemaphoreType.DMA((positions // POSITIONS, 4)),
            pltpu.VMEM((tiles, 1), jnp.int32),
            pltpu.VMEM((frames, 2, 2, 8 * POSITIONS, LANES), jnp.float32),
        ],
        compiler_params=pltpu.CompilerParams(vmem_limit_bytes=TILE_LIMIT),
        cost_estimate=pl.CostEstimate(
            flops=4 * tiles * pixels * pixels * VOX,
            bytes_accessed=sum(array.size * 2 for array in arrays),
            transcendentals=0,
        ),
        name="tile_sums",
    )(angles, lorentz, owner, box, *arrays)


def scatter_kernel(plan, olds, outs, payload, *refs):
    before, after = refs[:olds], refs[len(refs) - outs :]
    tiles = LANES
    half = payload.shape[0] // 2
    ids = [payload[start + tiles : start + tiles + 1, :tiles] for start in (0, half)]
    ids = plan.box_row(jnp.concatenate(ids, axis=1).astype(jnp.int32) ^ (plan.here() * plan.share))
    values = jnp.concatenate([payload[:tiles, :], payload[half : half + tiles, :]], axis=0)
    high = values.astype(jnp.bfloat16)
    low = (values - high.astype(jnp.float32)).astype(jnp.bfloat16)
    for number, out in enumerate(after):
        boxes = lax.broadcasted_iota(jnp.int32, (out.shape[0], ids.shape[1]), 0) + number * out.shape[0]
        pick = (boxes == ids).astype(jnp.float32).astype(jnp.bfloat16)
        total = jnp.dot(pick, high, preferred_element_type=jnp.float32)
        total = total + jnp.dot(pick, low, preferred_element_type=jnp.float32)
        out[...] = total + before[number][...] if olds else total


def stage_kernel(first, second, first_out, second_out):
    first_out[...] = first[...]
    second_out[...] = second[...]


def join_kernel(first, second, *rest):
    half, out = first.shape[0], rest[-1]
    out[:half, :] = first[...]
    out[half:, :] = second[...]


def add_kernel(count, *refs):
    inputs, outs = refs[:count], refs[count:]
    start = 0
    for out in outs:
        span = slice(start, start + out.shape[0])
        total = inputs[0][span, :]
        for ref in inputs[1:]:
            total = total + ref[span, :]
        out[...] = total
        start += out.shape[0]


def intensity_kernel(value, *refs):
    inputs, out = refs[:-1], refs[-1]
    weight = inputs[0][...]
    for ref in inputs[1:]:
        weight = weight + ref[...]
    out[...] = value[...] * 0.125 / jnp.maximum(weight * 0.125, 1.0)


def unfold_kernel(plan, *refs):
    inputs, out = refs[:-1], refs[-1]
    upper = plan.upper(plan.here())
    own = masked(upper, (4, 2, 1))
    local = masked(upper, plan.flip_local)
    mask = masked(upper, FLIP_VOX)
    index = lax.broadcasted_iota(jnp.int32, (8, LANES), 1) ^ (mask & (LANES - 1))
    turn = lax.broadcasted_iota(jnp.int32, (8, LANES), 0) ^ (local & 7)
    swap = (mask & LANES) != 0
    for relative, ref in enumerate(inputs):
        base = (relative ^ own) * plan.share
        for group in range(0, plan.share, 8):
            rows = ref[group : group + 8, :]
            low, high = rows[:, :LANES], rows[:, LANES:]
            target = (base + group) ^ (local & ~7)
            place = pl.ds(pl.multiple_of(target, 8), 8)
            for at, item in enumerate((jnp.where(swap, high, low), jnp.where(swap, low, high))):
                item = jnp.take_along_axis(item, turn, axis=0, mode="promise_in_bounds")
                out[place, at * LANES : (at + 1) * LANES] = lane_gather(item, index)


def small_call(kernel, shapes, name, *arrays, flops=1):
    return pl.pallas_call(
        kernel,
        out_shape=[jax.ShapeDtypeStruct(shape, jnp.float32) for shape in shapes],
        compiler_params=pltpu.CompilerParams(vmem_limit_bytes=VMEM_LIMIT),
        cost_estimate=pl.CostEstimate(flops=flops, bytes_accessed=1, transcendentals=0),
        name=name,
    )(*arrays)


def shards(plan, counts, row_split, col_split, efficiency, lorentz, angles, tile_owner, tile_box):
    def swap(array, even, odd=None):
        odd = even if odd is None else odd
        pairs = [(i, i ^ (odd if i // plan.sz % 2 else even)) for i in range(plan.devices)]
        return lax.ppermute(array, AXES, pairs)

    def join(first, second, *order):
        rows, width = first.shape
        return small_call(join_kernel, [(2 * rows, width)], "join", first, second, *order)[0]

    gather_steps, reduce_steps = plan.steps()
    owner = tile_owner.reshape(1, -1)
    box = tile_box.reshape(1, -1)
    own = accumulate(plan, counts, row_split, col_split, efficiency, lorentz, angles, owner, box)
    arrived = [swap(array, *gather_steps) for array in own]
    held = small_call(stage_kernel, [array.shape for array in own], "stage", *own, flops=LARGE)
    near = [join(held[0], arrived[0])]
    near.append(join(held[1], arrived[1], near[0]))
    far = [swap(array, *gather_steps[::-1]) for array in near]
    def box_sums(payload, olds, *waits, flops=1):
        kernel = functools.partial(scatter_kernel, plan, len(olds), plan.sy)
        shapes = [(4 * plan.share, VOX)] * plan.sy
        return small_call(kernel, shapes, "box_sums", payload, *olds, *waits, flops=flops)

    def added(arrays, pieces, flops=1):
        shape = (arrays[0].shape[0] // pieces, VOX)
        kernel = functools.partial(add_kernel, len(arrays))
        return small_call(kernel, [shape] * pieces, "added", *arrays, flops=flops)

    sums = [box_sums(near[0], []), box_sums(near[1], [], flops=LARGE)]
    value = box_sums(far[0], sums[0], sums[1][0])
    weight = box_sums(far[1], sums[1], value[0])
    pairs = []
    for parts in (value, weight):
        parts = [parts[0]] + [swap(parts[i], i * plan.sz) for i in range(1, plan.sy)]
        for even, odd in (reduce_steps, reduce_steps[::-1]):
            keep, give = added(parts, 2)
            parts = [keep, swap(give, even, odd)]
        pairs.append(parts)
    (value,) = added(pairs[0], 1, flops=LARGE)
    (own,) = small_call(intensity_kernel, [(plan.share, VOX)], "intensity", value, *pairs[1])
    flip_x, flip_y, flip_z = plan.flip_dev
    near = [own, swap(own, flip_z), swap(own, flip_x), swap(own, flip_x ^ flip_z)]
    far = [swap(array, flip_y) for array in near]
    ordered = [near[0], near[1], far[0], far[1], near[2], near[3], far[2], far[3]]
    (result,) = small_call(functools.partial(unfold_kernel, plan), [(plan.boxes, VOX)], "unfold", *ordered)
    return result.reshape(GX // plan.sx, GY // plan.sy, GZ // plan.sz, BOX_BRICK, VOX)


def solution(mesh):
    return jax.shard_map(
        functools.partial(shards, Plan(mesh)),
        mesh=mesh,
        in_specs=(
            P(AXES, None, None, None),
            P(AXES, None, None, None),
            P(AXES, None, None, None),
            P(),
            P(),
            P(AXES),
            P(AXES, None),
            P(AXES),
        ),
        out_specs=P("bx", "by", "bz", None, None),
        check_vma=False,
    )
```

```python
import functools

import jax
import jax.numpy as jnp
from jax import lax
from jax.experimental import pallas as pl
from jax.experimental.pallas import tpu as pltpu
from jax.sharding import PartitionSpec as P

VOX = 256
LANES = 128
GX = 8
GY = 8
GZ = 4
BOX_BRICK = 64
FLIP_VOX = (0b11100000, 0b00011100, 0b00000011)
FLIP_BOX = (0b110000, 0b001100, 0b000011)
AXES = ("bx", "by", "bz")
POSITIONS = 8
FIRST = 2
TILE_LIMIT = 56 * 1024 * 1024
VMEM_LIMIT = 24 * 1024 * 1024
LARGE = 10**10
PIXEL_ROWS = 64


class Plan:
    def __init__(self, mesh):
        self.sx, self.sy, self.sz = (mesh.shape[name] for name in AXES)
        self.devices = self.sx * self.sy * self.sz
        lx, ly, lz = GX // self.sx, GY // self.sy, GZ // self.sz
        self.boxes = lx * ly * lz * BOX_BRICK
        self.share = self.boxes // 8
        self.flip_dev = ((self.sx - 1) * self.sy * self.sz, (self.sy - 1) * self.sz, self.sz - 1)
        self.half = (self.sx * self.sy * self.sz // 2, self.sy * self.sz // 2, self.sz // 2)
        self.flip_local = (
            (lx - 1) * ly * lz * BOX_BRICK + FLIP_BOX[0],
            (ly - 1) * lz * BOX_BRICK + FLIP_BOX[1],
            (lz - 1) * BOX_BRICK + FLIP_BOX[2],
        )

    def upper(self, device):
        return [(device & half) != 0 for half in self.half]

    def steps(self):
        row = self.sy * self.sz
        return (row, 1), (2 * row, 2)

    def box_row(self, place):
        (gather_a, gather_b), (first, second) = self.steps()
        has = lambda mask: (place & (mask * self.share)) != 0
        other_y = place // (self.sz * self.share) % self.sy
        odd = ((other_y ^ lax.axis_index("by")) & 1) != 0
        part = jnp.where(has(first), jnp.where(odd, 1, 2), 0) + jnp.where(has(second), jnp.where(odd, 2, 1), 0)
        row = (other_y * 4 + part) * self.share + place % self.share
        return jnp.where(has(gather_a) | has(gather_b), -1, row)

    def here(self):
        return (lax.axis_index("bx") * self.sy + lax.axis_index("by")) * self.sz + lax.axis_index("bz")


def masked(flags, masks):
    total = jnp.where(flags[0], masks[0], 0)
    for flag, mask in zip(flags[1:], masks[1:]):
        total = total ^ jnp.where(flag, mask, 0)
    return total


def lane_gather(values, index):
    return jnp.take_along_axis(values, index, axis=1, mode="promise_in_bounds")


def destination(plan, owner, box):
    upper = plan.upper(owner)
    local = box ^ masked(upper, plan.flip_local)
    part = local // plan.share
    row = local % plan.share
    holder = owner ^ masked(upper, plan.flip_dev)
    holder = holder ^ masked([(part & bit) != 0 for bit in (4, 2, 1)], plan.flip_dev)
    return holder * plan.share + row


def accumulate_kernel(plan, angles, lorentz, owner, box, counts, rows, cols, seen, value_out, weight_out, *scratch):
    arrays, sems, turned, partial = scratch[:4], scratch[4], scratch[5], scratch[6]
    frames, positions = counts.shape[0], counts.shape[1]
    blocks = positions // POSITIONS

    def copies(start, count, slot):
        span = pl.ds(start, count)
        views = [(ref.at[:, span], held.at[:, span]) for ref, held in zip((counts, rows, cols), arrays)]
        views.append((seen.at[span], arrays[3].at[span]))
        return [pltpu.make_async_copy(src, dst, sems.at[slot, i]) for i, (src, dst) in enumerate(views)]

    early = [(0, FIRST, 0), (FIRST, POSITIONS - FIRST, 1)]
    for start, count, slot in early + [(block * POSITIONS, POSITIONS, block + 1) for block in range(1, blocks)]:
        for copy in copies(start, count, slot):
            copy.start(priority=slot % 2)

    tiles = frames * positions
    across = lax.broadcasted_iota(jnp.int32, (tiles, tiles), 1)
    down = lax.broadcasted_iota(jnp.int32, (tiles, tiles), 0)
    flips = masked(plan.upper(owner[...]), FLIP_VOX)
    turned[...] = jnp.sum(jnp.where(across == down, flips, 0), axis=1, keepdims=True)
    ids = destination(plan, owner[...], box[...])
    for out in (value_out, weight_out):
        out[tiles : tiles + 8, :] = jnp.zeros((8, VOX), jnp.float32)
        out[tiles : tiles + 8, :tiles] = jnp.broadcast_to(ids.astype(jnp.float32), (8, tiles))

    def compute(block, landings):
        held_counts, held_rows, held_cols, held_seen = arrays
        lanes = lax.broadcasted_iota(jnp.int32, (POSITIONS, LANES), 1)
        for p in range(POSITIONS):
            for copy in copies(*landings[p]) if p in landings else ():
                copy.wait()
            at = block * POSITIONS + p
            for f in range(frames):
                weights = held_cols[f, at]
                for kind in range(2):
                    total = None
                    for start in range(0, held_rows.shape[2], PIXEL_ROWS):
                        span = pl.ds(start, PIXEL_ROWS)
                        pixels = held_seen[at, span, :] if kind else held_counts[f, at, span, :]
                        item = jnp.dot(pixels, weights, preferred_element_type=jnp.float32)
                        item = held_rows[f, at, span, :].astype(jnp.float32) * item
                        item = jnp.sum(item.reshape(-1, 8, VOX), axis=0)
                        total = item if total is None else total + item
                    partial[f, kind, 0, p * 8 : (p + 1) * 8, :] = total[:, :LANES]
                    partial[f, kind, 1, p * 8 : (p + 1) * 8, :] = total[:, LANES:]
        for f in range(frames):
            place = pl.ds(pl.multiple_of(f * positions + block * POSITIONS, POSITIONS), POSITIONS)
            mask = jnp.broadcast_to(turned[place, :], (POSITIONS, LANES))
            index = lanes ^ (mask & (LANES - 1))
            swap = (mask & LANES) != 0
            for kind, out in enumerate((value_out, weight_out)):
                low, high = (
                    sum(partial[f, kind, half, pl.ds(row, POSITIONS, stride=8), :] for row in range(8))
                    for half in range(2)
                )
                scale = lorentz[angles[f]] if kind == 0 else 1.0
                out[place, :LANES] = lane_gather(jnp.where(swap, high, low), index) * scale
                out[place, LANES:] = lane_gather(jnp.where(swap, low, high), index) * scale

    compute(0, {landing[0]: landing for landing in early})

    @pl.loop(1, blocks)
    def _(block):
        compute(block, {0: (block * POSITIONS, POSITIONS, block + 1)})


def accumulate(plan, counts, row_split, col_split, efficiency, lorentz, angles, owner, box):
    frames, positions, pixels, _ = counts.shape
    tiles = frames * positions
    arrays = (counts, row_split, col_split, efficiency)
    return pl.pallas_call(
        functools.partial(accumulate_kernel, plan),
        in_specs=[pl.BlockSpec(memory_space=pltpu.SMEM)] * 2
        + [pl.BlockSpec(memory_space=pltpu.VMEM)] * 2
        + [pl.BlockSpec(memory_space=pl.ANY)] * 4,
        out_specs=[pl.BlockSpec(memory_space=pltpu.VMEM)] * 2,
        out_shape=[jax.ShapeDtypeStruct((tiles + 8, VOX), jnp.float32)] * 2,
        scratch_shapes=[pltpu.VMEM(array.shape, array.dtype) for array in arrays]
        + [
            pltpu.SemaphoreType.DMA((positions // POSITIONS + 1, 4)),
            pltpu.VMEM((tiles, 1), jnp.int32),
            pltpu.VMEM((frames, 2, 2, 8 * POSITIONS, LANES), jnp.float32),
        ],
        compiler_params=pltpu.CompilerParams(vmem_limit_bytes=TILE_LIMIT),
        cost_estimate=pl.CostEstimate(
            flops=4 * tiles * pixels * pixels * VOX,
            bytes_accessed=sum(array.size * 2 for array in arrays),
            transcendentals=0,
        ),
        name="tile_sums",
    )(angles, lorentz, owner, box, *arrays)


def scatter_kernel(plan, olds, outs, payload, *refs):
    before, after = refs[:olds], refs[len(refs) - outs :]
    tiles = LANES
    half = payload.shape[0] // 2
    ids = [payload[start + tiles : start + tiles + 1, :tiles] for start in (0, half)]
    ids = plan.box_row(jnp.concatenate(ids, axis=1).astype(jnp.int32) ^ (plan.here() * plan.share))
    values = jnp.concatenate([payload[:tiles, :], payload[half : half + tiles, :]], axis=0)
    high = values.astype(jnp.bfloat16)
    low = (values - high.astype(jnp.float32)).astype(jnp.bfloat16)
    for number, out in enumerate(after):
        boxes = lax.broadcasted_iota(jnp.int32, (out.shape[0], ids.shape[1]), 0) + number * out.shape[0]
        pick = (boxes == ids).astype(jnp.float32).astype(jnp.bfloat16)
        total = jnp.dot(pick, high, preferred_element_type=jnp.float32)
        total = total + jnp.dot(pick, low, preferred_element_type=jnp.float32)
        out[...] = total + before[number][...] if olds else total


def stage_kernel(first, second, first_out, second_out):
    first_out[...] = first[...]
    second_out[...] = second[...]


def join_kernel(first, second, *rest):
    half, out = first.shape[0], rest[-1]
    out[:half, :] = first[...]
    out[half:, :] = second[...]


def add_kernel(count, *refs):
    inputs, outs = refs[:count], refs[count:]
    start = 0
    for out in outs:
        span = slice(start, start + out.shape[0])
        total = inputs[0][span, :]
        for ref in inputs[1:]:
            total = total + ref[span, :]
        out[...] = total
        start += out.shape[0]


def intensity_kernel(value, *refs):
    inputs, out = refs[:-1], refs[-1]
    weight = inputs[0][...]
    for ref in inputs[1:]:
        weight = weight + ref[...]
    out[...] = value[...] * 0.125 / jnp.maximum(weight * 0.125, 1.0)


def unfold_kernel(plan, *refs):
    inputs, out = refs[:-1], refs[-1]
    upper = plan.upper(plan.here())
    own = masked(upper, (4, 2, 1))
    local = masked(upper, plan.flip_local)
    mask = masked(upper, FLIP_VOX)
    index = lax.broadcasted_iota(jnp.int32, (8, LANES), 1) ^ (mask & (LANES - 1))
    turn = lax.broadcasted_iota(jnp.int32, (8, LANES), 0) ^ (local & 7)
    swap = (mask & LANES) != 0
    for relative, ref in enumerate(inputs):
        base = (relative ^ own) * plan.share
        for group in range(0, plan.share, 8):
            rows = ref[group : group + 8, :]
            low, high = rows[:, :LANES], rows[:, LANES:]
            target = (base + group) ^ (local & ~7)
            place = pl.ds(pl.multiple_of(target, 8), 8)
            for at, item in enumerate((jnp.where(swap, high, low), jnp.where(swap, low, high))):
                item = jnp.take_along_axis(item, turn, axis=0, mode="promise_in_bounds")
                out[place, at * LANES : (at + 1) * LANES] = lane_gather(item, index)


def small_call(kernel, shapes, name, *arrays, flops=1):
    return pl.pallas_call(
        kernel,
        out_shape=[jax.ShapeDtypeStruct(shape, jnp.float32) for shape in shapes],
        compiler_params=pltpu.CompilerParams(vmem_limit_bytes=VMEM_LIMIT),
        cost_estimate=pl.CostEstimate(flops=flops, bytes_accessed=1, transcendentals=0),
        name=name,
    )(*arrays)


def shards(plan, counts, row_split, col_split, efficiency, lorentz, angles, tile_owner, tile_box):
    def swap(array, even, odd=None):
        odd = even if odd is None else odd
        pairs = [(i, i ^ (odd if i // plan.sz % 2 else even)) for i in range(plan.devices)]
        return lax.ppermute(array, AXES, pairs)

    def join(first, second, *order):
        rows, width = first.shape
        return small_call(join_kernel, [(2 * rows, width)], "join", first, second, *order)[0]

    gather_steps, reduce_steps = plan.steps()
    owner = tile_owner.reshape(1, -1)
    box = tile_box.reshape(1, -1)
    own = accumulate(plan, counts, row_split, col_split, efficiency, lorentz, angles, owner, box)
    arrived = [swap(array, *gather_steps) for array in own]
    held = small_call(stage_kernel, [array.shape for array in own], "stage", *own, flops=LARGE)
    near = [join(held[0], arrived[0])]
    near.append(join(held[1], arrived[1], near[0]))
    far = [swap(array, *gather_steps[::-1]) for array in near]
    def box_sums(payload, olds, *waits, flops=1):
        kernel = functools.partial(scatter_kernel, plan, len(olds), plan.sy)
        shapes = [(4 * plan.share, VOX)] * plan.sy
        return small_call(kernel, shapes, "box_sums", payload, *olds, *waits, flops=flops)

    def added(arrays, pieces, flops=1):
        shape = (arrays[0].shape[0] // pieces, VOX)
        kernel = functools.partial(add_kernel, len(arrays))
        return small_call(kernel, [shape] * pieces, "added", *arrays, flops=flops)

    sums = [box_sums(near[0], []), box_sums(near[1], [], flops=LARGE)]
    value = box_sums(far[0], sums[0], sums[1][0])
    weight = box_sums(far[1], sums[1], value[0])
    pairs = []
    for parts in (value, weight):
        parts = [parts[0]] + [swap(parts[i], i * plan.sz) for i in range(1, plan.sy)]
        for even, odd in (reduce_steps, reduce_steps[::-1]):
            keep, give = added(parts, 2)
            parts = [keep, swap(give, even, odd)]
        pairs.append(parts)
    (value,) = added(pairs[0], 1, flops=LARGE)
    (own,) = small_call(intensity_kernel, [(plan.share, VOX)], "intensity", value, *pairs[1])
    flip_x, flip_y, flip_z = plan.flip_dev
    near = [own, swap(own, flip_z), swap(own, flip_x), swap(own, flip_x ^ flip_z)]
    far = [swap(array, flip_y) for array in near]
    ordered = [near[0], near[1], far[0], far[1], near[2], near[3], far[2], far[3]]
    (result,) = small_call(functools.partial(unfold_kernel, plan), [(plan.boxes, VOX)], "unfold", *ordered)
    return result.reshape(GX // plan.sx, GY // plan.sy, GZ // plan.sz, BOX_BRICK, VOX)


def solution(mesh):
    return jax.shard_map(
        functools.partial(shards, Plan(mesh)),
        mesh=mesh,
        in_specs=(
            P(AXES, None, None, None),
            P(AXES, None, None, None),
            P(AXES, None, None, None),
            P(),
            P(),
            P(AXES),
            P(AXES, None),
            P(AXES),
        ),
        out_specs=P("bx", "by", "bz", None, None),
        check_vma=False,
    )
```

```python
import functools

import jax
import jax.numpy as jnp
from jax import lax
from jax.experimental import pallas as pl
from jax.experimental.pallas import tpu as pltpu
from jax.sharding import PartitionSpec as P

VOX = 256
LANES = 128
GX = 8
GY = 8
GZ = 4
BOX_BRICK = 64
FLIP_VOX = (0b11100000, 0b00011100, 0b00000011)
FLIP_BOX = (0b110000, 0b001100, 0b000011)
AXES = ("bx", "by", "bz")
POSITIONS = 8
BODY = 4
TILE_LIMIT = 56 * 1024 * 1024
VMEM_LIMIT = 24 * 1024 * 1024
LARGE = 10**10
PIXEL_ROWS = 64


class Plan:
    def __init__(self, mesh):
        self.sx, self.sy, self.sz = (mesh.shape[name] for name in AXES)
        self.devices = self.sx * self.sy * self.sz
        lx, ly, lz = GX // self.sx, GY // self.sy, GZ // self.sz
        self.boxes = lx * ly * lz * BOX_BRICK
        self.share = self.boxes // 8
        self.flip_dev = ((self.sx - 1) * self.sy * self.sz, (self.sy - 1) * self.sz, self.sz - 1)
        self.half = (self.sx * self.sy * self.sz // 2, self.sy * self.sz // 2, self.sz // 2)
        self.flip_local = (
            (lx - 1) * ly * lz * BOX_BRICK + FLIP_BOX[0],
            (ly - 1) * lz * BOX_BRICK + FLIP_BOX[1],
            (lz - 1) * BOX_BRICK + FLIP_BOX[2],
        )

    def upper(self, device):
        return [(device & half) != 0 for half in self.half]

    def steps(self):
        row = self.sy * self.sz
        return (row, 1), (2 * row, 2)

    def box_row(self, place):
        (gather_a, gather_b), (first, second) = self.steps()
        has = lambda mask: (place & (mask * self.share)) != 0
        other_y = place // (self.sz * self.share) % self.sy
        odd = ((other_y ^ lax.axis_index("by")) & 1) != 0
        part = jnp.where(has(first), jnp.where(odd, 1, 2), 0) + jnp.where(has(second), jnp.where(odd, 2, 1), 0)
        row = (other_y * 4 + part) * self.share + place % self.share
        return jnp.where(has(gather_a) | has(gather_b), -1, row)

    def here(self):
        return (lax.axis_index("bx") * self.sy + lax.axis_index("by")) * self.sz + lax.axis_index("bz")


def masked(flags, masks):
    total = jnp.where(flags[0], masks[0], 0)
    for flag, mask in zip(flags[1:], masks[1:]):
        total = total ^ jnp.where(flag, mask, 0)
    return total


def lane_gather(values, index):
    return jnp.take_along_axis(values, index, axis=1, mode="promise_in_bounds")


def destination(plan, owner, box):
    upper = plan.upper(owner)
    local = box ^ masked(upper, plan.flip_local)
    part = local // plan.share
    row = local % plan.share
    holder = owner ^ masked(upper, plan.flip_dev)
    holder = holder ^ masked([(part & bit) != 0 for bit in (4, 2, 1)], plan.flip_dev)
    return holder * plan.share + row


def accumulate_kernel(plan, angles, lorentz, owner, box, counts, rows, cols, seen, value_out, weight_out, *scratch):
    arrays, sems, turned, partial = scratch[:4], scratch[4], scratch[5], scratch[6]
    frames, positions = counts.shape[0], counts.shape[1]
    blocks = positions // POSITIONS

    def copies(block):
        span = pl.ds(block * POSITIONS, POSITIONS)
        views = [(ref.at[:, span], held.at[:, span]) for ref, held in zip((counts, rows, cols), arrays)]
        views.append((seen.at[span], arrays[3].at[span]))
        return [pltpu.make_async_copy(src, dst, sems.at[block, i]) for i, (src, dst) in enumerate(views)]

    for block in range(blocks):
        for copy in copies(block):
            copy.start()

    tiles = frames * positions
    across = lax.broadcasted_iota(jnp.int32, (tiles, tiles), 1)
    down = lax.broadcasted_iota(jnp.int32, (tiles, tiles), 0)
    flips = masked(plan.upper(owner[...]), FLIP_VOX)
    turned[...] = jnp.sum(jnp.where(across == down, flips, 0), axis=1, keepdims=True)
    ids = destination(plan, owner[...], box[...])
    for out in (value_out, weight_out):
        out[tiles : tiles + 8, :] = jnp.zeros((8, VOX), jnp.float32)
        out[tiles : tiles + 8, :tiles] = jnp.broadcast_to(ids.astype(jnp.float32), (8, tiles))

    held_counts, held_rows, held_cols, held_seen = arrays
    turns = POSITIONS // BODY

    @pl.loop(0, blocks * turns)
    def _(turn):
        block, at_turn = turn // turns, turn % turns

        @pl.when(at_turn == 0)
        def _():
            for copy in copies(block):
                copy.wait()

        for p in range(BODY):
            at = turn * BODY + p
            place = pl.ds(pl.multiple_of((at_turn * BODY + p) * 8, 8), 8)
            for f in range(frames):
                weights = held_cols[f, at]
                for kind in range(2):
                    total = None
                    for start in range(0, held_rows.shape[2], PIXEL_ROWS):
                        span = pl.ds(start, PIXEL_ROWS)
                        pixels = held_seen[at, span, :] if kind else held_counts[f, at, span, :]
                        item = jnp.dot(pixels, weights, preferred_element_type=jnp.float32)
                        item = held_rows[f, at, span, :].astype(jnp.float32) * item
                        item = jnp.sum(item.reshape(-1, 8, VOX), axis=0)
                        total = item if total is None else total + item
                    partial[f, kind, 0, place, :] = total[:, :LANES]
                    partial[f, kind, 1, place, :] = total[:, LANES:]

        @pl.when(at_turn == turns - 1)
        def _():
            lanes = lax.broadcasted_iota(jnp.int32, (POSITIONS, LANES), 1)
            for f in range(frames):
                place = pl.ds(pl.multiple_of(f * positions + block * POSITIONS, POSITIONS), POSITIONS)
                mask = jnp.broadcast_to(turned[place, :], (POSITIONS, LANES))
                index = lanes ^ (mask & (LANES - 1))
                swap = (mask & LANES) != 0
                for kind, out in enumerate((value_out, weight_out)):
                    low, high = (
                        sum(partial[f, kind, half, pl.ds(row, POSITIONS, stride=8), :] for row in range(8))
                        for half in range(2)
                    )
                    scale = lorentz[angles[f]] if kind == 0 else 1.0
                    out[place, :LANES] = lane_gather(jnp.where(swap, high, low), index) * scale
                    out[place, LANES:] = lane_gather(jnp.where(swap, low, high), index) * scale


def accumulate(plan, counts, row_split, col_split, efficiency, lorentz, angles, owner, box):
    frames, positions, pixels, _ = counts.shape
    tiles = frames * positions
    arrays = (counts, row_split, col_split, efficiency)
    return pl.pallas_call(
        functools.partial(accumulate_kernel, plan),
        in_specs=[pl.BlockSpec(memory_space=pltpu.SMEM)] * 2
        + [pl.BlockSpec(memory_space=pltpu.VMEM)] * 2
        + [pl.BlockSpec(memory_space=pl.ANY)] * 4,
        out_specs=[pl.BlockSpec(memory_space=pltpu.VMEM)] * 2,
        out_shape=[jax.ShapeDtypeStruct((tiles + 8, VOX), jnp.float32)] * 2,
        scratch_shapes=[pltpu.VMEM(array.shape, array.dtype) for array in arrays]
        + [
            pltpu.SemaphoreType.DMA((positions // POSITIONS, 4)),
            pltpu.VMEM((tiles, 1), jnp.int32),
            pltpu.VMEM((frames, 2, 2, 8 * POSITIONS, LANES), jnp.float32),
        ],
        compiler_params=pltpu.CompilerParams(vmem_limit_bytes=TILE_LIMIT),
        cost_estimate=pl.CostEstimate(
            flops=4 * tiles * pixels * pixels * VOX,
            bytes_accessed=sum(array.size * 2 for array in arrays),
            transcendentals=0,
        ),
        name="tile_sums",
    )(angles, lorentz, owner, box, *arrays)


def scatter_kernel(plan, olds, outs, payload, *refs):
    before, after = refs[:olds], refs[len(refs) - outs :]
    tiles = LANES
    half = payload.shape[0] // 2
    ids = [payload[start + tiles : start + tiles + 1, :tiles] for start in (0, half)]
    ids = plan.box_row(jnp.concatenate(ids, axis=1).astype(jnp.int32) ^ (plan.here() * plan.share))
    values = jnp.concatenate([payload[:tiles, :], payload[half : half + tiles, :]], axis=0)
    high = values.astype(jnp.bfloat16)
    low = (values - high.astype(jnp.float32)).astype(jnp.bfloat16)
    for number, out in enumerate(after):
        boxes = lax.broadcasted_iota(jnp.int32, (out.shape[0], ids.shape[1]), 0) + number * out.shape[0]
        pick = (boxes == ids).astype(jnp.float32).astype(jnp.bfloat16)
        total = jnp.dot(pick, high, preferred_element_type=jnp.float32)
        total = total + jnp.dot(pick, low, preferred_element_type=jnp.float32)
        out[...] = total + before[number][...] if olds else total


def stage_kernel(first, second, first_out, second_out):
    first_out[...] = first[...]
    second_out[...] = second[...]


def join_kernel(first, second, *rest):
    half, out = first.shape[0], rest[-1]
    out[:half, :] = first[...]
    out[half:, :] = second[...]


def add_kernel(count, *refs):
    inputs, outs = refs[:count], refs[count:]
    start = 0
    for out in outs:
        span = slice(start, start + out.shape[0])
        total = inputs[0][span, :]
        for ref in inputs[1:]:
            total = total + ref[span, :]
        out[...] = total
        start += out.shape[0]


def intensity_kernel(value, *refs):
    inputs, out = refs[:-1], refs[-1]
    weight = inputs[0][...]
    for ref in inputs[1:]:
        weight = weight + ref[...]
    out[...] = value[...] * 0.125 / jnp.maximum(weight * 0.125, 1.0)


def unfold_kernel(plan, *refs):
    inputs, out = refs[:-1], refs[-1]
    upper = plan.upper(plan.here())
    own = masked(upper, (4, 2, 1))
    local = masked(upper, plan.flip_local)
    mask = masked(upper, FLIP_VOX)
    index = lax.broadcasted_iota(jnp.int32, (8, LANES), 1) ^ (mask & (LANES - 1))
    turn = lax.broadcasted_iota(jnp.int32, (8, LANES), 0) ^ (local & 7)
    swap = (mask & LANES) != 0
    for relative, ref in enumerate(inputs):
        base = (relative ^ own) * plan.share
        for group in range(0, plan.share, 8):
            rows = ref[group : group + 8, :]
            low, high = rows[:, :LANES], rows[:, LANES:]
            target = (base + group) ^ (local & ~7)
            place = pl.ds(pl.multiple_of(target, 8), 8)
            for at, item in enumerate((jnp.where(swap, high, low), jnp.where(swap, low, high))):
                item = jnp.take_along_axis(item, turn, axis=0, mode="promise_in_bounds")
                out[place, at * LANES : (at + 1) * LANES] = lane_gather(item, index)


def small_call(kernel, shapes, name, *arrays, flops=1):
    return pl.pallas_call(
        kernel,
        out_shape=[jax.ShapeDtypeStruct(shape, jnp.float32) for shape in shapes],
        compiler_params=pltpu.CompilerParams(vmem_limit_bytes=VMEM_LIMIT),
        cost_estimate=pl.CostEstimate(flops=flops, bytes_accessed=1, transcendentals=0),
        name=name,
    )(*arrays)


def shards(plan, counts, row_split, col_split, efficiency, lorentz, angles, tile_owner, tile_box):
    def swap(array, even, odd=None):
        odd = even if odd is None else odd
        pairs = [(i, i ^ (odd if i // plan.sz % 2 else even)) for i in range(plan.devices)]
        return lax.ppermute(array, AXES, pairs)

    def join(first, second, *order):
        rows, width = first.shape
        return small_call(join_kernel, [(2 * rows, width)], "join", first, second, *order)[0]

    gather_steps, reduce_steps = plan.steps()
    owner = tile_owner.reshape(1, -1)
    box = tile_box.reshape(1, -1)
    own = accumulate(plan, counts, row_split, col_split, efficiency, lorentz, angles, owner, box)
    arrived = [swap(array, *gather_steps) for array in own]
    held = small_call(stage_kernel, [array.shape for array in own], "stage", *own, flops=LARGE)
    near = [join(held[0], arrived[0])]
    near.append(join(held[1], arrived[1], near[0]))
    far = [swap(array, *gather_steps[::-1]) for array in near]
    def box_sums(payload, olds, *waits, flops=1):
        kernel = functools.partial(scatter_kernel, plan, len(olds), plan.sy)
        shapes = [(4 * plan.share, VOX)] * plan.sy
        return small_call(kernel, shapes, "box_sums", payload, *olds, *waits, flops=flops)

    def added(arrays, pieces, flops=1):
        shape = (arrays[0].shape[0] // pieces, VOX)
        kernel = functools.partial(add_kernel, len(arrays))
        return small_call(kernel, [shape] * pieces, "added", *arrays, flops=flops)

    sums = [box_sums(near[0], []), box_sums(near[1], [], flops=LARGE)]
    value = box_sums(far[0], sums[0], sums[1][0])
    weight = box_sums(far[1], sums[1], value[0])
    pairs = []
    for parts in (value, weight):
        parts = [parts[0]] + [swap(parts[i], i * plan.sz) for i in range(1, plan.sy)]
        for even, odd in (reduce_steps, reduce_steps[::-1]):
            keep, give = added(parts, 2)
            parts = [keep, swap(give, even, odd)]
        pairs.append(parts)
    (value,) = added(pairs[0], 1, flops=LARGE)
    (own,) = small_call(intensity_kernel, [(plan.share, VOX)], "intensity", value, *pairs[1])
    flip_x, flip_y, flip_z = plan.flip_dev
    near = [own, swap(own, flip_z), swap(own, flip_x), swap(own, flip_x ^ flip_z)]
    far = [swap(array, flip_y) for array in near]
    ordered = [near[0], near[1], far[0], far[1], near[2], near[3], far[2], far[3]]
    (result,) = small_call(functools.partial(unfold_kernel, plan), [(plan.boxes, VOX)], "unfold", *ordered)
    return result.reshape(GX // plan.sx, GY // plan.sy, GZ // plan.sz, BOX_BRICK, VOX)


def solution(mesh):
    return jax.shard_map(
        functools.partial(shards, Plan(mesh)),
        mesh=mesh,
        in_specs=(
            P(AXES, None, None, None),
            P(AXES, None, None, None),
            P(AXES, None, None, None),
            P(),
            P(),
            P(AXES),
            P(AXES, None),
            P(AXES),
        ),
        out_specs=P("bx", "by", "bz", None, None),
        check_vma=False,
    )
```

```python
import functools

import jax
import jax.numpy as jnp
from jax import lax
from jax.experimental import pallas as pl
from jax.experimental.pallas import tpu as pltpu
from jax.sharding import PartitionSpec as P

VOX = 256
LANES = 128
GX = 8
GY = 8
GZ = 4
BOX_BRICK = 64
FLIP_VOX = (0b11100000, 0b00011100, 0b00000011)
FLIP_BOX = (0b110000, 0b001100, 0b000011)
AXES = ("bx", "by", "bz")
POSITIONS = 8
TILE_LIMIT = 56 * 1024 * 1024
VMEM_LIMIT = 24 * 1024 * 1024
LARGE = 10**10
PIXEL_ROWS = 64


class Plan:
    def __init__(self, mesh):
        self.sx, self.sy, self.sz = (mesh.shape[name] for name in AXES)
        self.devices = self.sx * self.sy * self.sz
        lx, ly, lz = GX // self.sx, GY // self.sy, GZ // self.sz
        self.boxes = lx * ly * lz * BOX_BRICK
        self.share = self.boxes // 8
        self.flip_dev = ((self.sx - 1) * self.sy * self.sz, (self.sy - 1) * self.sz, self.sz - 1)
        self.half = (self.sx * self.sy * self.sz // 2, self.sy * self.sz // 2, self.sz // 2)
        self.flip_local = (
            (lx - 1) * ly * lz * BOX_BRICK + FLIP_BOX[0],
            (ly - 1) * lz * BOX_BRICK + FLIP_BOX[1],
            (lz - 1) * BOX_BRICK + FLIP_BOX[2],
        )

    def upper(self, device):
        return [(device & half) != 0 for half in self.half]

    def steps(self):
        row = self.sy * self.sz
        return (row, 1), (2 * row, 2)

    def box_row(self, place):
        (gather_a, gather_b), (first, second) = self.steps()
        has = lambda mask: (place & (mask * self.share)) != 0
        other_y = place // (self.sz * self.share) % self.sy
        odd = ((other_y ^ lax.axis_index("by")) & 1) != 0
        part = jnp.where(has(first), jnp.where(odd, 1, 2), 0) + jnp.where(has(second), jnp.where(odd, 2, 1), 0)
        row = (other_y * 4 + part) * self.share + place % self.share
        return jnp.where(has(gather_a) | has(gather_b), -1, row)

    def here(self):
        return (lax.axis_index("bx") * self.sy + lax.axis_index("by")) * self.sz + lax.axis_index("bz")


def masked(flags, masks):
    total = jnp.where(flags[0], masks[0], 0)
    for flag, mask in zip(flags[1:], masks[1:]):
        total = total ^ jnp.where(flag, mask, 0)
    return total


def lane_gather(values, index):
    return jnp.take_along_axis(values, index, axis=1, mode="promise_in_bounds")


def destination(plan, owner, box):
    upper = plan.upper(owner)
    local = box ^ masked(upper, plan.flip_local)
    part = local // plan.share
    row = local % plan.share
    holder = owner ^ masked(upper, plan.flip_dev)
    holder = holder ^ masked([(part & bit) != 0 for bit in (4, 2, 1)], plan.flip_dev)
    return holder * plan.share + row


def accumulate_kernel(plan, angles, lorentz, owner, box, counts, rows, cols, seen, value_out, weight_out, *scratch):
    arrays, sems, turned, partial = scratch[:4], scratch[4], scratch[5], scratch[6]
    frames, positions = counts.shape[0], counts.shape[1]
    blocks = positions // POSITIONS

    def copies(block):
        span = pl.ds(block * POSITIONS, POSITIONS)
        views = [(ref.at[:, span], held.at[:, span]) for ref, held in zip((counts, rows, cols), arrays)]
        views.append((seen.at[span], arrays[3].at[span]))
        return [pltpu.make_async_copy(src, dst, sems.at[block, i]) for i, (src, dst) in enumerate(views)]

    for block in range(blocks):
        for copy in copies(block):
            copy.start(priority=1 if block == 0 else 0)

    tiles = frames * positions
    across = lax.broadcasted_iota(jnp.int32, (tiles, tiles), 1)
    down = lax.broadcasted_iota(jnp.int32, (tiles, tiles), 0)
    flips = masked(plan.upper(owner[...]), FLIP_VOX)
    turned[...] = jnp.sum(jnp.where(across == down, flips, 0), axis=1, keepdims=True)
    ids = destination(plan, owner[...], box[...])
    for out in (value_out, weight_out):
        out[tiles : tiles + 8, :] = jnp.zeros((8, VOX), jnp.float32)
        out[tiles : tiles + 8, :tiles] = jnp.broadcast_to(ids.astype(jnp.float32), (8, tiles))

    held_counts, held_rows, held_cols, held_seen = arrays

    def compute(block):
        for p in range(POSITIONS):
            at = block * POSITIONS + p
            for f in range(frames):
                weights = held_cols[f, at]
                for kind in range(2):
                    total = None
                    for start in range(0, held_rows.shape[2], PIXEL_ROWS):
                        span = pl.ds(start, PIXEL_ROWS)
                        pixels = held_seen[at, span, :] if kind else held_counts[f, at, span, :]
                        item = jnp.dot(pixels, weights, preferred_element_type=jnp.float32)
                        item = held_rows[f, at, span, :].astype(jnp.float32) * item
                        item = jnp.sum(item.reshape(-1, 8, VOX), axis=0)
                        total = item if total is None else total + item
                    partial[f, kind, 0, p * 8 : (p + 1) * 8, :] = total[:, :LANES]
                    partial[f, kind, 1, p * 8 : (p + 1) * 8, :] = total[:, LANES:]

    def finish(block):
        lanes = lax.broadcasted_iota(jnp.int32, (POSITIONS, LANES), 1)
        for f in range(frames):
            place = pl.ds(pl.multiple_of(f * positions + block * POSITIONS, POSITIONS), POSITIONS)
            mask = jnp.broadcast_to(turned[place, :], (POSITIONS, LANES))
            index = lanes ^ (mask & (LANES - 1))
            swap = (mask & LANES) != 0
            for kind, out in enumerate((value_out, weight_out)):
                low, high = (
                    sum(partial[f, kind, half, pl.ds(row, POSITIONS, stride=8), :] for row in range(8))
                    for half in range(2)
                )
                scale = lorentz[angles[f]] if kind == 0 else 1.0
                out[place, :LANES] = lane_gather(jnp.where(swap, high, low), index) * scale
                out[place, LANES:] = lane_gather(jnp.where(swap, low, high), index) * scale

    partial[...] = jnp.zeros_like(partial)

    @pl.loop(0, blocks)
    def _(block):
        for copy in copies(block):
            copy.wait()
        finish(jnp.maximum(block - 1, 0))
        compute(block)

    finish(blocks - 1)


def accumulate(plan, counts, row_split, col_split, efficiency, lorentz, angles, owner, box):
    frames, positions, pixels, _ = counts.shape
    tiles = frames * positions
    arrays = (counts, row_split, col_split, efficiency)
    return pl.pallas_call(
        functools.partial(accumulate_kernel, plan),
        in_specs=[pl.BlockSpec(memory_space=pltpu.SMEM)] * 2
        + [pl.BlockSpec(memory_space=pltpu.VMEM)] * 2
        + [pl.BlockSpec(memory_space=pl.ANY)] * 4,
        out_specs=[pl.BlockSpec(memory_space=pltpu.VMEM)] * 2,
        out_shape=[jax.ShapeDtypeStruct((tiles + 8, VOX), jnp.float32)] * 2,
        scratch_shapes=[pltpu.VMEM(array.shape, array.dtype) for array in arrays]
        + [
            pltpu.SemaphoreType.DMA((positions // POSITIONS, 4)),
            pltpu.VMEM((tiles, 1), jnp.int32),
            pltpu.VMEM((frames, 2, 2, 8 * POSITIONS, LANES), jnp.float32),
        ],
        compiler_params=pltpu.CompilerParams(vmem_limit_bytes=TILE_LIMIT),
        cost_estimate=pl.CostEstimate(
            flops=4 * tiles * pixels * pixels * VOX,
            bytes_accessed=sum(array.size * 2 for array in arrays),
            transcendentals=0,
        ),
        name="tile_sums",
    )(angles, lorentz, owner, box, *arrays)


def scatter_kernel(plan, olds, outs, payload, *refs):
    before, after = refs[:olds], refs[len(refs) - outs :]
    tiles = LANES
    half = payload.shape[0] // 2
    ids = [payload[start + tiles : start + tiles + 1, :tiles] for start in (0, half)]
    ids = plan.box_row(jnp.concatenate(ids, axis=1).astype(jnp.int32) ^ (plan.here() * plan.share))
    values = jnp.concatenate([payload[:tiles, :], payload[half : half + tiles, :]], axis=0)
    high = values.astype(jnp.bfloat16)
    low = (values - high.astype(jnp.float32)).astype(jnp.bfloat16)
    for number, out in enumerate(after):
        boxes = lax.broadcasted_iota(jnp.int32, (out.shape[0], ids.shape[1]), 0) + number * out.shape[0]
        pick = (boxes == ids).astype(jnp.float32).astype(jnp.bfloat16)
        total = jnp.dot(pick, high, preferred_element_type=jnp.float32)
        total = total + jnp.dot(pick, low, preferred_element_type=jnp.float32)
        out[...] = total + before[number][...] if olds else total


def stage_kernel(first, second, first_out, second_out):
    first_out[...] = first[...]
    second_out[...] = second[...]


def join_kernel(first, second, *rest):
    half, out = first.shape[0], rest[-1]
    out[:half, :] = first[...]
    out[half:, :] = second[...]


def add_kernel(count, *refs):
    inputs, outs = refs[:count], refs[count:]
    start = 0
    for out in outs:
        span = slice(start, start + out.shape[0])
        total = inputs[0][span, :]
        for ref in inputs[1:]:
            total = total + ref[span, :]
        out[...] = total
        start += out.shape[0]


def intensity_kernel(value, *refs):
    inputs, out = refs[:-1], refs[-1]
    weight = inputs[0][...]
    for ref in inputs[1:]:
        weight = weight + ref[...]
    out[...] = value[...] * 0.125 / jnp.maximum(weight * 0.125, 1.0)


def unfold_kernel(plan, *refs):
    inputs, out = refs[:-1], refs[-1]
    upper = plan.upper(plan.here())
    own = masked(upper, (4, 2, 1))
    local = masked(upper, plan.flip_local)
    mask = masked(upper, FLIP_VOX)
    index = lax.broadcasted_iota(jnp.int32, (8, LANES), 1) ^ (mask & (LANES - 1))
    turn = lax.broadcasted_iota(jnp.int32, (8, LANES), 0) ^ (local & 7)
    swap = (mask & LANES) != 0
    for relative, ref in enumerate(inputs):
        base = (relative ^ own) * plan.share
        for group in range(0, plan.share, 8):
            rows = ref[group : group + 8, :]
            low, high = rows[:, :LANES], rows[:, LANES:]
            target = (base + group) ^ (local & ~7)
            place = pl.ds(pl.multiple_of(target, 8), 8)
            for at, item in enumerate((jnp.where(swap, high, low), jnp.where(swap, low, high))):
                item = jnp.take_along_axis(item, turn, axis=0, mode="promise_in_bounds")
                out[place, at * LANES : (at + 1) * LANES] = lane_gather(item, index)


def small_call(kernel, shapes, name, *arrays, flops=1):
    return pl.pallas_call(
        kernel,
        out_shape=[jax.ShapeDtypeStruct(shape, jnp.float32) for shape in shapes],
        compiler_params=pltpu.CompilerParams(vmem_limit_bytes=VMEM_LIMIT),
        cost_estimate=pl.CostEstimate(flops=flops, bytes_accessed=1, transcendentals=0),
        name=name,
    )(*arrays)


def shards(plan, counts, row_split, col_split, efficiency, lorentz, angles, tile_owner, tile_box):
    def swap(array, even, odd=None):
        odd = even if odd is None else odd
        pairs = [(i, i ^ (odd if i // plan.sz % 2 else even)) for i in range(plan.devices)]
        return lax.ppermute(array, AXES, pairs)

    def join(first, second, *order):
        rows, width = first.shape
        return small_call(join_kernel, [(2 * rows, width)], "join", first, second, *order)[0]

    gather_steps, reduce_steps = plan.steps()
    owner = tile_owner.reshape(1, -1)
    box = tile_box.reshape(1, -1)
    own = accumulate(plan, counts, row_split, col_split, efficiency, lorentz, angles, owner, box)
    arrived = [swap(array, *gather_steps) for array in own]
    held = small_call(stage_kernel, [array.shape for array in own], "stage", *own, flops=LARGE)
    near = [join(held[0], arrived[0])]
    near.append(join(held[1], arrived[1], near[0]))
    far = [swap(array, *gather_steps[::-1]) for array in near]
    def box_sums(payload, olds, *waits, flops=1):
        kernel = functools.partial(scatter_kernel, plan, len(olds), plan.sy)
        shapes = [(4 * plan.share, VOX)] * plan.sy
        return small_call(kernel, shapes, "box_sums", payload, *olds, *waits, flops=flops)

    def added(arrays, pieces, flops=1):
        shape = (arrays[0].shape[0] // pieces, VOX)
        kernel = functools.partial(add_kernel, len(arrays))
        return small_call(kernel, [shape] * pieces, "added", *arrays, flops=flops)

    sums = [box_sums(near[0], []), box_sums(near[1], [], flops=LARGE)]
    pairs, waits = [], [sums[1][0]]
    for kind in range(2):
        parts = box_sums(far[kind], sums[kind], *waits, flops=LARGE if kind else 1)
        waits = [parts[0]]
        parts = [parts[0]] + [swap(parts[i], i * plan.sz) for i in range(1, plan.sy)]
        for even, odd in (reduce_steps, reduce_steps[::-1]):
            keep, give = added(parts, 2)
            parts = [keep, swap(give, even, odd)]
        pairs.append(parts)
    (value,) = added(pairs[0], 1, flops=LARGE)
    (own,) = small_call(intensity_kernel, [(plan.share, VOX)], "intensity", value, *pairs[1])
    flip_x, flip_y, flip_z = plan.flip_dev
    near = [own, swap(own, flip_z), swap(own, flip_x), swap(own, flip_x ^ flip_z)]
    far = [swap(array, flip_y) for array in near]
    ordered = [near[0], near[1], far[0], far[1], near[2], near[3], far[2], far[3]]
    (result,) = small_call(functools.partial(unfold_kernel, plan), [(plan.boxes, VOX)], "unfold", *ordered)
    return result.reshape(GX // plan.sx, GY // plan.sy, GZ // plan.sz, BOX_BRICK, VOX)


def solution(mesh):
    return jax.shard_map(
        functools.partial(shards, Plan(mesh)),
        mesh=mesh,
        in_specs=(
            P(AXES, None, None, None),
            P(AXES, None, None, None),
            P(AXES, None, None, None),
            P(),
            P(),
            P(AXES),
            P(AXES, None),
            P(AXES),
        ),
        out_specs=P("bx", "by", "bz", None, None),
        check_vma=False,
    )
```

```python
import functools

import jax
import jax.numpy as jnp
from jax import lax
from jax.experimental import pallas as pl
from jax.experimental.pallas import tpu as pltpu
from jax.sharding import PartitionSpec as P

VOX = 256
LANES = 128
GX = 8
GY = 8
GZ = 4
BOX_BRICK = 64
FLIP_VOX = (0b11100000, 0b00011100, 0b00000011)
FLIP_BOX = (0b110000, 0b001100, 0b000011)
AXES = ("bx", "by", "bz")
POSITIONS = 8
TILE_LIMIT = 56 * 1024 * 1024
VMEM_LIMIT = 24 * 1024 * 1024
LARGE = 10**10
PIXEL_ROWS = 64


class Plan:
    def __init__(self, mesh):
        self.sx, self.sy, self.sz = (mesh.shape[name] for name in AXES)
        self.devices = self.sx * self.sy * self.sz
        lx, ly, lz = GX // self.sx, GY // self.sy, GZ // self.sz
        self.boxes = lx * ly * lz * BOX_BRICK
        self.share = self.boxes // 8
        self.flip_dev = ((self.sx - 1) * self.sy * self.sz, (self.sy - 1) * self.sz, self.sz - 1)
        self.half = (self.sx * self.sy * self.sz // 2, self.sy * self.sz // 2, self.sz // 2)
        self.flip_local = (
            (lx - 1) * ly * lz * BOX_BRICK + FLIP_BOX[0],
            (ly - 1) * lz * BOX_BRICK + FLIP_BOX[1],
            (lz - 1) * BOX_BRICK + FLIP_BOX[2],
        )

    def upper(self, device):
        return [(device & half) != 0 for half in self.half]

    def steps(self):
        row = self.sy * self.sz
        return (row, 1), (2 * row, 2)

    def box_row(self, place):
        (gather_a, gather_b), (first, second) = self.steps()
        has = lambda mask: (place & (mask * self.share)) != 0
        other_y = place // (self.sz * self.share) % self.sy
        odd = ((other_y ^ lax.axis_index("by")) & 1) != 0
        part = jnp.where(has(first), jnp.where(odd, 1, 2), 0) + jnp.where(has(second), jnp.where(odd, 2, 1), 0)
        row = (other_y * 4 + part) * self.share + place % self.share
        return jnp.where(has(gather_a) | has(gather_b), -1, row)

    def here(self):
        return (lax.axis_index("bx") * self.sy + lax.axis_index("by")) * self.sz + lax.axis_index("bz")


def masked(flags, masks):
    total = jnp.where(flags[0], masks[0], 0)
    for flag, mask in zip(flags[1:], masks[1:]):
        total = total ^ jnp.where(flag, mask, 0)
    return total


def lane_gather(values, index):
    return jnp.take_along_axis(values, index, axis=1, mode="promise_in_bounds")


def destination(plan, owner, box):
    upper = plan.upper(owner)
    local = box ^ masked(upper, plan.flip_local)
    part = local // plan.share
    row = local % plan.share
    holder = owner ^ masked(upper, plan.flip_dev)
    holder = holder ^ masked([(part & bit) != 0 for bit in (4, 2, 1)], plan.flip_dev)
    return holder * plan.share + row


def accumulate_kernel(plan, angles, lorentz, owner, box, counts, rows, cols, seen, value_out, weight_out, *scratch):
    arrays, sems, turned, partial = scratch[:4], scratch[4], scratch[5], scratch[6]
    frames, positions = counts.shape[0], counts.shape[1]
    blocks = positions // POSITIONS

    def copies(block):
        span = pl.ds(block * POSITIONS, POSITIONS)
        views = [(ref.at[:, span], held.at[:, span]) for ref, held in zip((counts, rows, cols), arrays)]
        views.append((seen.at[span], arrays[3].at[span]))
        return [pltpu.make_async_copy(src, dst, sems.at[block, i]) for i, (src, dst) in enumerate(views)]

    for block in range(blocks):
        for copy in copies(block):
            copy.start(priority=min(block, 1))

    tiles = frames * positions
    across = lax.broadcasted_iota(jnp.int32, (tiles, tiles), 1)
    down = lax.broadcasted_iota(jnp.int32, (tiles, tiles), 0)
    flips = masked(plan.upper(owner[...]), FLIP_VOX)
    turned[...] = jnp.sum(jnp.where(across == down, flips, 0), axis=1, keepdims=True)
    ids = destination(plan, owner[...], box[...])
    for out in (value_out, weight_out):
        out[tiles : tiles + 8, :] = jnp.zeros((8, VOX), jnp.float32)
        out[tiles : tiles + 8, :tiles] = jnp.broadcast_to(ids.astype(jnp.float32), (8, tiles))

    held_counts, held_rows, held_cols, held_seen = arrays

    def compute(block):
        for p in range(POSITIONS):
            at = block * POSITIONS + p
            for f in range(frames):
                weights = held_cols[f, at]
                for kind in range(2):
                    total = None
                    for start in range(0, held_rows.shape[2], PIXEL_ROWS):
                        span = pl.ds(start, PIXEL_ROWS)
                        pixels = held_seen[at, span, :] if kind else held_counts[f, at, span, :]
                        item = jnp.dot(pixels, weights, preferred_element_type=jnp.float32)
                        item = held_rows[f, at, span, :].astype(jnp.float32) * item
                        item = jnp.sum(item.reshape(-1, 8, VOX), axis=0)
                        total = item if total is None else total + item
                    partial[f, kind, 0, p * 8 : (p + 1) * 8, :] = total[:, :LANES]
                    partial[f, kind, 1, p * 8 : (p + 1) * 8, :] = total[:, LANES:]

    def finish(block):
        lanes = lax.broadcasted_iota(jnp.int32, (POSITIONS, LANES), 1)
        for f in range(frames):
            place = pl.ds(pl.multiple_of(f * positions + block * POSITIONS, POSITIONS), POSITIONS)
            mask = jnp.broadcast_to(turned[place, :], (POSITIONS, LANES))
            index = lanes ^ (mask & (LANES - 1))
            swap = (mask & LANES) != 0
            for kind, out in enumerate((value_out, weight_out)):
                low, high = (
                    sum(partial[f, kind, half, pl.ds(row, POSITIONS, stride=8), :] for row in range(8))
                    for half in range(2)
                )
                scale = lorentz[angles[f]] if kind == 0 else 1.0
                out[place, :LANES] = lane_gather(jnp.where(swap, high, low), index) * scale
                out[place, LANES:] = lane_gather(jnp.where(swap, low, high), index) * scale

    partial[...] = jnp.zeros_like(partial)

    @pl.loop(0, blocks)
    def _(block):
        for copy in copies(block):
            copy.wait()
        finish(jnp.maximum(block - 1, 0))
        compute(block)

    finish(blocks - 1)


def accumulate(plan, counts, row_split, col_split, efficiency, lorentz, angles, owner, box):
    frames, positions, pixels, _ = counts.shape
    tiles = frames * positions
    arrays = (counts, row_split, col_split, efficiency)
    return pl.pallas_call(
        functools.partial(accumulate_kernel, plan),
        in_specs=[pl.BlockSpec(memory_space=pltpu.SMEM)] * 2
        + [pl.BlockSpec(memory_space=pltpu.VMEM)] * 2
        + [pl.BlockSpec(memory_space=pl.ANY)] * 4,
        out_specs=[pl.BlockSpec(memory_space=pltpu.VMEM)] * 2,
        out_shape=[jax.ShapeDtypeStruct((tiles + 8, VOX), jnp.float32)] * 2,
        scratch_shapes=[pltpu.VMEM(array.shape, array.dtype) for array in arrays]
        + [
            pltpu.SemaphoreType.DMA((positions // POSITIONS, 4)),
            pltpu.VMEM((tiles, 1), jnp.int32),
            pltpu.VMEM((frames, 2, 2, 8 * POSITIONS, LANES), jnp.float32),
        ],
        compiler_params=pltpu.CompilerParams(vmem_limit_bytes=TILE_LIMIT),
        cost_estimate=pl.CostEstimate(
            flops=4 * tiles * pixels * pixels * VOX,
            bytes_accessed=sum(array.size * 2 for array in arrays),
            transcendentals=0,
        ),
        name="tile_sums",
    )(angles, lorentz, owner, box, *arrays)


def scatter_kernel(plan, olds, outs, payload, *refs):
    before, after = refs[:olds], refs[len(refs) - outs :]
    tiles = LANES
    half = payload.shape[0] // 2
    ids = [payload[start + tiles : start + tiles + 1, :tiles] for start in (0, half)]
    ids = plan.box_row(jnp.concatenate(ids, axis=1).astype(jnp.int32) ^ (plan.here() * plan.share))
    values = jnp.concatenate([payload[:tiles, :], payload[half : half + tiles, :]], axis=0)
    high = values.astype(jnp.bfloat16)
    low = (values - high.astype(jnp.float32)).astype(jnp.bfloat16)
    for number, out in enumerate(after):
        boxes = lax.broadcasted_iota(jnp.int32, (out.shape[0], ids.shape[1]), 0) + number * out.shape[0]
        pick = (boxes == ids).astype(jnp.float32).astype(jnp.bfloat16)
        total = jnp.dot(pick, high, preferred_element_type=jnp.float32)
        total = total + jnp.dot(pick, low, preferred_element_type=jnp.float32)
        out[...] = total + before[number][...] if olds else total


def stage_kernel(first, second, first_out, second_out):
    first_out[...] = first[...]
    second_out[...] = second[...]


def join_kernel(first, second, *rest):
    half, out = first.shape[0], rest[-1]
    out[:half, :] = first[...]
    out[half:, :] = second[...]


def add_kernel(count, *refs):
    inputs, outs = refs[:count], refs[count:]
    start = 0
    for out in outs:
        span = slice(start, start + out.shape[0])
        total = inputs[0][span, :]
        for ref in inputs[1:]:
            total = total + ref[span, :]
        out[...] = total
        start += out.shape[0]


def intensity_kernel(value, *refs):
    inputs, out = refs[:-1], refs[-1]
    weight = inputs[0][...]
    for ref in inputs[1:]:
        weight = weight + ref[...]
    out[...] = value[...] * 0.125 / jnp.maximum(weight * 0.125, 1.0)


def unfold_kernel(plan, *refs):
    inputs, out = refs[:-1], refs[-1]
    upper = plan.upper(plan.here())
    own = masked(upper, (4, 2, 1))
    local = masked(upper, plan.flip_local)
    mask = masked(upper, FLIP_VOX)
    index = lax.broadcasted_iota(jnp.int32, (8, LANES), 1) ^ (mask & (LANES - 1))
    turn = lax.broadcasted_iota(jnp.int32, (8, LANES), 0) ^ (local & 7)
    swap = (mask & LANES) != 0
    for relative, ref in enumerate(inputs):
        base = (relative ^ own) * plan.share
        for group in range(0, plan.share, 8):
            rows = ref[group : group + 8, :]
            low, high = rows[:, :LANES], rows[:, LANES:]
            target = (base + group) ^ (local & ~7)
            place = pl.ds(pl.multiple_of(target, 8), 8)
            for at, item in enumerate((jnp.where(swap, high, low), jnp.where(swap, low, high))):
                item = jnp.take_along_axis(item, turn, axis=0, mode="promise_in_bounds")
                out[place, at * LANES : (at + 1) * LANES] = lane_gather(item, index)


def small_call(kernel, shapes, name, *arrays, flops=1):
    return pl.pallas_call(
        kernel,
        out_shape=[jax.ShapeDtypeStruct(shape, jnp.float32) for shape in shapes],
        compiler_params=pltpu.CompilerParams(vmem_limit_bytes=VMEM_LIMIT),
        cost_estimate=pl.CostEstimate(flops=flops, bytes_accessed=1, transcendentals=0),
        name=name,
    )(*arrays)


def shards(plan, counts, row_split, col_split, efficiency, lorentz, angles, tile_owner, tile_box):
    def swap(array, even, odd=None):
        odd = even if odd is None else odd
        pairs = [(i, i ^ (odd if i // plan.sz % 2 else even)) for i in range(plan.devices)]
        return lax.ppermute(array, AXES, pairs)

    def join(first, second, *order):
        rows, width = first.shape
        return small_call(join_kernel, [(2 * rows, width)], "join", first, second, *order)[0]

    gather_steps, reduce_steps = plan.steps()
    owner = tile_owner.reshape(1, -1)
    box = tile_box.reshape(1, -1)
    own = accumulate(plan, counts, row_split, col_split, efficiency, lorentz, angles, owner, box)
    arrived = [swap(array, *gather_steps) for array in own]
    held = small_call(stage_kernel, [array.shape for array in own], "stage", *own, flops=LARGE)
    near = [join(held[0], arrived[0])]
    near.append(join(held[1], arrived[1], near[0]))
    far = [swap(array, *gather_steps[::-1]) for array in near]
    def box_sums(payload, olds, *waits, flops=1):
        kernel = functools.partial(scatter_kernel, plan, len(olds), plan.sy)
        shapes = [(4 * plan.share, VOX)] * plan.sy
        return small_call(kernel, shapes, "box_sums", payload, *olds, *waits, flops=flops)

    def added(arrays, pieces, flops=1):
        shape = (arrays[0].shape[0] // pieces, VOX)
        kernel = functools.partial(add_kernel, len(arrays))
        return small_call(kernel, [shape] * pieces, "added", *arrays, flops=flops)

    sums = [box_sums(near[0], []), box_sums(near[1], [], flops=LARGE)]
    pairs, waits = [], [sums[1][0]]
    for kind in range(2):
        parts = box_sums(far[kind], sums[kind], *waits, flops=LARGE if kind else 1)
        waits = [parts[0]]
        parts = [parts[0]] + [swap(parts[i], i * plan.sz) for i in range(1, plan.sy)]
        for even, odd in (reduce_steps, reduce_steps[::-1]):
            keep, give = added(parts, 2)
            parts = [keep, swap(give, even, odd)]
        pairs.append(parts)
    (value,) = added(pairs[0], 1, flops=LARGE)
    (own,) = small_call(intensity_kernel, [(plan.share, VOX)], "intensity", value, *pairs[1])
    flip_x, flip_y, flip_z = plan.flip_dev
    near = [own, swap(own, flip_z), swap(own, flip_x), swap(own, flip_x ^ flip_z)]
    far = [swap(array, flip_y) for array in near]
    ordered = [near[0], near[1], far[0], far[1], near[2], near[3], far[2], far[3]]
    (result,) = small_call(functools.partial(unfold_kernel, plan), [(plan.boxes, VOX)], "unfold", *ordered)
    return result.reshape(GX // plan.sx, GY // plan.sy, GZ // plan.sz, BOX_BRICK, VOX)


def solution(mesh):
    return jax.shard_map(
        functools.partial(shards, Plan(mesh)),
        mesh=mesh,
        in_specs=(
            P(AXES, None, None, None),
            P(AXES, None, None, None),
            P(AXES, None, None, None),
            P(),
            P(),
            P(AXES),
            P(AXES, None),
            P(AXES),
        ),
        out_specs=P("bx", "by", "bz", None, None),
        check_vma=False,
    )
```

```python
import functools

import jax
import jax.numpy as jnp
from jax import lax
from jax.experimental import pallas as pl
from jax.experimental.pallas import tpu as pltpu
from jax.sharding import PartitionSpec as P

VOX = 256
LANES = 128
GX = 8
GY = 8
GZ = 4
BOX_BRICK = 64
FLIP_VOX = (0b11100000, 0b00011100, 0b00000011)
FLIP_BOX = (0b110000, 0b001100, 0b000011)
AXES = ("bx", "by", "bz")
POSITIONS = 8
AHEAD = 3
TILE_LIMIT = 56 * 1024 * 1024
VMEM_LIMIT = 24 * 1024 * 1024
LARGE = 10**10
PIXEL_ROWS = 64


class Plan:
    def __init__(self, mesh):
        self.sx, self.sy, self.sz = (mesh.shape[name] for name in AXES)
        self.devices = self.sx * self.sy * self.sz
        lx, ly, lz = GX // self.sx, GY // self.sy, GZ // self.sz
        self.boxes = lx * ly * lz * BOX_BRICK
        self.share = self.boxes // 8
        self.flip_dev = ((self.sx - 1) * self.sy * self.sz, (self.sy - 1) * self.sz, self.sz - 1)
        self.half = (self.sx * self.sy * self.sz // 2, self.sy * self.sz // 2, self.sz // 2)
        self.flip_local = (
            (lx - 1) * ly * lz * BOX_BRICK + FLIP_BOX[0],
            (ly - 1) * lz * BOX_BRICK + FLIP_BOX[1],
            (lz - 1) * BOX_BRICK + FLIP_BOX[2],
        )

    def upper(self, device):
        return [(device & half) != 0 for half in self.half]

    def steps(self):
        row = self.sy * self.sz
        return (row, 1), (2 * row, 2)

    def box_row(self, place):
        (gather_a, gather_b), (first, second) = self.steps()
        has = lambda mask: (place & (mask * self.share)) != 0
        other_y = place // (self.sz * self.share) % self.sy
        odd = ((other_y ^ lax.axis_index("by")) & 1) != 0
        part = jnp.where(has(first), jnp.where(odd, 1, 2), 0) + jnp.where(has(second), jnp.where(odd, 2, 1), 0)
        row = (other_y * 4 + part) * self.share + place % self.share
        return jnp.where(has(gather_a) | has(gather_b), -1, row)

    def here(self):
        return (lax.axis_index("bx") * self.sy + lax.axis_index("by")) * self.sz + lax.axis_index("bz")


def masked(flags, masks):
    total = jnp.where(flags[0], masks[0], 0)
    for flag, mask in zip(flags[1:], masks[1:]):
        total = total ^ jnp.where(flag, mask, 0)
    return total


def lane_gather(values, index):
    return jnp.take_along_axis(values, index, axis=1, mode="promise_in_bounds")


def destination(plan, owner, box):
    upper = plan.upper(owner)
    local = box ^ masked(upper, plan.flip_local)
    part = local // plan.share
    row = local % plan.share
    holder = owner ^ masked(upper, plan.flip_dev)
    holder = holder ^ masked([(part & bit) != 0 for bit in (4, 2, 1)], plan.flip_dev)
    return holder * plan.share + row


def accumulate_kernel(plan, angles, lorentz, owner, box, counts, rows, cols, seen, value_out, weight_out, *scratch):
    arrays, sems, turned, partial = scratch[:4], scratch[4], scratch[5], scratch[6]
    frames, positions = counts.shape[0], counts.shape[1]
    blocks = positions // POSITIONS

    def copies(block):
        span = pl.ds(block * POSITIONS, POSITIONS)
        views = [(ref.at[:, span], held.at[:, span]) for ref, held in zip((counts, rows, cols), arrays)]
        views.append((seen.at[span], arrays[3].at[span]))
        return [pltpu.make_async_copy(src, dst, sems.at[block, i]) for i, (src, dst) in enumerate(views)]

    for block in range(AHEAD):
        for copy in copies(block):
            copy.start()

    tiles = frames * positions
    across = lax.broadcasted_iota(jnp.int32, (tiles, tiles), 1)
    down = lax.broadcasted_iota(jnp.int32, (tiles, tiles), 0)
    flips = masked(plan.upper(owner[...]), FLIP_VOX)
    turned[...] = jnp.sum(jnp.where(across == down, flips, 0), axis=1, keepdims=True)
    ids = destination(plan, owner[...], box[...])
    for out in (value_out, weight_out):
        out[tiles : tiles + 8, :] = jnp.zeros((8, VOX), jnp.float32)
        out[tiles : tiles + 8, :tiles] = jnp.broadcast_to(ids.astype(jnp.float32), (8, tiles))

    held_counts, held_rows, held_cols, held_seen = arrays

    def compute(block):
        for p in range(POSITIONS):
            at = block * POSITIONS + p
            for f in range(frames):
                weights = held_cols[f, at]
                for kind in range(2):
                    total = None
                    for start in range(0, held_rows.shape[2], PIXEL_ROWS):
                        span = pl.ds(start, PIXEL_ROWS)
                        pixels = held_seen[at, span, :] if kind else held_counts[f, at, span, :]
                        item = jnp.dot(pixels, weights, preferred_element_type=jnp.float32)
                        item = held_rows[f, at, span, :].astype(jnp.float32) * item
                        item = jnp.sum(item.reshape(-1, 8, VOX), axis=0)
                        total = item if total is None else total + item
                    partial[f, kind, 0, p * 8 : (p + 1) * 8, :] = total[:, :LANES]
                    partial[f, kind, 1, p * 8 : (p + 1) * 8, :] = total[:, LANES:]

    def finish(block):
        lanes = lax.broadcasted_iota(jnp.int32, (POSITIONS, LANES), 1)
        for f in range(frames):
            place = pl.ds(pl.multiple_of(f * positions + block * POSITIONS, POSITIONS), POSITIONS)
            mask = jnp.broadcast_to(turned[place, :], (POSITIONS, LANES))
            index = lanes ^ (mask & (LANES - 1))
            swap = (mask & LANES) != 0
            for kind, out in enumerate((value_out, weight_out)):
                low, high = (
                    sum(partial[f, kind, half, pl.ds(row, POSITIONS, stride=8), :] for row in range(8))
                    for half in range(2)
                )
                scale = lorentz[angles[f]] if kind == 0 else 1.0
                out[place, :LANES] = lane_gather(jnp.where(swap, high, low), index) * scale
                out[place, LANES:] = lane_gather(jnp.where(swap, low, high), index) * scale

    partial[...] = jnp.zeros_like(partial)

    @pl.loop(0, blocks)
    def _(block):
        for copy in copies(block):
            copy.wait()

        @pl.when(block + AHEAD < blocks)
        def _():
            for copy in copies(block + AHEAD):
                copy.start()

        finish(jnp.maximum(block - 1, 0))
        compute(block)

    finish(blocks - 1)


def accumulate(plan, counts, row_split, col_split, efficiency, lorentz, angles, owner, box):
    frames, positions, pixels, _ = counts.shape
    tiles = frames * positions
    arrays = (counts, row_split, col_split, efficiency)
    return pl.pallas_call(
        functools.partial(accumulate_kernel, plan),
        in_specs=[pl.BlockSpec(memory_space=pltpu.SMEM)] * 2
        + [pl.BlockSpec(memory_space=pltpu.VMEM)] * 2
        + [pl.BlockSpec(memory_space=pl.ANY)] * 4,
        out_specs=[pl.BlockSpec(memory_space=pltpu.VMEM)] * 2,
        out_shape=[jax.ShapeDtypeStruct((tiles + 8, VOX), jnp.float32)] * 2,
        scratch_shapes=[pltpu.VMEM(array.shape, array.dtype) for array in arrays]
        + [
            pltpu.SemaphoreType.DMA((positions // POSITIONS, 4)),
            pltpu.VMEM((tiles, 1), jnp.int32),
            pltpu.VMEM((frames, 2, 2, 8 * POSITIONS, LANES), jnp.float32),
        ],
        compiler_params=pltpu.CompilerParams(vmem_limit_bytes=TILE_LIMIT),
        cost_estimate=pl.CostEstimate(
            flops=4 * tiles * pixels * pixels * VOX,
            bytes_accessed=sum(array.size * 2 for array in arrays),
            transcendentals=0,
        ),
        name="tile_sums",
    )(angles, lorentz, owner, box, *arrays)


def scatter_kernel(plan, olds, outs, payload, *refs):
    before, after = refs[:olds], refs[len(refs) - outs :]
    tiles = LANES
    half = payload.shape[0] // 2
    ids = [payload[start + tiles : start + tiles + 1, :tiles] for start in (0, half)]
    ids = plan.box_row(jnp.concatenate(ids, axis=1).astype(jnp.int32) ^ (plan.here() * plan.share))
    values = jnp.concatenate([payload[:tiles, :], payload[half : half + tiles, :]], axis=0)
    high = values.astype(jnp.bfloat16)
    low = (values - high.astype(jnp.float32)).astype(jnp.bfloat16)
    for number, out in enumerate(after):
        boxes = lax.broadcasted_iota(jnp.int32, (out.shape[0], ids.shape[1]), 0) + number * out.shape[0]
        pick = (boxes == ids).astype(jnp.float32).astype(jnp.bfloat16)
        total = jnp.dot(pick, high, preferred_element_type=jnp.float32)
        total = total + jnp.dot(pick, low, preferred_element_type=jnp.float32)
        out[...] = total + before[number][...] if olds else total


def stage_kernel(first, second, first_out, second_out):
    first_out[...] = first[...]
    second_out[...] = second[...]


def join_kernel(first, second, *rest):
    half, out = first.shape[0], rest[-1]
    out[:half, :] = first[...]
    out[half:, :] = second[...]


def add_kernel(count, *refs):
    inputs, outs = refs[:count], refs[count:]
    start = 0
    for out in outs:
        span = slice(start, start + out.shape[0])
        total = inputs[0][span, :]
        for ref in inputs[1:]:
            total = total + ref[span, :]
        out[...] = total
        start += out.shape[0]


def intensity_kernel(value, *refs):
    inputs, out = refs[:-1], refs[-1]
    weight = inputs[0][...]
    for ref in inputs[1:]:
        weight = weight + ref[...]
    out[...] = value[...] * 0.125 / jnp.maximum(weight * 0.125, 1.0)


def unfold_kernel(plan, *refs):
    inputs, out = refs[:-1], refs[-1]
    upper = plan.upper(plan.here())
    own = masked(upper, (4, 2, 1))
    local = masked(upper, plan.flip_local)
    mask = masked(upper, FLIP_VOX)
    index = lax.broadcasted_iota(jnp.int32, (8, LANES), 1) ^ (mask & (LANES - 1))
    turn = lax.broadcasted_iota(jnp.int32, (8, LANES), 0) ^ (local & 7)
    swap = (mask & LANES) != 0
    for relative, ref in enumerate(inputs):
        base = (relative ^ own) * plan.share
        for group in range(0, plan.share, 8):
            rows = ref[group : group + 8, :]
            low, high = rows[:, :LANES], rows[:, LANES:]
            target = (base + group) ^ (local & ~7)
            place = pl.ds(pl.multiple_of(target, 8), 8)
            for at, item in enumerate((jnp.where(swap, high, low), jnp.where(swap, low, high))):
                item = jnp.take_along_axis(item, turn, axis=0, mode="promise_in_bounds")
                out[place, at * LANES : (at + 1) * LANES] = lane_gather(item, index)


def small_call(kernel, shapes, name, *arrays, flops=1):
    return pl.pallas_call(
        kernel,
        out_shape=[jax.ShapeDtypeStruct(shape, jnp.float32) for shape in shapes],
        compiler_params=pltpu.CompilerParams(vmem_limit_bytes=VMEM_LIMIT),
        cost_estimate=pl.CostEstimate(flops=flops, bytes_accessed=1, transcendentals=0),
        name=name,
    )(*arrays)


def shards(plan, counts, row_split, col_split, efficiency, lorentz, angles, tile_owner, tile_box):
    def swap(array, even, odd=None):
        odd = even if odd is None else odd
        pairs = [(i, i ^ (odd if i // plan.sz % 2 else even)) for i in range(plan.devices)]
        return lax.ppermute(array, AXES, pairs)

    def join(first, second, *order):
        rows, width = first.shape
        return small_call(join_kernel, [(2 * rows, width)], "join", first, second, *order)[0]

    gather_steps, reduce_steps = plan.steps()
    owner = tile_owner.reshape(1, -1)
    box = tile_box.reshape(1, -1)
    own = accumulate(plan, counts, row_split, col_split, efficiency, lorentz, angles, owner, box)
    arrived = [swap(array, *gather_steps) for array in own]
    held = small_call(stage_kernel, [array.shape for array in own], "stage", *own, flops=LARGE)
    near = [join(held[0], arrived[0])]
    near.append(join(held[1], arrived[1], near[0]))
    far = [swap(array, *gather_steps[::-1]) for array in near]
    def box_sums(payload, olds, *waits, flops=1):
        kernel = functools.partial(scatter_kernel, plan, len(olds), plan.sy)
        shapes = [(4 * plan.share, VOX)] * plan.sy
        return small_call(kernel, shapes, "box_sums", payload, *olds, *waits, flops=flops)

    def added(arrays, pieces, flops=1):
        shape = (arrays[0].shape[0] // pieces, VOX)
        kernel = functools.partial(add_kernel, len(arrays))
        return small_call(kernel, [shape] * pieces, "added", *arrays, flops=flops)

    sums = [box_sums(near[0], []), box_sums(near[1], [], flops=LARGE)]
    pairs, waits = [], [sums[1][0]]
    for kind in range(2):
        parts = box_sums(far[kind], sums[kind], *waits, flops=LARGE if kind else 1)
        waits = [parts[0]]
        parts = [parts[0]] + [swap(parts[i], i * plan.sz) for i in range(1, plan.sy)]
        for even, odd in (reduce_steps, reduce_steps[::-1]):
            keep, give = added(parts, 2)
            parts = [keep, swap(give, even, odd)]
        pairs.append(parts)
    (value,) = added(pairs[0], 1, flops=LARGE)
    (own,) = small_call(intensity_kernel, [(plan.share, VOX)], "intensity", value, *pairs[1])
    flip_x, flip_y, flip_z = plan.flip_dev
    near = [own, swap(own, flip_z), swap(own, flip_x)]
    near.append(swap(near[1], flip_x))
    far = [swap(array, flip_y) for array in near]
    ordered = [near[0], near[1], far[0], far[1], near[2], near[3], far[2], far[3]]
    (result,) = small_call(functools.partial(unfold_kernel, plan), [(plan.boxes, VOX)], "unfold", *ordered)
    return result.reshape(GX // plan.sx, GY // plan.sy, GZ // plan.sz, BOX_BRICK, VOX)


def solution(mesh):
    return jax.shard_map(
        functools.partial(shards, Plan(mesh)),
        mesh=mesh,
        in_specs=(
            P(AXES, None, None, None),
            P(AXES, None, None, None),
            P(AXES, None, None, None),
            P(),
            P(),
            P(AXES),
            P(AXES, None),
            P(AXES),
        ),
        out_specs=P("bx", "by", "bz", None, None),
        check_vma=False,
    )
```

```python
import functools

import jax
import jax.numpy as jnp
from jax import lax
from jax.experimental import pallas as pl
from jax.experimental.pallas import tpu as pltpu
from jax.sharding import PartitionSpec as P

VOX = 256
LANES = 128
GX = 8
GY = 8
GZ = 4
BOX_BRICK = 64
FLIP_VOX = (0b11100000, 0b00011100, 0b00000011)
FLIP_BOX = (0b110000, 0b001100, 0b000011)
AXES = ("bx", "by", "bz")
POSITIONS = 8
TILE_LIMIT = 56 * 1024 * 1024
VMEM_LIMIT = 24 * 1024 * 1024
LARGE = 10**10
SWAPPED = (0, 4, 2, 6, 1, 5, 3, 7)
PIXEL_ROWS = 64


class Plan:
    def __init__(self, mesh):
        self.sx, self.sy, self.sz = (mesh.shape[name] for name in AXES)
        self.devices = self.sx * self.sy * self.sz
        lx, ly, lz = GX // self.sx, GY // self.sy, GZ // self.sz
        self.boxes = lx * ly * lz * BOX_BRICK
        self.share = self.boxes // 8
        self.flip_dev = ((self.sx - 1) * self.sy * self.sz, (self.sy - 1) * self.sz, self.sz - 1)
        self.half = (self.sx * self.sy * self.sz // 2, self.sy * self.sz // 2, self.sz // 2)
        self.flip_local = (
            (lx - 1) * ly * lz * BOX_BRICK + FLIP_BOX[0],
            (ly - 1) * lz * BOX_BRICK + FLIP_BOX[1],
            (lz - 1) * BOX_BRICK + FLIP_BOX[2],
        )

    def upper(self, device):
        return [(device & half) != 0 for half in self.half]

    def steps(self):
        row = self.sy * self.sz
        return (row, 1), (2 * row, 2)

    def box_row(self, place):
        (gather_a, gather_b), (first, second) = self.steps()
        has = lambda mask: (place & (mask * self.share)) != 0
        other_y = place // (self.sz * self.share) % self.sy
        odd = ((other_y ^ lax.axis_index("by")) & 1) != 0
        part = jnp.where(has(first), jnp.where(odd, 1, 2), 0) + jnp.where(has(second), jnp.where(odd, 2, 1), 0)
        row = (other_y * 4 + part) * self.share + place % self.share
        return jnp.where(has(gather_a) | has(gather_b), -1, row)

    def here(self):
        return (lax.axis_index("bx") * self.sy + lax.axis_index("by")) * self.sz + lax.axis_index("bz")


def masked(flags, masks):
    total = jnp.where(flags[0], masks[0], 0)
    for flag, mask in zip(flags[1:], masks[1:]):
        total = total ^ jnp.where(flag, mask, 0)
    return total


def lane_gather(values, index):
    return jnp.take_along_axis(values, index, axis=1, mode="promise_in_bounds")


def destination(plan, owner, box):
    upper = plan.upper(owner)
    local = box ^ masked(upper, plan.flip_local)
    part = local // plan.share
    row = local % plan.share
    holder = owner ^ masked(upper, plan.flip_dev)
    holder = holder ^ masked([(part & bit) != 0 for bit in (4, 2, 1)], plan.flip_dev)
    return holder * plan.share + row


def accumulate_kernel(plan, angles, lorentz, owner, box, counts, rows, cols, seen, value_out, weight_out, *scratch):
    arrays, sems, turned, partial = scratch[:4], scratch[4], scratch[5], scratch[6]
    frames, positions = counts.shape[0], counts.shape[1]
    blocks = positions // POSITIONS

    def copies(block):
        span = pl.ds(block * POSITIONS, POSITIONS)
        views = [(ref.at[:, span], held.at[:, span]) for ref, held in zip((counts, rows, cols), arrays)]
        views.append((seen.at[span], arrays[3].at[span]))
        return [pltpu.make_async_copy(src, dst, sems.at[block, i]) for i, (src, dst) in enumerate(views)]

    for block in range(blocks):
        for copy in copies(block):
            copy.start()

    tiles = frames * positions
    across = lax.broadcasted_iota(jnp.int32, (tiles, tiles), 1)
    down = lax.broadcasted_iota(jnp.int32, (tiles, tiles), 0)
    flips = masked(plan.upper(owner[...]), FLIP_VOX)
    turned[...] = jnp.sum(jnp.where(across == down, flips, 0), axis=1, keepdims=True)
    ids = destination(plan, owner[...], box[...])
    for out in (value_out, weight_out):
        out[tiles : tiles + 8, :] = jnp.zeros((8, VOX), jnp.float32)
        out[tiles : tiles + 8, :tiles] = jnp.broadcast_to(ids.astype(jnp.float32), (8, tiles))

    held_counts, held_rows, held_cols, held_seen = arrays

    def compute(block):
        for p in range(POSITIONS):
            at = block * POSITIONS + p
            for f in range(frames):
                weights = held_cols[f, at]
                for kind in range(2):
                    total = None
                    for start in range(0, held_rows.shape[2], PIXEL_ROWS):
                        span = pl.ds(start, PIXEL_ROWS)
                        pixels = held_seen[at, span, :] if kind else held_counts[f, at, span, :]
                        item = jnp.dot(pixels, weights, preferred_element_type=jnp.float32)
                        item = held_rows[f, at, span, :].astype(jnp.float32) * item
                        item = jnp.sum(item.reshape(-1, 8, VOX), axis=0)
                        total = item if total is None else total + item
                    partial[f, kind, 0, p * 8 : (p + 1) * 8, :] = total[:, :LANES]
                    partial[f, kind, 1, p * 8 : (p + 1) * 8, :] = total[:, LANES:]

    def finish(block):
        lanes = lax.broadcasted_iota(jnp.int32, (POSITIONS, LANES), 1)
        for f in range(frames):
            place = pl.ds(pl.multiple_of(f * positions + block * POSITIONS, POSITIONS), POSITIONS)
            mask = jnp.broadcast_to(turned[place, :], (POSITIONS, LANES))
            index = lanes ^ (mask & (LANES - 1))
            swap = (mask & LANES) != 0
            for kind, out in enumerate((value_out, weight_out)):
                low, high = (
                    sum(partial[f, kind, half, pl.ds(row, POSITIONS, stride=8), :] for row in range(8))
                    for half in range(2)
                )
                scale = lorentz[angles[f]] if kind == 0 else 1.0
                out[place, :LANES] = lane_gather(jnp.where(swap, high, low), index) * scale
                out[place, LANES:] = lane_gather(jnp.where(swap, low, high), index) * scale

    @pl.loop(0, blocks)
    def _(block):
        for copy in copies(block):
            copy.wait()
        compute(block)
        finish(block)


def accumulate(plan, counts, row_split, col_split, efficiency, lorentz, angles, owner, box):
    frames, positions, pixels, _ = counts.shape
    tiles = frames * positions
    arrays = (counts, row_split, col_split, efficiency)
    return pl.pallas_call(
        functools.partial(accumulate_kernel, plan),
        in_specs=[pl.BlockSpec(memory_space=pltpu.SMEM)] * 2
        + [pl.BlockSpec(memory_space=pltpu.VMEM)] * 2
        + [pl.BlockSpec(memory_space=pl.ANY)] * 4,
        out_specs=[pl.BlockSpec(memory_space=pltpu.VMEM)] * 2,
        out_shape=[jax.ShapeDtypeStruct((tiles + 8, VOX), jnp.float32)] * 2,
        scratch_shapes=[pltpu.VMEM(array.shape, array.dtype) for array in arrays]
        + [
            pltpu.SemaphoreType.DMA((positions // POSITIONS, 4)),
            pltpu.VMEM((tiles, 1), jnp.int32),
            pltpu.VMEM((frames, 2, 2, 8 * POSITIONS, LANES), jnp.float32),
        ],
        compiler_params=pltpu.CompilerParams(vmem_limit_bytes=TILE_LIMIT),
        cost_estimate=pl.CostEstimate(
            flops=4 * tiles * pixels * pixels * VOX,
            bytes_accessed=sum(array.size * 2 for array in arrays),
            transcendentals=0,
        ),
        name="tile_sums",
    )(angles, lorentz, owner, box, *arrays)


def scatter_kernel(plan, olds, outs, payload, *refs):
    before, after = refs[:olds], refs[len(refs) - outs :]
    tiles = LANES
    half = payload.shape[0] // 2
    ids = [payload[start + tiles : start + tiles + 1, :tiles] for start in (0, half)]
    ids = plan.box_row(jnp.concatenate(ids, axis=1).astype(jnp.int32) ^ (plan.here() * plan.share))
    values = jnp.concatenate([payload[:tiles, :], payload[half : half + tiles, :]], axis=0)
    high = values.astype(jnp.bfloat16)
    low = (values - high.astype(jnp.float32)).astype(jnp.bfloat16)
    for number, out in enumerate(after):
        boxes = lax.broadcasted_iota(jnp.int32, (out.shape[0], ids.shape[1]), 0) + number * out.shape[0]
        pick = (boxes == ids).astype(jnp.float32).astype(jnp.bfloat16)
        total = jnp.dot(pick, high, preferred_element_type=jnp.float32)
        total = total + jnp.dot(pick, low, preferred_element_type=jnp.float32)
        out[...] = total + before[number][...] if olds else total


def stage_kernel(first, second, first_out, second_out):
    first_out[...] = first[...]
    second_out[...] = second[...]


def join_kernel(first, second, *rest):
    half, out = first.shape[0], rest[-1]
    out[:half, :] = first[...]
    out[half:, :] = second[...]


def add_kernel(count, *refs):
    inputs, outs = refs[:count], refs[count:]
    start = 0
    for out in outs:
        span = slice(start, start + out.shape[0])
        total = inputs[0][span, :]
        for ref in inputs[1:]:
            total = total + ref[span, :]
        out[...] = total
        start += out.shape[0]


def intensity_kernel(value, *refs):
    inputs, out = refs[:-1], refs[-1]
    weight = inputs[0][...]
    for ref in inputs[1:]:
        weight = weight + ref[...]
    out[...] = value[...] * 0.125 / jnp.maximum(weight * 0.125, 1.0)


def unfold_kernel(plan, *refs):
    inputs, out = refs[:-1], refs[-1]
    upper = plan.upper(plan.here())
    own = masked(upper, (4, 2, 1))
    local = masked(upper, plan.flip_local)
    mask = masked(upper, FLIP_VOX)
    index = lax.broadcasted_iota(jnp.int32, (8, LANES), 1) ^ (mask & (LANES - 1))
    turn = lax.broadcasted_iota(jnp.int32, (8, LANES), 0) ^ (local & 7)
    swap = (mask & LANES) != 0
    odd = (lax.axis_index("by") & 1) != 0
    for number, ref in enumerate(inputs):
        codes = (number, SWAPPED[number])
        far = (number & 2) != 0
        relative = jnp.where(odd, codes[1 - far], codes[far])
        base = (relative ^ own) * plan.share
        for group in range(0, plan.share, 8):
            rows = ref[group : group + 8, :]
            low, high = rows[:, :LANES], rows[:, LANES:]
            target = (base + group) ^ (local & ~7)
            place = pl.ds(pl.multiple_of(target, 8), 8)
            for at, item in enumerate((jnp.where(swap, high, low), jnp.where(swap, low, high))):
                item = jnp.take_along_axis(item, turn, axis=0, mode="promise_in_bounds")
                out[place, at * LANES : (at + 1) * LANES] = lane_gather(item, index)


def small_call(kernel, shapes, name, *arrays, flops=1):
    return pl.pallas_call(
        kernel,
        out_shape=[jax.ShapeDtypeStruct(shape, jnp.float32) for shape in shapes],
        compiler_params=pltpu.CompilerParams(vmem_limit_bytes=VMEM_LIMIT),
        cost_estimate=pl.CostEstimate(flops=flops, bytes_accessed=1, transcendentals=0),
        name=name,
    )(*arrays)


def shards(plan, counts, row_split, col_split, efficiency, lorentz, angles, tile_owner, tile_box):
    def swap(array, even, odd=None):
        odd = even if odd is None else odd
        pairs = [(i, i ^ (odd if i // plan.sz % 2 else even)) for i in range(plan.devices)]
        return lax.ppermute(array, AXES, pairs)

    def join(first, second, *order):
        rows, width = first.shape
        return small_call(join_kernel, [(2 * rows, width)], "join", first, second, *order)[0]

    gather_steps, reduce_steps = plan.steps()
    owner = tile_owner.reshape(1, -1)
    box = tile_box.reshape(1, -1)
    own = accumulate(plan, counts, row_split, col_split, efficiency, lorentz, angles, owner, box)
    arrived = [swap(array, *gather_steps) for array in own]
    held = small_call(stage_kernel, [array.shape for array in own], "stage", *own, flops=LARGE)
    near = [join(held[0], arrived[0])]
    near.append(join(held[1], arrived[1], near[0]))
    far = [swap(array, *gather_steps[::-1]) for array in near]
    def box_sums(payload, olds, *waits, flops=1):
        kernel = functools.partial(scatter_kernel, plan, len(olds), plan.sy)
        shapes = [(4 * plan.share, VOX)] * plan.sy
        return small_call(kernel, shapes, "box_sums", payload, *olds, *waits, flops=flops)

    def added(arrays, pieces, flops=1):
        shape = (arrays[0].shape[0] // pieces, VOX)
        kernel = functools.partial(add_kernel, len(arrays))
        return small_call(kernel, [shape] * pieces, "added", *arrays, flops=flops)

    sums = [box_sums(near[0], []), box_sums(near[1], [], flops=LARGE)]
    pairs, waits = [], [sums[1][0]]
    for kind in range(2):
        parts = box_sums(far[kind], sums[kind], *waits, flops=LARGE if kind else 1)
        waits = [parts[0]]
        parts = [parts[0]] + [swap(parts[i], i * plan.sz) for i in range(1, plan.sy)]
        for even, odd in (reduce_steps, reduce_steps[::-1]):
            keep, give = added(parts, 2)
            parts = [keep, swap(give, even, odd)]
        pairs.append(parts)
    (value,) = added(pairs[0], 1, flops=LARGE)
    (own,) = small_call(intensity_kernel, [(plan.share, VOX)], "intensity", value, *pairs[1])
    flip_x, flip_y, flip_z = plan.flip_dev
    near = [own, swap(own, flip_z, flip_x), swap(own, flip_x, flip_z)]
    near.append(swap(near[1], flip_x, flip_z))
    far = [swap(array, flip_y) for array in near]
    ordered = [near[0], near[1], far[0], far[1], near[2], near[3], far[2], far[3]]
    (result,) = small_call(functools.partial(unfold_kernel, plan), [(plan.boxes, VOX)], "unfold", *ordered)
    return result.reshape(GX // plan.sx, GY // plan.sy, GZ // plan.sz, BOX_BRICK, VOX)


def solution(mesh):
    return jax.shard_map(
        functools.partial(shards, Plan(mesh)),
        mesh=mesh,
        in_specs=(
            P(AXES, None, None, None),
            P(AXES, None, None, None),
            P(AXES, None, None, None),
            P(),
            P(),
            P(AXES),
            P(AXES, None),
            P(AXES),
        ),
        out_specs=P("bx", "by", "bz", None, None),
        check_vma=False,
    )
```

```python
import functools

import jax
import jax.numpy as jnp
from jax import lax
from jax.experimental import pallas as pl
from jax.experimental.pallas import tpu as pltpu
from jax.sharding import PartitionSpec as P

VOX = 256
LANES = 128
GX = 8
GY = 8
GZ = 4
BOX_BRICK = 64
FLIP_VOX = (0b11100000, 0b00011100, 0b00000011)
FLIP_BOX = (0b110000, 0b001100, 0b000011)
AXES = ("bx", "by", "bz")
POSITIONS = 8
BLOCKS = 2
TILE_LIMIT = 56 * 1024 * 1024
VMEM_LIMIT = 24 * 1024 * 1024
LARGE = 10**10
SWAPPED = (0, 4, 2, 6, 1, 5, 3, 7)
PIXEL_ROWS = 64


class Plan:
    def __init__(self, mesh):
        self.sx, self.sy, self.sz = (mesh.shape[name] for name in AXES)
        self.devices = self.sx * self.sy * self.sz
        lx, ly, lz = GX // self.sx, GY // self.sy, GZ // self.sz
        self.boxes = lx * ly * lz * BOX_BRICK
        self.share = self.boxes // 8
        self.flip_dev = ((self.sx - 1) * self.sy * self.sz, (self.sy - 1) * self.sz, self.sz - 1)
        self.half = (self.sx * self.sy * self.sz // 2, self.sy * self.sz // 2, self.sz // 2)
        self.flip_local = (
            (lx - 1) * ly * lz * BOX_BRICK + FLIP_BOX[0],
            (ly - 1) * lz * BOX_BRICK + FLIP_BOX[1],
            (lz - 1) * BOX_BRICK + FLIP_BOX[2],
        )

    def upper(self, device):
        return [(device & half) != 0 for half in self.half]

    def steps(self):
        row = self.sy * self.sz
        return (row, 1), (2 * row, 2)

    def box_row(self, place):
        (gather_a, gather_b), (first, second) = self.steps()
        has = lambda mask: (place & (mask * self.share)) != 0
        other_y = place // (self.sz * self.share) % self.sy
        odd = ((other_y ^ lax.axis_index("by")) & 1) != 0
        part = jnp.where(has(first), jnp.where(odd, 1, 2), 0) + jnp.where(has(second), jnp.where(odd, 2, 1), 0)
        row = (other_y * 4 + part) * self.share + place % self.share
        return jnp.where(has(gather_a) | has(gather_b), -1, row)

    def here(self):
        return (lax.axis_index("bx") * self.sy + lax.axis_index("by")) * self.sz + lax.axis_index("bz")


def masked(flags, masks):
    total = jnp.where(flags[0], masks[0], 0)
    for flag, mask in zip(flags[1:], masks[1:]):
        total = total ^ jnp.where(flag, mask, 0)
    return total


def lane_gather(values, index):
    return jnp.take_along_axis(values, index, axis=1, mode="promise_in_bounds")


def destination(plan, owner, box):
    upper = plan.upper(owner)
    local = box ^ masked(upper, plan.flip_local)
    part = local // plan.share
    row = local % plan.share
    holder = owner ^ masked(upper, plan.flip_dev)
    holder = holder ^ masked([(part & bit) != 0 for bit in (4, 2, 1)], plan.flip_dev)
    return holder * plan.share + row


def accumulate_kernel(plan, angles, lorentz, owner, box, counts, rows, cols, seen, value_out, weight_out, *scratch):
    arrays, sems, turned, partial = scratch[:4], scratch[4], scratch[5], scratch[6]
    frames, positions = counts.shape[0], counts.shape[1]
    blocks = positions // POSITIONS

    def copies(block):
        span = pl.ds(block * POSITIONS, POSITIONS)
        views = [(ref.at[:, span], held.at[:, span]) for ref, held in zip((counts, rows, cols), arrays)]
        views.append((seen.at[span], arrays[3].at[span]))
        return [pltpu.make_async_copy(src, dst, sems.at[block, i]) for i, (src, dst) in enumerate(views)]

    for block in range(blocks):
        for copy in copies(block):
            copy.start()

    tiles = frames * positions
    across = lax.broadcasted_iota(jnp.int32, (tiles, tiles), 1)
    down = lax.broadcasted_iota(jnp.int32, (tiles, tiles), 0)
    flips = masked(plan.upper(owner[...]), FLIP_VOX)
    turned[...] = jnp.sum(jnp.where(across == down, flips, 0), axis=1, keepdims=True)
    ids = destination(plan, owner[...], box[...])
    for out in (value_out, weight_out):
        out[tiles : tiles + 8, :] = jnp.zeros((8, VOX), jnp.float32)
        out[tiles : tiles + 8, :tiles] = jnp.broadcast_to(ids.astype(jnp.float32), (8, tiles))

    held_counts, held_rows, held_cols, held_seen = arrays

    def compute(block, base):
        for p in range(POSITIONS):
            at = block * POSITIONS + p
            for f in range(frames):
                weights = held_cols[f, at]
                for kind in range(2):
                    total = None
                    for start in range(0, held_rows.shape[2], PIXEL_ROWS):
                        span = pl.ds(start, PIXEL_ROWS)
                        pixels = held_seen[at, span, :] if kind else held_counts[f, at, span, :]
                        item = jnp.dot(pixels, weights, preferred_element_type=jnp.float32)
                        item = held_rows[f, at, span, :].astype(jnp.float32) * item
                        item = jnp.sum(item.reshape(-1, 8, VOX), axis=0)
                        total = item if total is None else total + item
                    partial[base, f, kind, 0, p * 8 : (p + 1) * 8, :] = total[:, :LANES]
                    partial[base, f, kind, 1, p * 8 : (p + 1) * 8, :] = total[:, LANES:]

    def finish(block, base):
        lanes = lax.broadcasted_iota(jnp.int32, (POSITIONS, LANES), 1)
        for f in range(frames):
            place = pl.ds(pl.multiple_of(f * positions + block * POSITIONS, POSITIONS), POSITIONS)
            mask = jnp.broadcast_to(turned[place, :], (POSITIONS, LANES))
            index = lanes ^ (mask & (LANES - 1))
            swap = (mask & LANES) != 0
            for kind, out in enumerate((value_out, weight_out)):
                low, high = (
                    sum(partial[base, f, kind, half, pl.ds(row, POSITIONS, stride=8), :] for row in range(8))
                    for half in range(2)
                )
                scale = lorentz[angles[f]] if kind == 0 else 1.0
                out[place, :LANES] = lane_gather(jnp.where(swap, high, low), index) * scale
                out[place, LANES:] = lane_gather(jnp.where(swap, low, high), index) * scale

    @pl.loop(0, blocks // BLOCKS)
    def _(turn):
        for base in range(BLOCKS):
            block = turn * BLOCKS + base
            for copy in copies(block):
                copy.wait()
            compute(block, base)
            finish(block, base)


def accumulate(plan, counts, row_split, col_split, efficiency, lorentz, angles, owner, box):
    frames, positions, pixels, _ = counts.shape
    tiles = frames * positions
    arrays = (counts, row_split, col_split, efficiency)
    return pl.pallas_call(
        functools.partial(accumulate_kernel, plan),
        in_specs=[pl.BlockSpec(memory_space=pltpu.SMEM)] * 2
        + [pl.BlockSpec(memory_space=pltpu.VMEM)] * 2
        + [pl.BlockSpec(memory_space=pl.ANY)] * 4,
        out_specs=[pl.BlockSpec(memory_space=pltpu.VMEM)] * 2,
        out_shape=[jax.ShapeDtypeStruct((tiles + 8, VOX), jnp.float32)] * 2,
        scratch_shapes=[pltpu.VMEM(array.shape, array.dtype) for array in arrays]
        + [
            pltpu.SemaphoreType.DMA((positions // POSITIONS, 4)),
            pltpu.VMEM((tiles, 1), jnp.int32),
            pltpu.VMEM((BLOCKS, frames, 2, 2, 8 * POSITIONS, LANES), jnp.float32),
        ],
        compiler_params=pltpu.CompilerParams(vmem_limit_bytes=TILE_LIMIT),
        cost_estimate=pl.CostEstimate(
            flops=4 * tiles * pixels * pixels * VOX,
            bytes_accessed=sum(array.size * 2 for array in arrays),
            transcendentals=0,
        ),
        name="tile_sums",
    )(angles, lorentz, owner, box, *arrays)


def scatter_kernel(plan, olds, outs, payload, *refs):
    before, after = refs[:olds], refs[len(refs) - outs :]
    tiles = LANES
    half = payload.shape[0] // 2
    ids = [payload[start + tiles : start + tiles + 1, :tiles] for start in (0, half)]
    ids = plan.box_row(jnp.concatenate(ids, axis=1).astype(jnp.int32) ^ (plan.here() * plan.share))
    values = jnp.concatenate([payload[:tiles, :], payload[half : half + tiles, :]], axis=0)
    high = values.astype(jnp.bfloat16)
    low = (values - high.astype(jnp.float32)).astype(jnp.bfloat16)
    for number, out in enumerate(after):
        boxes = lax.broadcasted_iota(jnp.int32, (out.shape[0], ids.shape[1]), 0) + number * out.shape[0]
        pick = (boxes == ids).astype(jnp.float32).astype(jnp.bfloat16)
        total = jnp.dot(pick, high, preferred_element_type=jnp.float32)
        total = total + jnp.dot(pick, low, preferred_element_type=jnp.float32)
        out[...] = total + before[number][...] if olds else total


def stage_kernel(first, second, first_out, second_out):
    first_out[...] = first[...]
    second_out[...] = second[...]


def join_kernel(first, second, *rest):
    half, out = first.shape[0], rest[-1]
    out[:half, :] = first[...]
    out[half:, :] = second[...]


def add_kernel(count, *refs):
    inputs, outs = refs[:count], refs[count:]
    start = 0
    for out in outs:
        span = slice(start, start + out.shape[0])
        total = inputs[0][span, :]
        for ref in inputs[1:]:
            total = total + ref[span, :]
        out[...] = total
        start += out.shape[0]


def intensity_kernel(value, *refs):
    inputs, out = refs[:-1], refs[-1]
    weight = inputs[0][...]
    for ref in inputs[1:]:
        weight = weight + ref[...]
    out[...] = value[...] * 0.125 / jnp.maximum(weight * 0.125, 1.0)


def unfold_kernel(plan, *refs):
    inputs, out = refs[:-1], refs[-1]
    upper = plan.upper(plan.here())
    own = masked(upper, (4, 2, 1))
    local = masked(upper, plan.flip_local)
    mask = masked(upper, FLIP_VOX)
    index = lax.broadcasted_iota(jnp.int32, (8, LANES), 1) ^ (mask & (LANES - 1))
    turn = lax.broadcasted_iota(jnp.int32, (8, LANES), 0) ^ (local & 7)
    swap = (mask & LANES) != 0
    odd = (lax.axis_index("by") & 1) != 0
    for number, ref in enumerate(inputs):
        codes = (number, SWAPPED[number])
        far = (number & 2) != 0
        relative = jnp.where(odd, codes[1 - far], codes[far])
        base = (relative ^ own) * plan.share
        for group in range(0, plan.share, 8):
            rows = ref[group : group + 8, :]
            low, high = rows[:, :LANES], rows[:, LANES:]
            target = (base + group) ^ (local & ~7)
            place = pl.ds(pl.multiple_of(target, 8), 8)
            for at, item in enumerate((jnp.where(swap, high, low), jnp.where(swap, low, high))):
                item = jnp.take_along_axis(item, turn, axis=0, mode="promise_in_bounds")
                out[place, at * LANES : (at + 1) * LANES] = lane_gather(item, index)


def small_call(kernel, shapes, name, *arrays, flops=1):
    return pl.pallas_call(
        kernel,
        out_shape=[jax.ShapeDtypeStruct(shape, jnp.float32) for shape in shapes],
        compiler_params=pltpu.CompilerParams(vmem_limit_bytes=VMEM_LIMIT),
        cost_estimate=pl.CostEstimate(flops=flops, bytes_accessed=1, transcendentals=0),
        name=name,
    )(*arrays)


def shards(plan, counts, row_split, col_split, efficiency, lorentz, angles, tile_owner, tile_box):
    def swap(array, even, odd=None):
        odd = even if odd is None else odd
        pairs = [(i, i ^ (odd if i // plan.sz % 2 else even)) for i in range(plan.devices)]
        return lax.ppermute(array, AXES, pairs)

    def join(first, second, *order):
        rows, width = first.shape
        return small_call(join_kernel, [(2 * rows, width)], "join", first, second, *order)[0]

    gather_steps, reduce_steps = plan.steps()
    owner = tile_owner.reshape(1, -1)
    box = tile_box.reshape(1, -1)
    own = accumulate(plan, counts, row_split, col_split, efficiency, lorentz, angles, owner, box)
    arrived = [swap(array, *gather_steps) for array in own]
    held = small_call(stage_kernel, [array.shape for array in own], "stage", *own, flops=LARGE)
    near = [join(held[0], arrived[0])]
    near.append(join(held[1], arrived[1], near[0]))
    far = [swap(array, *gather_steps[::-1]) for array in near]
    def box_sums(payload, olds, *waits, flops=1):
        kernel = functools.partial(scatter_kernel, plan, len(olds), plan.sy)
        shapes = [(4 * plan.share, VOX)] * plan.sy
        return small_call(kernel, shapes, "box_sums", payload, *olds, *waits, flops=flops)

    def added(arrays, pieces, flops=1):
        shape = (arrays[0].shape[0] // pieces, VOX)
        kernel = functools.partial(add_kernel, len(arrays))
        return small_call(kernel, [shape] * pieces, "added", *arrays, flops=flops)

    sums = [box_sums(near[0], []), box_sums(near[1], [], flops=LARGE)]
    pairs, waits = [], [sums[1][0]]
    for kind in range(2):
        parts = box_sums(far[kind], sums[kind], *waits, flops=LARGE if kind else 1)
        waits = [parts[0]]
        parts = [parts[0]] + [swap(parts[i], i * plan.sz) for i in range(1, plan.sy)]
        for even, odd in (reduce_steps, reduce_steps[::-1]):
            keep, give = added(parts, 2)
            parts = [keep, swap(give, even, odd)]
        pairs.append(parts)
    (value,) = added(pairs[0], 1, flops=LARGE)
    (own,) = small_call(intensity_kernel, [(plan.share, VOX)], "intensity", value, *pairs[1])
    flip_x, flip_y, flip_z = plan.flip_dev
    near = [own, swap(own, flip_z, flip_x), swap(own, flip_x, flip_z)]
    near.append(swap(near[1], flip_x, flip_z))
    far = [swap(array, flip_y) for array in near]
    ordered = [near[0], near[1], far[0], far[1], near[2], near[3], far[2], far[3]]
    (result,) = small_call(functools.partial(unfold_kernel, plan), [(plan.boxes, VOX)], "unfold", *ordered)
    return result.reshape(GX // plan.sx, GY // plan.sy, GZ // plan.sz, BOX_BRICK, VOX)


def solution(mesh):
    return jax.shard_map(
        functools.partial(shards, Plan(mesh)),
        mesh=mesh,
        in_specs=(
            P(AXES, None, None, None),
            P(AXES, None, None, None),
            P(AXES, None, None, None),
            P(),
            P(),
            P(AXES),
            P(AXES, None),
            P(AXES),
        ),
        out_specs=P("bx", "by", "bz", None, None),
        check_vma=False,
    )
```

```python
import functools

import jax
import jax.numpy as jnp
from jax import lax
from jax.experimental import pallas as pl
from jax.experimental.pallas import tpu as pltpu
from jax.sharding import PartitionSpec as P

VOX = 256
LANES = 128
GX = 8
GY = 8
GZ = 4
BOX_BRICK = 64
FLIP_VOX = (0b11100000, 0b00011100, 0b00000011)
FLIP_BOX = (0b110000, 0b001100, 0b000011)
AXES = ("bx", "by", "bz")
POSITIONS = 8
TILE_LIMIT = 53 * 1024 * 1024
VMEM_LIMIT = 24 * 1024 * 1024
LARGE = 10**10
SWAPPED = (0, 4, 2, 6, 1, 5, 3, 7)
PIXEL_ROWS = 64


class Plan:
    def __init__(self, mesh):
        self.sx, self.sy, self.sz = (mesh.shape[name] for name in AXES)
        self.devices = self.sx * self.sy * self.sz
        lx, ly, lz = GX // self.sx, GY // self.sy, GZ // self.sz
        self.boxes = lx * ly * lz * BOX_BRICK
        self.share = self.boxes // 8
        self.flip_dev = ((self.sx - 1) * self.sy * self.sz, (self.sy - 1) * self.sz, self.sz - 1)
        self.half = (self.sx * self.sy * self.sz // 2, self.sy * self.sz // 2, self.sz // 2)
        self.flip_local = (
            (lx - 1) * ly * lz * BOX_BRICK + FLIP_BOX[0],
            (ly - 1) * lz * BOX_BRICK + FLIP_BOX[1],
            (lz - 1) * BOX_BRICK + FLIP_BOX[2],
        )

    def upper(self, device):
        return [(device & half) != 0 for half in self.half]

    def steps(self):
        row = self.sy * self.sz
        return (row, 1), (2 * row, 2)

    def box_row(self, place):
        (gather_a, gather_b), (first, second) = self.steps()
        has = lambda mask: (place & (mask * self.share)) != 0
        other_y = place // (self.sz * self.share) % self.sy
        odd = ((other_y ^ lax.axis_index("by")) & 1) != 0
        part = jnp.where(has(first), jnp.where(odd, 1, 2), 0) + jnp.where(has(second), jnp.where(odd, 2, 1), 0)
        row = (other_y * 4 + part) * self.share + place % self.share
        return jnp.where(has(gather_a) | has(gather_b), -1, row)

    def here(self):
        return (lax.axis_index("bx") * self.sy + lax.axis_index("by")) * self.sz + lax.axis_index("bz")


def masked(flags, masks):
    total = jnp.where(flags[0], masks[0], 0)
    for flag, mask in zip(flags[1:], masks[1:]):
        total = total ^ jnp.where(flag, mask, 0)
    return total


def lane_gather(values, index):
    return jnp.take_along_axis(values, index, axis=1, mode="promise_in_bounds")


def destination(plan, owner, box):
    upper = plan.upper(owner)
    local = box ^ masked(upper, plan.flip_local)
    part = local // plan.share
    row = local % plan.share
    holder = owner ^ masked(upper, plan.flip_dev)
    holder = holder ^ masked([(part & bit) != 0 for bit in (4, 2, 1)], plan.flip_dev)
    return holder * plan.share + row


def accumulate_kernel(counts, rows, cols, seen, value_out, weight_out, *scratch):
    arrays, sems, partial = scratch[:4], scratch[4], scratch[5]
    frames, positions = counts.shape[0], counts.shape[1]
    blocks = positions // POSITIONS

    def copies(block):
        span = pl.ds(block * POSITIONS, POSITIONS)
        views = [(ref.at[:, span], held.at[:, span]) for ref, held in zip((counts, rows, cols), arrays)]
        views.append((seen.at[span], arrays[3].at[span]))
        return [pltpu.make_async_copy(src, dst, sems.at[block, i]) for i, (src, dst) in enumerate(views)]

    for block in range(blocks):
        for copy in copies(block):
            copy.start()

    held_counts, held_rows, held_cols, held_seen = arrays

    @pl.loop(0, blocks)
    def _(block):
        for copy in copies(block):
            copy.wait()
        for p in range(POSITIONS):
            at = block * POSITIONS + p
            for f in range(frames):
                weights = held_cols[f, at]
                for kind in range(2):
                    total = None
                    for start in range(0, held_rows.shape[2], PIXEL_ROWS):
                        span = pl.ds(start, PIXEL_ROWS)
                        pixels = held_seen[at, span, :] if kind else held_counts[f, at, span, :]
                        item = jnp.dot(pixels, weights, preferred_element_type=jnp.float32)
                        item = held_rows[f, at, span, :].astype(jnp.float32) * item
                        item = jnp.sum(item.reshape(-1, 8, VOX), axis=0)
                        total = item if total is None else total + item
                    partial[f, kind, 0, p * 8 : (p + 1) * 8, :] = total[:, :LANES]
                    partial[f, kind, 1, p * 8 : (p + 1) * 8, :] = total[:, LANES:]
        for f in range(frames):
            place = pl.ds(pl.multiple_of(f * positions + block * POSITIONS, POSITIONS), POSITIONS)
            for kind, out in enumerate((value_out, weight_out)):
                for half in range(2):
                    lanes = pl.ds(half * LANES, LANES)
                    parts = [partial[f, kind, half, pl.ds(row, POSITIONS, stride=8), :] for row in range(8)]
                    out[place, lanes] = sum(parts)


def accumulate(counts, row_split, col_split, efficiency):
    frames, positions, pixels, _ = counts.shape
    tiles = frames * positions
    arrays = (counts, row_split, col_split, efficiency)
    return pl.pallas_call(
        accumulate_kernel,
        in_specs=[pl.BlockSpec(memory_space=pl.ANY)] * 4,
        out_specs=[pl.BlockSpec(memory_space=pltpu.VMEM)] * 2,
        out_shape=[jax.ShapeDtypeStruct((tiles, VOX), jnp.float32)] * 2,
        scratch_shapes=[pltpu.VMEM(array.shape, array.dtype) for array in arrays]
        + [
            pltpu.SemaphoreType.DMA((positions // POSITIONS, 4)),
            pltpu.VMEM((frames, 2, 2, 8 * POSITIONS, LANES), jnp.float32),
        ],
        compiler_params=pltpu.CompilerParams(vmem_limit_bytes=TILE_LIMIT),
        cost_estimate=pl.CostEstimate(
            flops=4 * tiles * pixels * pixels * VOX,
            bytes_accessed=sum(array.size * 2 for array in arrays),
            transcendentals=0,
        ),
        name="tile_sums",
    )(*arrays)


def payload_kernel(plan, angles, lorentz, owner, box, value, weight, value_out, weight_out):
    tiles = value.shape[0]
    frames = angles.shape[0]
    across = lax.broadcasted_iota(jnp.int32, (tiles, tiles), 1)
    down = lax.broadcasted_iota(jnp.int32, (tiles, tiles), 0)
    flips = masked(plan.upper(owner[...]), FLIP_VOX)
    flips = jnp.sum(jnp.where(across == down, flips, 0), axis=1, keepdims=True)
    ids = destination(plan, owner[...], box[...])
    for out in (value_out, weight_out):
        out[tiles : tiles + 8, :] = jnp.zeros((8, VOX), jnp.float32)
        out[tiles : tiles + 8, :tiles] = jnp.broadcast_to(ids.astype(jnp.float32), (8, tiles))
    lanes = lax.broadcasted_iota(jnp.int32, (8, LANES), 1)
    for start in range(0, tiles, 8):
        span = slice(start, start + 8)
        mask = jnp.broadcast_to(flips[span, :], (8, LANES))
        index = lanes ^ (mask & (LANES - 1))
        swap = (mask & LANES) != 0
        factor = lorentz[angles[start // (tiles // frames)]]
        for ref, out, scale in ((value, value_out, factor), (weight, weight_out, 1.0)):
            low, high = ref[span, :LANES], ref[span, LANES:]
            out[span, :LANES] = lane_gather(jnp.where(swap, high, low), index) * scale
            out[span, LANES:] = lane_gather(jnp.where(swap, low, high), index) * scale


def labelled(plan, angles, lorentz, owner, box, value, weight):
    shape = (value.shape[0] + 8, VOX)
    return pl.pallas_call(
        functools.partial(payload_kernel, plan),
        in_specs=[pl.BlockSpec(memory_space=pltpu.SMEM)] * 2 + [pl.BlockSpec(memory_space=pltpu.VMEM)] * 4,
        out_shape=[jax.ShapeDtypeStruct(shape, jnp.float32)] * 2,
        compiler_params=pltpu.CompilerParams(vmem_limit_bytes=VMEM_LIMIT),
        cost_estimate=pl.CostEstimate(flops=1, bytes_accessed=1, transcendentals=0),
        name="payload",
    )(angles, lorentz, owner, box, value, weight)


def scatter_kernel(plan, olds, outs, payload, *refs):
    before, after = refs[:olds], refs[len(refs) - outs :]
    tiles = LANES
    half = payload.shape[0] // 2
    ids = [payload[start + tiles : start + tiles + 1, :tiles] for start in (0, half)]
    ids = plan.box_row(jnp.concatenate(ids, axis=1).astype(jnp.int32) ^ (plan.here() * plan.share))
    values = jnp.concatenate([payload[:tiles, :], payload[half : half + tiles, :]], axis=0)
    high = values.astype(jnp.bfloat16)
    low = (values - high.astype(jnp.float32)).astype(jnp.bfloat16)
    for number, out in enumerate(after):
        boxes = lax.broadcasted_iota(jnp.int32, (out.shape[0], ids.shape[1]), 0) + number * out.shape[0]
        pick = (boxes == ids).astype(jnp.float32).astype(jnp.bfloat16)
        total = jnp.dot(pick, high, preferred_element_type=jnp.float32)
        total = total + jnp.dot(pick, low, preferred_element_type=jnp.float32)
        out[...] = total + before[number][...] if olds else total


def join_kernel(first, second, *rest):
    half, out = first.shape[0], rest[-1]
    out[:half, :] = first[...]
    out[half:, :] = second[...]


def add_kernel(count, *refs):
    inputs, outs = refs[:count], refs[count:]
    start = 0
    for out in outs:
        span = slice(start, start + out.shape[0])
        total = inputs[0][span, :]
        for ref in inputs[1:]:
            total = total + ref[span, :]
        out[...] = total
        start += out.shape[0]


def intensity_kernel(value, *refs):
    inputs, out = refs[:-1], refs[-1]
    weight = inputs[0][...]
    for ref in inputs[1:]:
        weight = weight + ref[...]
    out[...] = value[...] * 0.125 / jnp.maximum(weight * 0.125, 1.0)


def unfold_kernel(plan, *refs):
    inputs, out = refs[:-1], refs[-1]
    upper = plan.upper(plan.here())
    own = masked(upper, (4, 2, 1))
    local = masked(upper, plan.flip_local)
    mask = masked(upper, FLIP_VOX)
    index = lax.broadcasted_iota(jnp.int32, (8, LANES), 1) ^ (mask & (LANES - 1))
    turn = lax.broadcasted_iota(jnp.int32, (8, LANES), 0) ^ (local & 7)
    swap = (mask & LANES) != 0
    odd = (lax.axis_index("by") & 1) != 0
    for number, ref in enumerate(inputs):
        codes = (number, SWAPPED[number])
        far = (number & 2) != 0
        relative = jnp.where(odd, codes[1 - far], codes[far])
        base = (relative ^ own) * plan.share
        for group in range(0, plan.share, 8):
            rows = ref[group : group + 8, :]
            low, high = rows[:, :LANES], rows[:, LANES:]
            target = (base + group) ^ (local & ~7)
            place = pl.ds(pl.multiple_of(target, 8), 8)
            for at, item in enumerate((jnp.where(swap, high, low), jnp.where(swap, low, high))):
                item = jnp.take_along_axis(item, turn, axis=0, mode="promise_in_bounds")
                out[place, at * LANES : (at + 1) * LANES] = lane_gather(item, index)


def small_call(kernel, shapes, name, *arrays, flops=1):
    return pl.pallas_call(
        kernel,
        out_shape=[jax.ShapeDtypeStruct(shape, jnp.float32) for shape in shapes],
        compiler_params=pltpu.CompilerParams(vmem_limit_bytes=VMEM_LIMIT),
        cost_estimate=pl.CostEstimate(flops=flops, bytes_accessed=1, transcendentals=0),
        name=name,
    )(*arrays)


def shards(plan, counts, row_split, col_split, efficiency, lorentz, angles, tile_owner, tile_box):
    def swap(array, even, odd=None):
        odd = even if odd is None else odd
        pairs = [(i, i ^ (odd if i // plan.sz % 2 else even)) for i in range(plan.devices)]
        return lax.ppermute(array, AXES, pairs)

    def join(first, second, *order):
        rows, width = first.shape
        return small_call(join_kernel, [(2 * rows, width)], "join", first, second, *order)[0]

    gather_steps, reduce_steps = plan.steps()
    owner = tile_owner.reshape(1, -1)
    box = tile_box.reshape(1, -1)
    own = accumulate(counts, row_split, col_split, efficiency)
    own = labelled(plan, angles, lorentz, owner, box, *own)
    arrived = [swap(array, *gather_steps) for array in own]
    near = [join(own[0], arrived[0])]
    near.append(join(own[1], arrived[1], near[0]))
    far = [swap(array, *gather_steps[::-1]) for array in near]
    def box_sums(payload, olds, *waits, flops=1):
        kernel = functools.partial(scatter_kernel, plan, len(olds), plan.sy)
        shapes = [(4 * plan.share, VOX)] * plan.sy
        return small_call(kernel, shapes, "box_sums", payload, *olds, *waits, flops=flops)

    def added(arrays, pieces, flops=1):
        shape = (arrays[0].shape[0] // pieces, VOX)
        kernel = functools.partial(add_kernel, len(arrays))
        return small_call(kernel, [shape] * pieces, "added", *arrays, flops=flops)

    sums = [box_sums(near[0], []), box_sums(near[1], [], flops=LARGE)]
    pairs, waits = [], [sums[1][0]]
    for kind in range(2):
        parts = box_sums(far[kind], sums[kind], *waits, flops=LARGE if kind else 1)
        waits = [parts[0]]
        parts = [parts[0]] + [swap(parts[i], i * plan.sz) for i in range(1, plan.sy)]
        for even, odd in (reduce_steps, reduce_steps[::-1]):
            keep, give = added(parts, 2)
            parts = [keep, swap(give, even, odd)]
        pairs.append(parts)
    (value,) = added(pairs[0], 1, flops=LARGE)
    (own,) = small_call(intensity_kernel, [(plan.share, VOX)], "intensity", value, *pairs[1])
    flip_x, flip_y, flip_z = plan.flip_dev
    near = [own, swap(own, flip_z, flip_x), swap(own, flip_x, flip_z)]
    near.append(swap(near[1], flip_x, flip_z))
    far = [swap(array, flip_y) for array in near]
    ordered = [near[0], near[1], far[0], far[1], near[2], near[3], far[2], far[3]]
    (result,) = small_call(functools.partial(unfold_kernel, plan), [(plan.boxes, VOX)], "unfold", *ordered)
    return result.reshape(GX // plan.sx, GY // plan.sy, GZ // plan.sz, BOX_BRICK, VOX)


def solution(mesh):
    return jax.shard_map(
        functools.partial(shards, Plan(mesh)),
        mesh=mesh,
        in_specs=(
            P(AXES, None, None, None),
            P(AXES, None, None, None),
            P(AXES, None, None, None),
            P(),
            P(),
            P(AXES),
            P(AXES, None),
            P(AXES),
        ),
        out_specs=P("bx", "by", "bz", None, None),
        check_vma=False,
    )
```

```python
import functools

import jax
import jax.numpy as jnp
from jax import lax
from jax.experimental import pallas as pl
from jax.experimental.pallas import tpu as pltpu
from jax.sharding import PartitionSpec as P

VOX = 256
LANES = 128
GX = 8
GY = 8
GZ = 4
BOX_BRICK = 64
FLIP_VOX = (0b11100000, 0b00011100, 0b00000011)
FLIP_BOX = (0b110000, 0b001100, 0b000011)
AXES = ("bx", "by", "bz")
POSITIONS = 8
TILE_LIMIT = 53 * 1024 * 1024
VMEM_LIMIT = 24 * 1024 * 1024
LARGE = 10**10
SWAPPED = (0, 4, 2, 6, 1, 5, 3, 7)
PIXEL_ROWS = 64


class Plan:
    def __init__(self, mesh):
        self.sx, self.sy, self.sz = (mesh.shape[name] for name in AXES)
        self.devices = self.sx * self.sy * self.sz
        lx, ly, lz = GX // self.sx, GY // self.sy, GZ // self.sz
        self.boxes = lx * ly * lz * BOX_BRICK
        self.share = self.boxes // 8
        self.flip_dev = ((self.sx - 1) * self.sy * self.sz, (self.sy - 1) * self.sz, self.sz - 1)
        self.half = (self.sx * self.sy * self.sz // 2, self.sy * self.sz // 2, self.sz // 2)
        self.flip_local = (
            (lx - 1) * ly * lz * BOX_BRICK + FLIP_BOX[0],
            (ly - 1) * lz * BOX_BRICK + FLIP_BOX[1],
            (lz - 1) * BOX_BRICK + FLIP_BOX[2],
        )

    def upper(self, device):
        return [(device & half) != 0 for half in self.half]

    def steps(self):
        row = self.sy * self.sz
        return (row, 1), (2 * row, 2)

    def box_row(self, place):
        (gather_a, gather_b), (first, second) = self.steps()
        has = lambda mask: (place & (mask * self.share)) != 0
        other_y = place // (self.sz * self.share) % self.sy
        odd = ((other_y ^ lax.axis_index("by")) & 1) != 0
        part = jnp.where(has(first), jnp.where(odd, 1, 2), 0) + jnp.where(has(second), jnp.where(odd, 2, 1), 0)
        row = (other_y * 4 + part) * self.share + place % self.share
        return jnp.where(has(gather_a) | has(gather_b), -1, row)

    def here(self):
        return (lax.axis_index("bx") * self.sy + lax.axis_index("by")) * self.sz + lax.axis_index("bz")


def masked(flags, masks):
    total = jnp.where(flags[0], masks[0], 0)
    for flag, mask in zip(flags[1:], masks[1:]):
        total = total ^ jnp.where(flag, mask, 0)
    return total


def lane_gather(values, index):
    return jnp.take_along_axis(values, index, axis=1, mode="promise_in_bounds")


def destination(plan, owner, box):
    upper = plan.upper(owner)
    local = box ^ masked(upper, plan.flip_local)
    part = local // plan.share
    row = local % plan.share
    holder = owner ^ masked(upper, plan.flip_dev)
    holder = holder ^ masked([(part & bit) != 0 for bit in (4, 2, 1)], plan.flip_dev)
    return holder * plan.share + row


def accumulate_kernel(counts, rows, cols, seen, value_out, weight_out, *scratch):
    arrays, sems, partial = scratch[:4], scratch[4], scratch[5]
    frames, positions = counts.shape[0], counts.shape[1]
    blocks = positions // POSITIONS

    def copies(block):
        span = pl.ds(block * POSITIONS, POSITIONS)
        views = [(ref.at[:, span], held.at[:, span]) for ref, held in zip((counts, rows, cols), arrays)]
        views.append((seen.at[span], arrays[3].at[span]))
        return [pltpu.make_async_copy(src, dst, sems.at[block, i]) for i, (src, dst) in enumerate(views)]

    for block in range(blocks):
        for copy in copies(block):
            copy.start()

    held_counts, held_rows, held_cols, held_seen = arrays

    @pl.loop(0, blocks)
    def _(block):
        for copy in copies(block):
            copy.wait()
        for p in range(POSITIONS):
            at = block * POSITIONS + p
            for f in range(frames):
                weights = held_cols[f, at]
                for kind in range(2):
                    total = None
                    for start in range(0, held_rows.shape[2], PIXEL_ROWS):
                        span = pl.ds(start, PIXEL_ROWS)
                        pixels = held_seen[at, span, :] if kind else held_counts[f, at, span, :]
                        item = jnp.dot(pixels, weights, preferred_element_type=jnp.float32)
                        item = held_rows[f, at, span, :].astype(jnp.float32) * item
                        item = jnp.sum(item.reshape(-1, 8, VOX), axis=0)
                        total = item if total is None else total + item
                    partial[f, kind, 0, p * 8 : (p + 1) * 8, :] = total[:, :LANES]
                    partial[f, kind, 1, p * 8 : (p + 1) * 8, :] = total[:, LANES:]
        for f in range(frames):
            place = pl.ds(pl.multiple_of(f * positions + block * POSITIONS, POSITIONS), POSITIONS)
            for kind, out in enumerate((value_out, weight_out)):
                for half in range(2):
                    lanes = pl.ds(half * LANES, LANES)
                    parts = [partial[f, kind, half, pl.ds(row, POSITIONS, stride=8), :] for row in range(8)]
                    out[place, lanes] = sum(parts)


def accumulate(counts, row_split, col_split, efficiency):
    frames, positions, pixels, _ = counts.shape
    tiles = frames * positions
    arrays = (counts, row_split, col_split, efficiency)
    return pl.pallas_call(
        accumulate_kernel,
        in_specs=[pl.BlockSpec(memory_space=pl.ANY)] * 4,
        out_specs=[pl.BlockSpec(memory_space=pltpu.VMEM)] * 2,
        out_shape=[jax.ShapeDtypeStruct((tiles, VOX), jnp.float32)] * 2,
        scratch_shapes=[pltpu.VMEM(array.shape, array.dtype) for array in arrays]
        + [
            pltpu.SemaphoreType.DMA((positions // POSITIONS, 4)),
            pltpu.VMEM((frames, 2, 2, 8 * POSITIONS, LANES), jnp.float32),
        ],
        compiler_params=pltpu.CompilerParams(vmem_limit_bytes=TILE_LIMIT),
        cost_estimate=pl.CostEstimate(
            flops=4 * tiles * pixels * pixels * VOX,
            bytes_accessed=sum(array.size * 2 for array in arrays),
            transcendentals=0,
        ),
        name="tile_sums",
    )(*arrays)


def payload_kernel(plan, angles, lorentz, owner, box, value, weight, value_out, weight_out):
    tiles = value.shape[0]
    frames = angles.shape[1]
    table = lorentz[...].reshape(1, -1)
    entry = lax.broadcasted_iota(jnp.int32, table.shape, 1)
    factors = [
        jnp.sum(jnp.where(entry == angles[:, f : f + 1], table, 0.0), axis=1, keepdims=True) for f in range(frames)
    ]
    across = lax.broadcasted_iota(jnp.int32, (tiles, tiles), 1)
    down = lax.broadcasted_iota(jnp.int32, (tiles, tiles), 0)
    flips = masked(plan.upper(owner[...]), FLIP_VOX)
    flips = jnp.sum(jnp.where(across == down, flips, 0), axis=1, keepdims=True)
    ids = destination(plan, owner[...], box[...])
    for out in (value_out, weight_out):
        out[tiles : tiles + 8, :] = jnp.zeros((8, VOX), jnp.float32)
        out[tiles : tiles + 8, :tiles] = jnp.broadcast_to(ids.astype(jnp.float32), (8, tiles))
    lanes = lax.broadcasted_iota(jnp.int32, (8, LANES), 1)
    for start in range(0, tiles, 8):
        span = slice(start, start + 8)
        mask = jnp.broadcast_to(flips[span, :], (8, LANES))
        index = lanes ^ (mask & (LANES - 1))
        swap = (mask & LANES) != 0
        factor = factors[start // (tiles // frames)]
        for ref, out, scale in ((value, value_out, factor), (weight, weight_out, 1.0)):
            low, high = ref[span, :LANES], ref[span, LANES:]
            out[span, :LANES] = lane_gather(jnp.where(swap, high, low), index) * scale
            out[span, LANES:] = lane_gather(jnp.where(swap, low, high), index) * scale


def labelled(plan, angles, lorentz, owner, box, value, weight):
    shape = (value.shape[0] + 8, VOX)
    return pl.pallas_call(
        functools.partial(payload_kernel, plan),
        out_shape=[jax.ShapeDtypeStruct(shape, jnp.float32)] * 2,
        compiler_params=pltpu.CompilerParams(vmem_limit_bytes=VMEM_LIMIT),
        cost_estimate=pl.CostEstimate(flops=1, bytes_accessed=1, transcendentals=0),
        name="payload",
    )(angles.reshape(1, -1), lorentz, owner, box, value, weight)


def scatter_kernel(plan, olds, outs, payload, *refs):
    before, after = refs[:olds], refs[len(refs) - outs :]
    tiles = LANES
    half = payload.shape[0] // 2
    ids = [payload[start + tiles : start + tiles + 1, :tiles] for start in (0, half)]
    ids = plan.box_row(jnp.concatenate(ids, axis=1).astype(jnp.int32) ^ (plan.here() * plan.share))
    values = jnp.concatenate([payload[:tiles, :], payload[half : half + tiles, :]], axis=0)
    high = values.astype(jnp.bfloat16)
    low = (values - high.astype(jnp.float32)).astype(jnp.bfloat16)
    for number, out in enumerate(after):
        boxes = lax.broadcasted_iota(jnp.int32, (out.shape[0], ids.shape[1]), 0) + number * out.shape[0]
        pick = (boxes == ids).astype(jnp.float32).astype(jnp.bfloat16)
        total = jnp.dot(pick, high, preferred_element_type=jnp.float32)
        total = total + jnp.dot(pick, low, preferred_element_type=jnp.float32)
        out[...] = total + before[number][...] if olds else total


def join_kernel(first, second, *rest):
    half, out = first.shape[0], rest[-1]
    out[:half, :] = first[...]
    out[half:, :] = second[...]


def add_kernel(count, *refs):
    inputs, outs = refs[:count], refs[count:]
    start = 0
    for out in outs:
        span = slice(start, start + out.shape[0])
        total = inputs[0][span, :]
        for ref in inputs[1:]:
            total = total + ref[span, :]
        out[...] = total
        start += out.shape[0]


def intensity_kernel(value, *refs):
    inputs, out = refs[:-1], refs[-1]
    weight = inputs[0][...]
    for ref in inputs[1:]:
        weight = weight + ref[...]
    out[...] = value[...] * 0.125 / jnp.maximum(weight * 0.125, 1.0)


def unfold_kernel(plan, *refs):
    inputs, out = refs[:-1], refs[-1]
    upper = plan.upper(plan.here())
    own = masked(upper, (4, 2, 1))
    local = masked(upper, plan.flip_local)
    mask = masked(upper, FLIP_VOX)
    index = lax.broadcasted_iota(jnp.int32, (8, LANES), 1) ^ (mask & (LANES - 1))
    turn = lax.broadcasted_iota(jnp.int32, (8, LANES), 0) ^ (local & 7)
    swap = (mask & LANES) != 0
    odd = (lax.axis_index("by") & 1) != 0
    for number, ref in enumerate(inputs):
        codes = (number, SWAPPED[number])
        far = (number & 2) != 0
        relative = jnp.where(odd, codes[1 - far], codes[far])
        base = (relative ^ own) * plan.share
        for group in range(0, plan.share, 8):
            rows = ref[group : group + 8, :]
            low, high = rows[:, :LANES], rows[:, LANES:]
            target = (base + group) ^ (local & ~7)
            place = pl.ds(pl.multiple_of(target, 8), 8)
            for at, item in enumerate((jnp.where(swap, high, low), jnp.where(swap, low, high))):
                item = jnp.take_along_axis(item, turn, axis=0, mode="promise_in_bounds")
                out[place, at * LANES : (at + 1) * LANES] = lane_gather(item, index)


def small_call(kernel, shapes, name, *arrays, flops=1):
    return pl.pallas_call(
        kernel,
        out_shape=[jax.ShapeDtypeStruct(shape, jnp.float32) for shape in shapes],
        compiler_params=pltpu.CompilerParams(vmem_limit_bytes=VMEM_LIMIT),
        cost_estimate=pl.CostEstimate(flops=flops, bytes_accessed=1, transcendentals=0),
        name=name,
    )(*arrays)


def shards(plan, counts, row_split, col_split, efficiency, lorentz, angles, tile_owner, tile_box):
    def swap(array, even, odd=None):
        odd = even if odd is None else odd
        pairs = [(i, i ^ (odd if i // plan.sz % 2 else even)) for i in range(plan.devices)]
        return lax.ppermute(array, AXES, pairs)

    def join(first, second, *order):
        rows, width = first.shape
        return small_call(join_kernel, [(2 * rows, width)], "join", first, second, *order)[0]

    gather_steps, reduce_steps = plan.steps()
    owner = tile_owner.reshape(1, -1)
    box = tile_box.reshape(1, -1)
    own = accumulate(counts, row_split, col_split, efficiency)
    own = labelled(plan, angles, lorentz, owner, box, *own)
    arrived = [swap(array, *gather_steps) for array in own]
    near = [join(own[0], arrived[0])]
    near.append(join(own[1], arrived[1], near[0]))
    far = [swap(array, *gather_steps[::-1]) for array in near]
    def box_sums(payload, olds, *waits, flops=1):
        kernel = functools.partial(scatter_kernel, plan, len(olds), plan.sy)
        shapes = [(4 * plan.share, VOX)] * plan.sy
        return small_call(kernel, shapes, "box_sums", payload, *olds, *waits, flops=flops)

    def added(arrays, pieces, flops=1):
        shape = (arrays[0].shape[0] // pieces, VOX)
        kernel = functools.partial(add_kernel, len(arrays))
        return small_call(kernel, [shape] * pieces, "added", *arrays, flops=flops)

    sums = [box_sums(near[0], []), box_sums(near[1], [], flops=LARGE)]
    pairs, waits = [], [sums[1][0]]
    for kind in range(2):
        parts = box_sums(far[kind], sums[kind], *waits, flops=LARGE if kind else 1)
        waits = [parts[0]]
        parts = [parts[0]] + [swap(parts[i], i * plan.sz) for i in range(1, plan.sy)]
        for even, odd in (reduce_steps, reduce_steps[::-1]):
            keep, give = added(parts, 2)
            parts = [keep, swap(give, even, odd)]
        pairs.append(parts)
    (value,) = added(pairs[0], 1, flops=LARGE)
    (own,) = small_call(intensity_kernel, [(plan.share, VOX)], "intensity", value, *pairs[1])
    flip_x, flip_y, flip_z = plan.flip_dev
    near = [own, swap(own, flip_z, flip_x), swap(own, flip_x, flip_z)]
    near.append(swap(near[1], flip_x, flip_z))
    far = [swap(array, flip_y) for array in near]
    ordered = [near[0], near[1], far[0], far[1], near[2], near[3], far[2], far[3]]
    (result,) = small_call(functools.partial(unfold_kernel, plan), [(plan.boxes, VOX)], "unfold", *ordered)
    return result.reshape(GX // plan.sx, GY // plan.sy, GZ // plan.sz, BOX_BRICK, VOX)


def solution(mesh):
    return jax.shard_map(
        functools.partial(shards, Plan(mesh)),
        mesh=mesh,
        in_specs=(
            P(AXES, None, None, None),
            P(AXES, None, None, None),
            P(AXES, None, None, None),
            P(),
            P(),
            P(AXES),
            P(AXES, None),
            P(AXES),
        ),
        out_specs=P("bx", "by", "bz", None, None),
        check_vma=False,
    )
```

```python
import functools

import jax
import jax.numpy as jnp
from jax import lax
from jax.experimental import pallas as pl
from jax.experimental.pallas import tpu as pltpu
from jax.sharding import PartitionSpec as P

VOX = 256
LANES = 128
GX = 8
GY = 8
GZ = 4
BOX_BRICK = 64
FLIP_VOX = (0b11100000, 0b00011100, 0b00000011)
FLIP_BOX = (0b110000, 0b001100, 0b000011)
AXES = ("bx", "by", "bz")
POSITIONS = 8
LAST_PARTS = (4, 2, 2)
TILE_LIMIT = 53 * 1024 * 1024
VMEM_LIMIT = 24 * 1024 * 1024
LARGE = 10**10
SWAPPED = (0, 4, 2, 6, 1, 5, 3, 7)
PIXEL_ROWS = 64


class Plan:
    def __init__(self, mesh):
        self.sx, self.sy, self.sz = (mesh.shape[name] for name in AXES)
        self.devices = self.sx * self.sy * self.sz
        lx, ly, lz = GX // self.sx, GY // self.sy, GZ // self.sz
        self.boxes = lx * ly * lz * BOX_BRICK
        self.share = self.boxes // 8
        self.flip_dev = ((self.sx - 1) * self.sy * self.sz, (self.sy - 1) * self.sz, self.sz - 1)
        self.half = (self.sx * self.sy * self.sz // 2, self.sy * self.sz // 2, self.sz // 2)
        self.flip_local = (
            (lx - 1) * ly * lz * BOX_BRICK + FLIP_BOX[0],
            (ly - 1) * lz * BOX_BRICK + FLIP_BOX[1],
            (lz - 1) * BOX_BRICK + FLIP_BOX[2],
        )

    def upper(self, device):
        return [(device & half) != 0 for half in self.half]

    def steps(self):
        row = self.sy * self.sz
        return (row, 1), (2 * row, 2)

    def box_row(self, place):
        (gather_a, gather_b), (first, second) = self.steps()
        has = lambda mask: (place & (mask * self.share)) != 0
        other_y = place // (self.sz * self.share) % self.sy
        odd = ((other_y ^ lax.axis_index("by")) & 1) != 0
        part = jnp.where(has(first), jnp.where(odd, 1, 2), 0) + jnp.where(has(second), jnp.where(odd, 2, 1), 0)
        row = (other_y * 4 + part) * self.share + place % self.share
        return jnp.where(has(gather_a) | has(gather_b), -1, row)

    def here(self):
        return (lax.axis_index("bx") * self.sy + lax.axis_index("by")) * self.sz + lax.axis_index("bz")


def masked(flags, masks):
    total = jnp.where(flags[0], masks[0], 0)
    for flag, mask in zip(flags[1:], masks[1:]):
        total = total ^ jnp.where(flag, mask, 0)
    return total


def lane_gather(values, index):
    return jnp.take_along_axis(values, index, axis=1, mode="promise_in_bounds")


def destination(plan, owner, box):
    upper = plan.upper(owner)
    local = box ^ masked(upper, plan.flip_local)
    part = local // plan.share
    row = local % plan.share
    holder = owner ^ masked(upper, plan.flip_dev)
    holder = holder ^ masked([(part & bit) != 0 for bit in (4, 2, 1)], plan.flip_dev)
    return holder * plan.share + row


def accumulate_kernel(counts, rows, cols, seen, value_out, weight_out, *scratch):
    arrays, sems, partial = scratch[:4], scratch[4], scratch[5]
    frames, positions = counts.shape[0], counts.shape[1]
    blocks = positions // POSITIONS

    def copies(start, count, slot):
        span = pl.ds(start, count)
        views = [(ref.at[:, span], held.at[:, span]) for ref, held in zip((counts, rows, cols), arrays)]
        views.append((seen.at[span], arrays[3].at[span]))
        return [pltpu.make_async_copy(src, dst, sems.at[slot, i]) for i, (src, dst) in enumerate(views)]

    last, start = {}, positions - POSITIONS
    for slot, count in enumerate(LAST_PARTS, blocks - 1):
        last[start + POSITIONS - positions] = (start, count, slot)
        start += count
    for landing in [(block * POSITIONS, POSITIONS, block) for block in range(blocks - 1)] + list(last.values()):
        for copy in copies(*landing):
            copy.start()

    held_counts, held_rows, held_cols, held_seen = arrays

    def compute(block, landings):
        for p in range(POSITIONS):
            if p in landings:
                for copy in copies(*landings[p]):
                    copy.wait()
            at = block * POSITIONS + p
            for f in range(frames):
                weights = held_cols[f, at]
                for kind in range(2):
                    total = None
                    for start in range(0, held_rows.shape[2], PIXEL_ROWS):
                        span = pl.ds(start, PIXEL_ROWS)
                        pixels = held_seen[at, span, :] if kind else held_counts[f, at, span, :]
                        item = jnp.dot(pixels, weights, preferred_element_type=jnp.float32)
                        item = held_rows[f, at, span, :].astype(jnp.float32) * item
                        item = jnp.sum(item.reshape(-1, 8, VOX), axis=0)
                        total = item if total is None else total + item
                    partial[f, kind, 0, p * 8 : (p + 1) * 8, :] = total[:, :LANES]
                    partial[f, kind, 1, p * 8 : (p + 1) * 8, :] = total[:, LANES:]
        for f in range(frames):
            place = pl.ds(pl.multiple_of(f * positions + block * POSITIONS, POSITIONS), POSITIONS)
            for kind, out in enumerate((value_out, weight_out)):
                for half in range(2):
                    lanes = pl.ds(half * LANES, LANES)
                    parts = [partial[f, kind, half, pl.ds(row, POSITIONS, stride=8), :] for row in range(8)]
                    out[place, lanes] = sum(parts)

    @pl.loop(0, blocks - 1)
    def _(block):
        compute(block, {0: (block * POSITIONS, POSITIONS, block)})

    compute(blocks - 1, last)


def accumulate(counts, row_split, col_split, efficiency):
    frames, positions, pixels, _ = counts.shape
    tiles = frames * positions
    arrays = (counts, row_split, col_split, efficiency)
    return pl.pallas_call(
        accumulate_kernel,
        in_specs=[pl.BlockSpec(memory_space=pl.ANY)] * 4,
        out_specs=[pl.BlockSpec(memory_space=pltpu.VMEM)] * 2,
        out_shape=[jax.ShapeDtypeStruct((tiles, VOX), jnp.float32)] * 2,
        scratch_shapes=[pltpu.VMEM(array.shape, array.dtype) for array in arrays]
        + [
            pltpu.SemaphoreType.DMA((positions // POSITIONS - 1 + len(LAST_PARTS), 4)),
            pltpu.VMEM((frames, 2, 2, 8 * POSITIONS, LANES), jnp.float32),
        ],
        compiler_params=pltpu.CompilerParams(vmem_limit_bytes=TILE_LIMIT),
        cost_estimate=pl.CostEstimate(
            flops=4 * tiles * pixels * pixels * VOX,
            bytes_accessed=sum(array.size * 2 for array in arrays),
            transcendentals=0,
        ),
        name="tile_sums",
    )(*arrays)


def payload_kernel(plan, angles, lorentz, owner, box, value, weight, value_out, weight_out):
    tiles = value.shape[0]
    frames = angles.shape[1]
    table = lorentz[...].reshape(1, -1)
    entry = lax.broadcasted_iota(jnp.int32, table.shape, 1)
    factors = [
        jnp.sum(jnp.where(entry == angles[:, f : f + 1], table, 0.0), axis=1, keepdims=True) for f in range(frames)
    ]
    across = lax.broadcasted_iota(jnp.int32, (tiles, tiles), 1)
    down = lax.broadcasted_iota(jnp.int32, (tiles, tiles), 0)
    flips = masked(plan.upper(owner[...]), FLIP_VOX)
    flips = jnp.sum(jnp.where(across == down, flips, 0), axis=1, keepdims=True)
    ids = destination(plan, owner[...], box[...])
    for out in (value_out, weight_out):
        out[tiles : tiles + 8, :] = jnp.zeros((8, VOX), jnp.float32)
        out[tiles : tiles + 8, :tiles] = jnp.broadcast_to(ids.astype(jnp.float32), (8, tiles))
    lanes = lax.broadcasted_iota(jnp.int32, (8, LANES), 1)
    for start in range(0, tiles, 8):
        span = slice(start, start + 8)
        mask = jnp.broadcast_to(flips[span, :], (8, LANES))
        index = lanes ^ (mask & (LANES - 1))
        swap = (mask & LANES) != 0
        factor = factors[start // (tiles // frames)]
        for ref, out, scale in ((value, value_out, factor), (weight, weight_out, 1.0)):
            low, high = ref[span, :LANES], ref[span, LANES:]
            out[span, :LANES] = lane_gather(jnp.where(swap, high, low), index) * scale
            out[span, LANES:] = lane_gather(jnp.where(swap, low, high), index) * scale


def labelled(plan, angles, lorentz, owner, box, value, weight):
    shape = (value.shape[0] + 8, VOX)
    return pl.pallas_call(
        functools.partial(payload_kernel, plan),
        out_shape=[jax.ShapeDtypeStruct(shape, jnp.float32)] * 2,
        compiler_params=pltpu.CompilerParams(vmem_limit_bytes=VMEM_LIMIT),
        cost_estimate=pl.CostEstimate(flops=1, bytes_accessed=1, transcendentals=0),
        name="payload",
    )(angles.reshape(1, -1), lorentz, owner, box, value, weight)


def scatter_kernel(plan, olds, outs, payload, *refs):
    before, after = refs[:olds], refs[len(refs) - outs :]
    tiles = LANES
    half = payload.shape[0] // 2
    ids = [payload[start + tiles : start + tiles + 1, :tiles] for start in (0, half)]
    ids = plan.box_row(jnp.concatenate(ids, axis=1).astype(jnp.int32) ^ (plan.here() * plan.share))
    values = jnp.concatenate([payload[:tiles, :], payload[half : half + tiles, :]], axis=0)
    high = values.astype(jnp.bfloat16)
    low = (values - high.astype(jnp.float32)).astype(jnp.bfloat16)
    for number, out in enumerate(after):
        boxes = lax.broadcasted_iota(jnp.int32, (out.shape[0], ids.shape[1]), 0) + number * out.shape[0]
        pick = (boxes == ids).astype(jnp.float32).astype(jnp.bfloat16)
        total = jnp.dot(pick, high, preferred_element_type=jnp.float32)
        total = total + jnp.dot(pick, low, preferred_element_type=jnp.float32)
        out[...] = total + before[number][...] if olds else total


def join_kernel(first, second, *rest):
    half, out = first.shape[0], rest[-1]
    out[:half, :] = first[...]
    out[half:, :] = second[...]


def add_kernel(count, *refs):
    inputs, outs = refs[:count], refs[count:]
    start = 0
    for out in outs:
        span = slice(start, start + out.shape[0])
        total = inputs[0][span, :]
        for ref in inputs[1:]:
            total = total + ref[span, :]
        out[...] = total
        start += out.shape[0]


def intensity_kernel(value, *refs):
    inputs, out = refs[:-1], refs[-1]
    weight = inputs[0][...]
    for ref in inputs[1:]:
        weight = weight + ref[...]
    out[...] = value[...] * 0.125 / jnp.maximum(weight * 0.125, 1.0)


def unfold_kernel(plan, *refs):
    inputs, out = refs[:-1], refs[-1]
    upper = plan.upper(plan.here())
    own = masked(upper, (4, 2, 1))
    local = masked(upper, plan.flip_local)
    mask = masked(upper, FLIP_VOX)
    index = lax.broadcasted_iota(jnp.int32, (8, LANES), 1) ^ (mask & (LANES - 1))
    turn = lax.broadcasted_iota(jnp.int32, (8, LANES), 0) ^ (local & 7)
    swap = (mask & LANES) != 0
    odd = (lax.axis_index("by") & 1) != 0
    for number, ref in enumerate(inputs):
        codes = (number, SWAPPED[number])
        far = (number & 2) != 0
        relative = jnp.where(odd, codes[1 - far], codes[far])
        base = (relative ^ own) * plan.share
        for group in range(0, plan.share, 8):
            rows = ref[group : group + 8, :]
            low, high = rows[:, :LANES], rows[:, LANES:]
            target = (base + group) ^ (local & ~7)
            place = pl.ds(pl.multiple_of(target, 8), 8)
            for at, item in enumerate((jnp.where(swap, high, low), jnp.where(swap, low, high))):
                item = jnp.take_along_axis(item, turn, axis=0, mode="promise_in_bounds")
                out[place, at * LANES : (at + 1) * LANES] = lane_gather(item, index)


def small_call(kernel, shapes, name, *arrays, flops=1):
    return pl.pallas_call(
        kernel,
        out_shape=[jax.ShapeDtypeStruct(shape, jnp.float32) for shape in shapes],
        compiler_params=pltpu.CompilerParams(vmem_limit_bytes=VMEM_LIMIT),
        cost_estimate=pl.CostEstimate(flops=flops, bytes_accessed=1, transcendentals=0),
        name=name,
    )(*arrays)


def shards(plan, counts, row_split, col_split, efficiency, lorentz, angles, tile_owner, tile_box):
    def swap(array, even, odd=None):
        odd = even if odd is None else odd
        pairs = [(i, i ^ (odd if i // plan.sz % 2 else even)) for i in range(plan.devices)]
        return lax.ppermute(array, AXES, pairs)

    def join(first, second, *order):
        rows, width = first.shape
        return small_call(join_kernel, [(2 * rows, width)], "join", first, second, *order)[0]

    gather_steps, reduce_steps = plan.steps()
    owner = tile_owner.reshape(1, -1)
    box = tile_box.reshape(1, -1)
    own = accumulate(counts, row_split, col_split, efficiency)
    own = labelled(plan, angles, lorentz, owner, box, *own)
    arrived = [swap(array, *gather_steps) for array in own]
    near = [join(own[0], arrived[0])]
    near.append(join(own[1], arrived[1], near[0]))
    far = [swap(array, *gather_steps[::-1]) for array in near]
    def box_sums(payload, olds, *waits, flops=1):
        kernel = functools.partial(scatter_kernel, plan, len(olds), plan.sy)
        shapes = [(4 * plan.share, VOX)] * plan.sy
        return small_call(kernel, shapes, "box_sums", payload, *olds, *waits, flops=flops)

    def added(arrays, pieces, flops=1):
        shape = (arrays[0].shape[0] // pieces, VOX)
        kernel = functools.partial(add_kernel, len(arrays))
        return small_call(kernel, [shape] * pieces, "added", *arrays, flops=flops)

    sums = [box_sums(near[0], []), box_sums(near[1], [], flops=LARGE)]
    pairs, waits = [], [sums[1][0]]
    for kind in range(2):
        parts = box_sums(far[kind], sums[kind], *waits, flops=LARGE if kind else 1)
        waits = [parts[0]]
        parts = [parts[0]] + [swap(parts[i], i * plan.sz) for i in range(1, plan.sy)]
        for even, odd in (reduce_steps, reduce_steps[::-1]):
            keep, give = added(parts, 2)
            parts = [keep, swap(give, even, odd)]
        pairs.append(parts)
    (value,) = added(pairs[0], 1, flops=LARGE)
    (own,) = small_call(intensity_kernel, [(plan.share, VOX)], "intensity", value, *pairs[1])
    flip_x, flip_y, flip_z = plan.flip_dev
    near = [own, swap(own, flip_z, flip_x), swap(own, flip_x, flip_z)]
    near.append(swap(near[1], flip_x, flip_z))
    far = [swap(array, flip_y) for array in near]
    ordered = [near[0], near[1], far[0], far[1], near[2], near[3], far[2], far[3]]
    (result,) = small_call(functools.partial(unfold_kernel, plan), [(plan.boxes, VOX)], "unfold", *ordered)
    return result.reshape(GX // plan.sx, GY // plan.sy, GZ // plan.sz, BOX_BRICK, VOX)


def solution(mesh):
    return jax.shard_map(
        functools.partial(shards, Plan(mesh)),
        mesh=mesh,
        in_specs=(
            P(AXES, None, None, None),
            P(AXES, None, None, None),
            P(AXES, None, None, None),
            P(),
            P(),
            P(AXES),
            P(AXES, None),
            P(AXES),
        ),
        out_specs=P("bx", "by", "bz", None, None),
        check_vma=False,
    )
```

```python
import functools

import jax
import jax.numpy as jnp
from jax import lax
from jax.experimental import pallas as pl
from jax.experimental.pallas import tpu as pltpu
from jax.sharding import PartitionSpec as P

VOX = 256
LANES = 128
GX = 8
GY = 8
GZ = 4
BOX_BRICK = 64
FLIP_VOX = (0b11100000, 0b00011100, 0b00000011)
FLIP_BOX = (0b110000, 0b001100, 0b000011)
AXES = ("bx", "by", "bz")
POSITIONS = 8
FIRST = 4
TILE_LIMIT = 53 * 1024 * 1024
VMEM_LIMIT = 24 * 1024 * 1024
LARGE = 10**10
SWAPPED = (0, 4, 2, 6, 1, 5, 3, 7)
PIXEL_ROWS = 64


class Plan:
    def __init__(self, mesh):
        self.sx, self.sy, self.sz = (mesh.shape[name] for name in AXES)
        self.devices = self.sx * self.sy * self.sz
        lx, ly, lz = GX // self.sx, GY // self.sy, GZ // self.sz
        self.boxes = lx * ly * lz * BOX_BRICK
        self.share = self.boxes // 8
        self.flip_dev = ((self.sx - 1) * self.sy * self.sz, (self.sy - 1) * self.sz, self.sz - 1)
        self.half = (self.sx * self.sy * self.sz // 2, self.sy * self.sz // 2, self.sz // 2)
        self.flip_local = (
            (lx - 1) * ly * lz * BOX_BRICK + FLIP_BOX[0],
            (ly - 1) * lz * BOX_BRICK + FLIP_BOX[1],
            (lz - 1) * BOX_BRICK + FLIP_BOX[2],
        )

    def upper(self, device):
        return [(device & half) != 0 for half in self.half]

    def steps(self):
        row = self.sy * self.sz
        return (row, 1), (2 * row, 2)

    def box_row(self, place):
        (gather_a, gather_b), (first, second) = self.steps()
        has = lambda mask: (place & (mask * self.share)) != 0
        other_y = place // (self.sz * self.share) % self.sy
        odd = ((other_y ^ lax.axis_index("by")) & 1) != 0
        part = jnp.where(has(first), jnp.where(odd, 1, 2), 0) + jnp.where(has(second), jnp.where(odd, 2, 1), 0)
        row = (other_y * 4 + part) * self.share + place % self.share
        return jnp.where(has(gather_a) | has(gather_b), -1, row)

    def here(self):
        return (lax.axis_index("bx") * self.sy + lax.axis_index("by")) * self.sz + lax.axis_index("bz")


def masked(flags, masks):
    total = jnp.where(flags[0], masks[0], 0)
    for flag, mask in zip(flags[1:], masks[1:]):
        total = total ^ jnp.where(flag, mask, 0)
    return total


def lane_gather(values, index):
    return jnp.take_along_axis(values, index, axis=1, mode="promise_in_bounds")


def destination(plan, owner, box):
    upper = plan.upper(owner)
    local = box ^ masked(upper, plan.flip_local)
    part = local // plan.share
    row = local % plan.share
    holder = owner ^ masked(upper, plan.flip_dev)
    holder = holder ^ masked([(part & bit) != 0 for bit in (4, 2, 1)], plan.flip_dev)
    return holder * plan.share + row


def accumulate_kernel(counts, rows, cols, seen, value_out, weight_out, *scratch):
    arrays, sems, partial = scratch[:4], scratch[4], scratch[5]
    frames, positions = counts.shape[0], counts.shape[1]
    blocks = positions // POSITIONS

    def copies(start, count, slot):
        span = pl.ds(start, count)
        views = [(ref.at[:, span], held.at[:, span]) for ref, held in zip((counts, rows, cols), arrays)]
        views.append((seen.at[span], arrays[3].at[span]))
        return [pltpu.make_async_copy(src, dst, sems.at[slot, i]) for i, (src, dst) in enumerate(views)]

    early = [(0, FIRST, blocks), (FIRST, POSITIONS - FIRST, 0)]
    for landing in early + [(block * POSITIONS, POSITIONS, block) for block in range(1, blocks)]:
        for copy in copies(*landing):
            copy.start()

    held_counts, held_rows, held_cols, held_seen = arrays

    def compute(block, landings):
        for p in range(POSITIONS):
            if p in landings:
                for copy in copies(*landings[p]):
                    copy.wait()
            at = block * POSITIONS + p
            for f in range(frames):
                weights = held_cols[f, at]
                for kind in range(2):
                    total = None
                    for start in range(0, held_rows.shape[2], PIXEL_ROWS):
                        span = pl.ds(start, PIXEL_ROWS)
                        pixels = held_seen[at, span, :] if kind else held_counts[f, at, span, :]
                        item = jnp.dot(pixels, weights, preferred_element_type=jnp.float32)
                        item = held_rows[f, at, span, :].astype(jnp.float32) * item
                        item = jnp.sum(item.reshape(-1, 8, VOX), axis=0)
                        total = item if total is None else total + item
                    partial[f, kind, 0, p * 8 : (p + 1) * 8, :] = total[:, :LANES]
                    partial[f, kind, 1, p * 8 : (p + 1) * 8, :] = total[:, LANES:]
        for f in range(frames):
            place = pl.ds(pl.multiple_of(f * positions + block * POSITIONS, POSITIONS), POSITIONS)
            for kind, out in enumerate((value_out, weight_out)):
                for half in range(2):
                    lanes = pl.ds(half * LANES, LANES)
                    parts = [partial[f, kind, half, pl.ds(row, POSITIONS, stride=8), :] for row in range(8)]
                    out[place, lanes] = sum(parts)

    compute(0, {landing[0]: landing for landing in early})

    @pl.loop(1, blocks)
    def _(block):
        compute(block, {0: (block * POSITIONS, POSITIONS, block)})


def accumulate(counts, row_split, col_split, efficiency):
    frames, positions, pixels, _ = counts.shape
    tiles = frames * positions
    arrays = (counts, row_split, col_split, efficiency)
    return pl.pallas_call(
        accumulate_kernel,
        in_specs=[pl.BlockSpec(memory_space=pl.ANY)] * 4,
        out_specs=[pl.BlockSpec(memory_space=pltpu.VMEM)] * 2,
        out_shape=[jax.ShapeDtypeStruct((tiles, VOX), jnp.float32)] * 2,
        scratch_shapes=[pltpu.VMEM(array.shape, array.dtype) for array in arrays]
        + [
            pltpu.SemaphoreType.DMA((positions // POSITIONS + 1, 4)),
            pltpu.VMEM((frames, 2, 2, 8 * POSITIONS, LANES), jnp.float32),
        ],
        compiler_params=pltpu.CompilerParams(vmem_limit_bytes=TILE_LIMIT),
        cost_estimate=pl.CostEstimate(
            flops=4 * tiles * pixels * pixels * VOX,
            bytes_accessed=sum(array.size * 2 for array in arrays),
            transcendentals=0,
        ),
        name="tile_sums",
    )(*arrays)


def payload_kernel(plan, angles, lorentz, owner, box, value, weight, value_out, weight_out):
    tiles = value.shape[0]
    frames = angles.shape[1]
    table = lorentz[...].reshape(1, -1)
    entry = lax.broadcasted_iota(jnp.int32, table.shape, 1)
    factors = [
        jnp.sum(jnp.where(entry == angles[:, f : f + 1], table, 0.0), axis=1, keepdims=True) for f in range(frames)
    ]
    across = lax.broadcasted_iota(jnp.int32, (tiles, tiles), 1)
    down = lax.broadcasted_iota(jnp.int32, (tiles, tiles), 0)
    flips = masked(plan.upper(owner[...]), FLIP_VOX)
    flips = jnp.sum(jnp.where(across == down, flips, 0), axis=1, keepdims=True)
    ids = destination(plan, owner[...], box[...])
    for out in (value_out, weight_out):
        out[tiles : tiles + 8, :] = jnp.zeros((8, VOX), jnp.float32)
        out[tiles : tiles + 8, :tiles] = jnp.broadcast_to(ids.astype(jnp.float32), (8, tiles))
    lanes = lax.broadcasted_iota(jnp.int32, (8, LANES), 1)
    for start in range(0, tiles, 8):
        span = slice(start, start + 8)
        mask = jnp.broadcast_to(flips[span, :], (8, LANES))
        index = lanes ^ (mask & (LANES - 1))
        swap = (mask & LANES) != 0
        factor = factors[start // (tiles // frames)]
        for ref, out, scale in ((value, value_out, factor), (weight, weight_out, 1.0)):
            low, high = ref[span, :LANES], ref[span, LANES:]
            out[span, :LANES] = lane_gather(jnp.where(swap, high, low), index) * scale
            out[span, LANES:] = lane_gather(jnp.where(swap, low, high), index) * scale


def labelled(plan, angles, lorentz, owner, box, value, weight):
    shape = (value.shape[0] + 8, VOX)
    return pl.pallas_call(
        functools.partial(payload_kernel, plan),
        out_shape=[jax.ShapeDtypeStruct(shape, jnp.float32)] * 2,
        compiler_params=pltpu.CompilerParams(vmem_limit_bytes=VMEM_LIMIT),
        cost_estimate=pl.CostEstimate(flops=1, bytes_accessed=1, transcendentals=0),
        name="payload",
    )(angles.reshape(1, -1), lorentz, owner, box, value, weight)


def scatter_kernel(plan, olds, outs, payload, *refs):
    before, after = refs[:olds], refs[len(refs) - outs :]
    tiles = LANES
    half = payload.shape[0] // 2
    ids = [payload[start + tiles : start + tiles + 1, :tiles] for start in (0, half)]
    ids = plan.box_row(jnp.concatenate(ids, axis=1).astype(jnp.int32) ^ (plan.here() * plan.share))
    values = jnp.concatenate([payload[:tiles, :], payload[half : half + tiles, :]], axis=0)
    high = values.astype(jnp.bfloat16)
    low = (values - high.astype(jnp.float32)).astype(jnp.bfloat16)
    for number, out in enumerate(after):
        boxes = lax.broadcasted_iota(jnp.int32, (out.shape[0], ids.shape[1]), 0) + number * out.shape[0]
        pick = (boxes == ids).astype(jnp.float32).astype(jnp.bfloat16)
        total = jnp.dot(pick, high, preferred_element_type=jnp.float32)
        total = total + jnp.dot(pick, low, preferred_element_type=jnp.float32)
        out[...] = total + before[number][...] if olds else total


def join_kernel(first, second, *rest):
    half, out = first.shape[0], rest[-1]
    out[:half, :] = first[...]
    out[half:, :] = second[...]


def add_kernel(count, *refs):
    inputs, outs = refs[:count], refs[count:]
    start = 0
    for out in outs:
        span = slice(start, start + out.shape[0])
        total = inputs[0][span, :]
        for ref in inputs[1:]:
            total = total + ref[span, :]
        out[...] = total
        start += out.shape[0]


def intensity_kernel(value, *refs):
    inputs, out = refs[:-1], refs[-1]
    weight = inputs[0][...]
    for ref in inputs[1:]:
        weight = weight + ref[...]
    out[...] = value[...] * 0.125 / jnp.maximum(weight * 0.125, 1.0)


def unfold(plan, ref, number, write):
    upper = plan.upper(plan.here())
    local = masked(upper, plan.flip_local)
    mask = masked(upper, FLIP_VOX)
    index = lax.broadcasted_iota(jnp.int32, (8, LANES), 1) ^ (mask & (LANES - 1))
    turn = lax.broadcasted_iota(jnp.int32, (8, LANES), 0) ^ (local & 7)
    swap = (mask & LANES) != 0
    odd = (lax.axis_index("by") & 1) != 0
    codes = (number, SWAPPED[number])
    far = (number & 2) != 0
    relative = jnp.where(odd, codes[1 - far], codes[far])
    base = ((relative ^ masked(upper, (4, 2, 1))) * plan.share) ^ (local & ~(plan.share - 1))
    for group in range(0, plan.share, 8):
        rows = ref[group : group + 8, :]
        low, high = rows[:, :LANES], rows[:, LANES:]
        place = group ^ (local & (plan.share - 1) & ~7)
        for at, item in enumerate((jnp.where(swap, high, low), jnp.where(swap, low, high))):
            item = jnp.take_along_axis(item, turn, axis=0, mode="promise_in_bounds")
            write(base, place, slice(at * LANES, (at + 1) * LANES), lane_gather(item, index))
    return base


def unfold_kernel(plan, *refs):
    inputs, out = refs[:-1], refs[-1]

    def write(base, place, lanes, item):
        out[pl.ds(pl.multiple_of(base + place, 8), 8), lanes] = item

    for number, ref in enumerate(inputs):
        unfold(plan, ref, number, write)


def last_kernel(plan, number, ref, before, out, held, sem):
    def write(base, place, lanes, item):
        held[pl.ds(pl.multiple_of(place, 8), 8), lanes] = item

    base = unfold(plan, ref, number, write)
    copy = pltpu.make_async_copy(held, out.at[pl.ds(pl.multiple_of(base, 8), plan.share)], sem)
    copy.start()
    copy.wait()


def small_call(kernel, shapes, name, *arrays, flops=1):
    return pl.pallas_call(
        kernel,
        out_shape=[jax.ShapeDtypeStruct(shape, jnp.float32) for shape in shapes],
        compiler_params=pltpu.CompilerParams(vmem_limit_bytes=VMEM_LIMIT),
        cost_estimate=pl.CostEstimate(flops=flops, bytes_accessed=1, transcendentals=0),
        name=name,
    )(*arrays)


def shards(plan, counts, row_split, col_split, efficiency, lorentz, angles, tile_owner, tile_box):
    def swap(array, even, odd=None):
        odd = even if odd is None else odd
        pairs = [(i, i ^ (odd if i // plan.sz % 2 else even)) for i in range(plan.devices)]
        return lax.ppermute(array, AXES, pairs)

    def join(first, second, *order):
        rows, width = first.shape
        return small_call(join_kernel, [(2 * rows, width)], "join", first, second, *order)[0]

    gather_steps, reduce_steps = plan.steps()
    owner = tile_owner.reshape(1, -1)
    box = tile_box.reshape(1, -1)
    own = accumulate(counts, row_split, col_split, efficiency)
    own = labelled(plan, angles, lorentz, owner, box, *own)
    arrived = [swap(array, *gather_steps) for array in own]
    near = [join(own[0], arrived[0])]
    near.append(join(own[1], arrived[1], near[0]))
    far = [swap(array, *gather_steps[::-1]) for array in near]
    def box_sums(payload, olds, *waits, flops=1):
        kernel = functools.partial(scatter_kernel, plan, len(olds), plan.sy)
        shapes = [(4 * plan.share, VOX)] * plan.sy
        return small_call(kernel, shapes, "box_sums", payload, *olds, *waits, flops=flops)

    def added(arrays, pieces, flops=1):
        shape = (arrays[0].shape[0] // pieces, VOX)
        kernel = functools.partial(add_kernel, len(arrays))
        return small_call(kernel, [shape] * pieces, "added", *arrays, flops=flops)

    sums = [box_sums(near[0], []), box_sums(near[1], [], flops=LARGE)]
    pairs, waits = [], [sums[1][0]]
    for kind in range(2):
        parts = box_sums(far[kind], sums[kind], *waits, flops=LARGE if kind else 1)
        waits = [parts[0]]
        parts = [parts[0]] + [swap(parts[i], i * plan.sz) for i in range(1, plan.sy)]
        for even, odd in (reduce_steps, reduce_steps[::-1]):
            keep, give = added(parts, 2)
            parts = [keep, swap(give, even, odd)]
        pairs.append(parts)
    (value,) = added(pairs[0], 1, flops=LARGE)
    (own,) = small_call(intensity_kernel, [(plan.share, VOX)], "intensity", value, *pairs[1])
    flip_x, flip_y, flip_z = plan.flip_dev
    near = [own, swap(own, flip_z, flip_x), swap(own, flip_x, flip_z)]
    near.append(swap(near[1], flip_x, flip_z))
    far = [swap(array, flip_y) for array in near]
    ordered = [near[0], near[1], far[0], far[1], near[2], near[3], far[2], far[3]]
    shape = jax.ShapeDtypeStruct((plan.boxes, VOX), jnp.float32)
    (result,) = small_call(functools.partial(unfold_kernel, plan), [shape.shape], "unfold", *ordered[:-1], flops=LARGE)
    result = pl.pallas_call(
        functools.partial(last_kernel, plan, len(ordered) - 1),
        in_specs=[pl.BlockSpec(memory_space=pltpu.VMEM), pl.BlockSpec(memory_space=pl.ANY)],
        out_specs=pl.BlockSpec(memory_space=pl.ANY),
        out_shape=shape,
        scratch_shapes=[pltpu.VMEM((plan.share, VOX), jnp.float32), pltpu.SemaphoreType.DMA(())],
        input_output_aliases={1: 0},
        compiler_params=pltpu.CompilerParams(vmem_limit_bytes=VMEM_LIMIT),
        name="last",
    )(ordered[-1], result)
    return result.reshape(GX // plan.sx, GY // plan.sy, GZ // plan.sz, BOX_BRICK, VOX)


def solution(mesh):
    return jax.shard_map(
        functools.partial(shards, Plan(mesh)),
        mesh=mesh,
        in_specs=(
            P(AXES, None, None, None),
            P(AXES, None, None, None),
            P(AXES, None, None, None),
            P(),
            P(),
            P(AXES),
            P(AXES, None),
            P(AXES),
        ),
        out_specs=P("bx", "by", "bz", None, None),
        check_vma=False,
    )
```

```python
import functools

import jax
import jax.numpy as jnp
from jax import lax
from jax.experimental import pallas as pl
from jax.experimental.pallas import tpu as pltpu
from jax.sharding import PartitionSpec as P

VOX = 256
LANES = 128
GX = 8
GY = 8
GZ = 4
BOX_BRICK = 64
FLIP_VOX = (0b11100000, 0b00011100, 0b00000011)
FLIP_BOX = (0b110000, 0b001100, 0b000011)
AXES = ("bx", "by", "bz")
POSITIONS = 8
FIRST = 4
TILE_LIMIT = 53 * 1024 * 1024
VMEM_LIMIT = 24 * 1024 * 1024
LARGE = 10**10
SWAPPED = (0, 4, 2, 6, 1, 5, 3, 7)
PIXEL_ROWS = 64


class Plan:
    def __init__(self, mesh):
        self.sx, self.sy, self.sz = (mesh.shape[name] for name in AXES)
        self.devices = self.sx * self.sy * self.sz
        lx, ly, lz = GX // self.sx, GY // self.sy, GZ // self.sz
        self.boxes = lx * ly * lz * BOX_BRICK
        self.share = self.boxes // 8
        self.flip_dev = ((self.sx - 1) * self.sy * self.sz, (self.sy - 1) * self.sz, self.sz - 1)
        self.half = (self.sx * self.sy * self.sz // 2, self.sy * self.sz // 2, self.sz // 2)
        self.flip_local = (
            (lx - 1) * ly * lz * BOX_BRICK + FLIP_BOX[0],
            (ly - 1) * lz * BOX_BRICK + FLIP_BOX[1],
            (lz - 1) * BOX_BRICK + FLIP_BOX[2],
        )

    def upper(self, device):
        return [(device & half) != 0 for half in self.half]

    def steps(self):
        row = self.sy * self.sz
        return (row, 1), (2 * row, 2)

    def box_row(self, place):
        (gather_a, gather_b), (first, second) = self.steps()
        has = lambda mask: (place & (mask * self.share)) != 0
        other_y = place // (self.sz * self.share) % self.sy
        odd = ((other_y ^ lax.axis_index("by")) & 1) != 0
        part = jnp.where(has(first), jnp.where(odd, 1, 2), 0) + jnp.where(has(second), jnp.where(odd, 2, 1), 0)
        row = (other_y * 4 + part) * self.share + place % self.share
        return jnp.where(has(gather_a) | has(gather_b), -1, row)

    def here(self):
        return (lax.axis_index("bx") * self.sy + lax.axis_index("by")) * self.sz + lax.axis_index("bz")


def masked(flags, masks):
    total = jnp.where(flags[0], masks[0], 0)
    for flag, mask in zip(flags[1:], masks[1:]):
        total = total ^ jnp.where(flag, mask, 0)
    return total


def lane_gather(values, index):
    return jnp.take_along_axis(values, index, axis=1, mode="promise_in_bounds")


def destination(plan, owner, box):
    upper = plan.upper(owner)
    local = box ^ masked(upper, plan.flip_local)
    part = local // plan.share
    row = local % plan.share
    holder = owner ^ masked(upper, plan.flip_dev)
    holder = holder ^ masked([(part & bit) != 0 for bit in (4, 2, 1)], plan.flip_dev)
    return holder * plan.share + row


def accumulate_kernel(counts, rows, cols, seen, value_out, weight_out, *scratch):
    arrays, sems, partial = scratch[:4], scratch[4], scratch[5]
    frames, positions = counts.shape[0], counts.shape[1]
    blocks = positions // POSITIONS

    def copies(start, count, slot):
        span = pl.ds(start, count)
        views = [(ref.at[:, span], held.at[:, span]) for ref, held in zip((counts, rows, cols), arrays)]
        views.append((seen.at[span], arrays[3].at[span]))
        return [pltpu.make_async_copy(src, dst, sems.at[slot, i]) for i, (src, dst) in enumerate(views)]

    early = [(0, FIRST, blocks), (FIRST, POSITIONS - FIRST, 0)]
    for landing in early + [(block * POSITIONS, POSITIONS, block) for block in range(1, blocks)]:
        for copy in copies(*landing):
            copy.start()

    held_counts, held_rows, held_cols, held_seen = arrays

    def compute(block, landings):
        for p in range(POSITIONS):
            if p in landings:
                for copy in copies(*landings[p]):
                    copy.wait()
            at = block * POSITIONS + p
            for f in range(frames):
                weights = held_cols[f, at]
                for kind in range(2):
                    total = None
                    for start in range(0, held_rows.shape[2], PIXEL_ROWS):
                        span = pl.ds(start, PIXEL_ROWS)
                        pixels = held_seen[at, span, :] if kind else held_counts[f, at, span, :]
                        item = jnp.dot(pixels, weights, preferred_element_type=jnp.float32)
                        item = held_rows[f, at, span, :].astype(jnp.float32) * item
                        item = jnp.sum(item.reshape(-1, 8, VOX), axis=0)
                        total = item if total is None else total + item
                    partial[f, kind, 0, p * 8 : (p + 1) * 8, :] = total[:, :LANES]
                    partial[f, kind, 1, p * 8 : (p + 1) * 8, :] = total[:, LANES:]
        for f in range(frames):
            place = pl.ds(pl.multiple_of(f * positions + block * POSITIONS, POSITIONS), POSITIONS)
            for kind, out in enumerate((value_out, weight_out)):
                for half in range(2):
                    lanes = pl.ds(half * LANES, LANES)
                    parts = [partial[f, kind, half, pl.ds(row, POSITIONS, stride=8), :] for row in range(8)]
                    out[place, lanes] = sum(parts)

    compute(0, {landing[0]: landing for landing in early})

    @pl.loop(1, blocks)
    def _(block):
        compute(block, {0: (block * POSITIONS, POSITIONS, block)})


def accumulate(counts, row_split, col_split, efficiency):
    frames, positions, pixels, _ = counts.shape
    tiles = frames * positions
    arrays = (counts, row_split, col_split, efficiency)
    return pl.pallas_call(
        accumulate_kernel,
        in_specs=[pl.BlockSpec(memory_space=pl.ANY)] * 4,
        out_specs=[pl.BlockSpec(memory_space=pltpu.VMEM)] * 2,
        out_shape=[jax.ShapeDtypeStruct((tiles, VOX), jnp.float32)] * 2,
        scratch_shapes=[pltpu.VMEM(array.shape, array.dtype) for array in arrays]
        + [
            pltpu.SemaphoreType.DMA((positions // POSITIONS + 1, 4)),
            pltpu.VMEM((frames, 2, 2, 8 * POSITIONS, LANES), jnp.float32),
        ],
        compiler_params=pltpu.CompilerParams(vmem_limit_bytes=TILE_LIMIT),
        cost_estimate=pl.CostEstimate(
            flops=4 * tiles * pixels * pixels * VOX,
            bytes_accessed=sum(array.size * 2 for array in arrays),
            transcendentals=0,
        ),
        name="tile_sums",
    )(*arrays)


def payload_kernel(plan, angles, lorentz, owner, box, value, weight, value_out, weight_out):
    tiles = value.shape[0]
    frames = angles.shape[1]
    table = lorentz[...].reshape(1, -1)
    entry = lax.broadcasted_iota(jnp.int32, table.shape, 1)
    factors = [
        jnp.sum(jnp.where(entry == angles[:, f : f + 1], table, 0.0), axis=1, keepdims=True) for f in range(frames)
    ]
    across = lax.broadcasted_iota(jnp.int32, (tiles, tiles), 1)
    down = lax.broadcasted_iota(jnp.int32, (tiles, tiles), 0)
    flips = masked(plan.upper(owner[...]), FLIP_VOX)
    flips = jnp.sum(jnp.where(across == down, flips, 0), axis=1, keepdims=True)
    ids = destination(plan, owner[...], box[...])
    value_out[tiles : tiles + 8, :] = jnp.zeros((8, VOX), jnp.float32)
    value_out[tiles : tiles + 8, :tiles] = jnp.broadcast_to(ids.astype(jnp.float32), (8, tiles))
    lanes = lax.broadcasted_iota(jnp.int32, (8, LANES), 1)
    for start in range(0, tiles, 8):
        span = slice(start, start + 8)
        mask = jnp.broadcast_to(flips[span, :], (8, LANES))
        index = lanes ^ (mask & (LANES - 1))
        swap = (mask & LANES) != 0
        factor = factors[start // (tiles // frames)]
        for ref, out, scale in ((value, value_out, factor), (weight, weight_out, 1.0)):
            low, high = ref[span, :LANES], ref[span, LANES:]
            out[span, :LANES] = lane_gather(jnp.where(swap, high, low), index) * scale
            out[span, LANES:] = lane_gather(jnp.where(swap, low, high), index) * scale


def labelled(plan, angles, lorentz, owner, box, value, weight):
    tiles = value.shape[0]
    return pl.pallas_call(
        functools.partial(payload_kernel, plan),
        out_shape=[jax.ShapeDtypeStruct((rows, VOX), jnp.float32) for rows in (tiles + 8, tiles)],
        compiler_params=pltpu.CompilerParams(vmem_limit_bytes=VMEM_LIMIT),
        cost_estimate=pl.CostEstimate(flops=1, bytes_accessed=1, transcendentals=0),
        name="payload",
    )(angles.reshape(1, -1), lorentz, owner, box, value, weight)


def scatter_kernel(plan, olds, outs, names, payload, *refs):
    before, after = refs[:olds], refs[len(refs) - outs :]
    tiles = LANES
    half = payload.shape[0] // 2
    ids = [names[start + tiles : start + tiles + 1, :tiles] for start in (0, names.shape[0] // 2)]
    ids = plan.box_row(jnp.concatenate(ids, axis=1).astype(jnp.int32) ^ (plan.here() * plan.share))
    values = jnp.concatenate([payload[:tiles, :], payload[half : half + tiles, :]], axis=0)
    high = values.astype(jnp.bfloat16)
    low = (values - high.astype(jnp.float32)).astype(jnp.bfloat16)
    for number, out in enumerate(after):
        boxes = lax.broadcasted_iota(jnp.int32, (out.shape[0], ids.shape[1]), 0) + number * out.shape[0]
        pick = (boxes == ids).astype(jnp.float32).astype(jnp.bfloat16)
        total = jnp.dot(pick, high, preferred_element_type=jnp.float32)
        total = total + jnp.dot(pick, low, preferred_element_type=jnp.float32)
        out[...] = total + before[number][...] if olds else total


def join_kernel(first, second, *rest):
    half, out = first.shape[0], rest[-1]
    out[:half, :] = first[...]
    out[half:, :] = second[...]


def add_kernel(count, *refs):
    inputs, outs = refs[:count], refs[count:]
    start = 0
    for out in outs:
        span = slice(start, start + out.shape[0])
        total = inputs[0][span, :]
        for ref in inputs[1:]:
            total = total + ref[span, :]
        out[...] = total
        start += out.shape[0]


def intensity_kernel(value, *refs):
    inputs, out = refs[:-1], refs[-1]
    weight = inputs[0][...]
    for ref in inputs[1:]:
        weight = weight + ref[...]
    out[...] = value[...] * 0.125 / jnp.maximum(weight * 0.125, 1.0)


def unfold(plan, ref, number, write):
    upper = plan.upper(plan.here())
    local = masked(upper, plan.flip_local)
    mask = masked(upper, FLIP_VOX)
    index = lax.broadcasted_iota(jnp.int32, (8, LANES), 1) ^ (mask & (LANES - 1))
    turn = lax.broadcasted_iota(jnp.int32, (8, LANES), 0) ^ (local & 7)
    swap = (mask & LANES) != 0
    odd = (lax.axis_index("by") & 1) != 0
    codes = (number, SWAPPED[number])
    far = (number & 2) != 0
    relative = jnp.where(odd, codes[1 - far], codes[far])
    base = ((relative ^ masked(upper, (4, 2, 1))) * plan.share) ^ (local & ~(plan.share - 1))
    for group in range(0, plan.share, 8):
        rows = ref[group : group + 8, :]
        low, high = rows[:, :LANES], rows[:, LANES:]
        place = group ^ (local & (plan.share - 1) & ~7)
        for at, item in enumerate((jnp.where(swap, high, low), jnp.where(swap, low, high))):
            item = jnp.take_along_axis(item, turn, axis=0, mode="promise_in_bounds")
            write(base, place, slice(at * LANES, (at + 1) * LANES), lane_gather(item, index))
    return base


def unfold_kernel(plan, *refs):
    inputs, out = refs[:-1], refs[-1]

    def write(base, place, lanes, item):
        out[pl.ds(pl.multiple_of(base + place, 8), 8), lanes] = item

    for number, ref in enumerate(inputs):
        unfold(plan, ref, number, write)


def last_kernel(plan, number, ref, before, out, held, sem):
    def write(base, place, lanes, item):
        held[pl.ds(pl.multiple_of(place, 8), 8), lanes] = item

    base = unfold(plan, ref, number, write)
    copy = pltpu.make_async_copy(held, out.at[pl.ds(pl.multiple_of(base, 8), plan.share)], sem)
    copy.start()
    copy.wait()


def small_call(kernel, shapes, name, *arrays, flops=1):
    return pl.pallas_call(
        kernel,
        out_shape=[jax.ShapeDtypeStruct(shape, jnp.float32) for shape in shapes],
        compiler_params=pltpu.CompilerParams(vmem_limit_bytes=VMEM_LIMIT),
        cost_estimate=pl.CostEstimate(flops=flops, bytes_accessed=1, transcendentals=0),
        name=name,
    )(*arrays)


def shards(plan, counts, row_split, col_split, efficiency, lorentz, angles, tile_owner, tile_box):
    def swap(array, even, odd=None):
        odd = even if odd is None else odd
        pairs = [(i, i ^ (odd if i // plan.sz % 2 else even)) for i in range(plan.devices)]
        return lax.ppermute(array, AXES, pairs)

    def join(first, second, *order):
        rows, width = first.shape
        return small_call(join_kernel, [(2 * rows, width)], "join", first, second, *order)[0]

    gather_steps, reduce_steps = plan.steps()
    owner = tile_owner.reshape(1, -1)
    box = tile_box.reshape(1, -1)
    own = accumulate(counts, row_split, col_split, efficiency)
    own = labelled(plan, angles, lorentz, owner, box, *own)
    arrived = [swap(array, *gather_steps) for array in own]
    near = [join(own[0], arrived[0])]
    near.append(join(own[1], arrived[1], near[0]))
    far = [swap(array, *gather_steps[::-1]) for array in near]
    def box_sums(names, payload, olds, *waits, flops=1):
        kernel = functools.partial(scatter_kernel, plan, len(olds), plan.sy)
        shapes = [(4 * plan.share, VOX)] * plan.sy
        return small_call(kernel, shapes, "box_sums", names, payload, *olds, *waits, flops=flops)

    def added(arrays, pieces, flops=1):
        shape = (arrays[0].shape[0] // pieces, VOX)
        kernel = functools.partial(add_kernel, len(arrays))
        return small_call(kernel, [shape] * pieces, "added", *arrays, flops=flops)

    sums = [box_sums(near[0], near[0], []), box_sums(near[0], near[1], [], flops=LARGE)]
    pairs, waits = [], [sums[1][0]]
    for kind in range(2):
        parts = box_sums(far[0], far[kind], sums[kind], *waits, flops=LARGE if kind else 1)
        waits = [parts[0]]
        parts = [parts[0]] + [swap(parts[i], i * plan.sz) for i in range(1, plan.sy)]
        for even, odd in (reduce_steps, reduce_steps[::-1]):
            keep, give = added(parts, 2)
            parts = [keep, swap(give, even, odd)]
        pairs.append(parts)
    (value,) = added(pairs[0], 1, flops=LARGE)
    (own,) = small_call(intensity_kernel, [(plan.share, VOX)], "intensity", value, *pairs[1])
    flip_x, flip_y, flip_z = plan.flip_dev
    near = [own, swap(own, flip_z, flip_x), swap(own, flip_x, flip_z)]
    near.append(swap(near[1], flip_x, flip_z))
    far = [swap(array, flip_y) for array in near]
    ordered = [near[0], near[1], far[0], far[1], near[2], near[3], far[2], far[3]]
    shape = jax.ShapeDtypeStruct((plan.boxes, VOX), jnp.float32)
    (result,) = small_call(functools.partial(unfold_kernel, plan), [shape.shape], "unfold", *ordered[:-1], flops=LARGE)
    result = pl.pallas_call(
        functools.partial(last_kernel, plan, len(ordered) - 1),
        in_specs=[pl.BlockSpec(memory_space=pltpu.VMEM), pl.BlockSpec(memory_space=pl.ANY)],
        out_specs=pl.BlockSpec(memory_space=pl.ANY),
        out_shape=shape,
        scratch_shapes=[pltpu.VMEM((plan.share, VOX), jnp.float32), pltpu.SemaphoreType.DMA(())],
        input_output_aliases={1: 0},
        compiler_params=pltpu.CompilerParams(vmem_limit_bytes=VMEM_LIMIT),
        name="last",
    )(ordered[-1], result)
    return result.reshape(GX // plan.sx, GY // plan.sy, GZ // plan.sz, BOX_BRICK, VOX)


def solution(mesh):
    return jax.shard_map(
        functools.partial(shards, Plan(mesh)),
        mesh=mesh,
        in_specs=(
            P(AXES, None, None, None),
            P(AXES, None, None, None),
            P(AXES, None, None, None),
            P(),
            P(),
            P(AXES),
            P(AXES, None),
            P(AXES),
        ),
        out_specs=P("bx", "by", "bz", None, None),
        check_vma=False,
    )
```

```python
import functools

import jax
import jax.numpy as jnp
from jax import lax
from jax.experimental import pallas as pl
from jax.experimental.pallas import tpu as pltpu
from jax.sharding import PartitionSpec as P

VOX = 256
LANES = 128
GX = 8
GY = 8
GZ = 4
BOX_BRICK = 64
FLIP_VOX = (0b11100000, 0b00011100, 0b00000011)
FLIP_BOX = (0b110000, 0b001100, 0b000011)
AXES = ("bx", "by", "bz")
POSITIONS = 8
FIRST = 4
TILE_LIMIT = 53 * 1024 * 1024
VMEM_LIMIT = 24 * 1024 * 1024
LARGE = 10**10
SWAPPED = (0, 4, 2, 6, 1, 5, 3, 7)
PIXEL_ROWS = 64


class Plan:
    def __init__(self, mesh):
        self.sx, self.sy, self.sz = (mesh.shape[name] for name in AXES)
        self.devices = self.sx * self.sy * self.sz
        lx, ly, lz = GX // self.sx, GY // self.sy, GZ // self.sz
        self.boxes = lx * ly * lz * BOX_BRICK
        self.share = self.boxes // 8
        self.flip_dev = ((self.sx - 1) * self.sy * self.sz, (self.sy - 1) * self.sz, self.sz - 1)
        self.half = (self.sx * self.sy * self.sz // 2, self.sy * self.sz // 2, self.sz // 2)
        self.flip_local = (
            (lx - 1) * ly * lz * BOX_BRICK + FLIP_BOX[0],
            (ly - 1) * lz * BOX_BRICK + FLIP_BOX[1],
            (lz - 1) * BOX_BRICK + FLIP_BOX[2],
        )

    def upper(self, device):
        return [(device & half) != 0 for half in self.half]

    def steps(self):
        row = self.sy * self.sz
        return (1, row), (2 * row, 2)

    def box_row(self, place):
        (gather_a, gather_b), (first, second) = self.steps()
        has = lambda mask: (place & (mask * self.share)) != 0
        other_y = place // (self.sz * self.share) % self.sy
        odd = ((other_y ^ lax.axis_index("by")) & 1) != 0
        part = jnp.where(has(first), jnp.where(odd, 1, 2), 0) + jnp.where(has(second), jnp.where(odd, 2, 1), 0)
        row = (other_y * 4 + part) * self.share + place % self.share
        return jnp.where(has(gather_a) | has(gather_b), -1, row)

    def here(self):
        return (lax.axis_index("bx") * self.sy + lax.axis_index("by")) * self.sz + lax.axis_index("bz")


def masked(flags, masks):
    total = jnp.where(flags[0], masks[0], 0)
    for flag, mask in zip(flags[1:], masks[1:]):
        total = total ^ jnp.where(flag, mask, 0)
    return total


def lane_gather(values, index):
    return jnp.take_along_axis(values, index, axis=1, mode="promise_in_bounds")


def destination(plan, owner, box):
    upper = plan.upper(owner)
    local = box ^ masked(upper, plan.flip_local)
    part = local // plan.share
    row = local % plan.share
    holder = owner ^ masked(upper, plan.flip_dev)
    holder = holder ^ masked([(part & bit) != 0 for bit in (4, 2, 1)], plan.flip_dev)
    return holder * plan.share + row


def accumulate_kernel(counts, rows, cols, seen, value_out, weight_out, *scratch):
    arrays, sems, partial = scratch[:4], scratch[4], scratch[5]
    frames, positions = counts.shape[0], counts.shape[1]
    blocks = positions // POSITIONS

    def copies(start, count, slot):
        span = pl.ds(start, count)
        views = [(ref.at[:, span], held.at[:, span]) for ref, held in zip((counts, rows, cols), arrays)]
        views.append((seen.at[span], arrays[3].at[span]))
        return [pltpu.make_async_copy(src, dst, sems.at[slot, i]) for i, (src, dst) in enumerate(views)]

    early = [(0, FIRST, blocks), (FIRST, POSITIONS - FIRST, 0)]
    for landing in early + [(block * POSITIONS, POSITIONS, block) for block in range(1, blocks)]:
        for copy in copies(*landing):
            copy.start()

    held_counts, held_rows, held_cols, held_seen = arrays

    def compute(block, landings):
        for p in range(POSITIONS):
            if p in landings:
                for copy in copies(*landings[p]):
                    copy.wait()
            at = block * POSITIONS + p
            for f in range(frames):
                weights = held_cols[f, at]
                for kind in range(2):
                    total = None
                    for start in range(0, held_rows.shape[2], PIXEL_ROWS):
                        span = pl.ds(start, PIXEL_ROWS)
                        pixels = held_seen[at, span, :] if kind else held_counts[f, at, span, :]
                        item = jnp.dot(pixels, weights, preferred_element_type=jnp.float32)
                        item = held_rows[f, at, span, :].astype(jnp.float32) * item
                        item = jnp.sum(item.reshape(-1, 8, VOX), axis=0)
                        total = item if total is None else total + item
                    partial[f, kind, 0, p * 8 : (p + 1) * 8, :] = total[:, :LANES]
                    partial[f, kind, 1, p * 8 : (p + 1) * 8, :] = total[:, LANES:]
        for f in range(frames):
            place = pl.ds(pl.multiple_of(f * positions + block * POSITIONS, POSITIONS), POSITIONS)
            for kind, out in enumerate((value_out, weight_out)):
                for half in range(2):
                    lanes = pl.ds(half * LANES, LANES)
                    parts = [partial[f, kind, half, pl.ds(row, POSITIONS, stride=8), :] for row in range(8)]
                    out[place, lanes] = sum(parts)

    compute(0, {landing[0]: landing for landing in early})

    @pl.loop(1, blocks)
    def _(block):
        compute(block, {0: (block * POSITIONS, POSITIONS, block)})


def accumulate(counts, row_split, col_split, efficiency):
    frames, positions, pixels, _ = counts.shape
    tiles = frames * positions
    arrays = (counts, row_split, col_split, efficiency)
    return pl.pallas_call(
        accumulate_kernel,
        in_specs=[pl.BlockSpec(memory_space=pl.ANY)] * 4,
        out_specs=[pl.BlockSpec(memory_space=pltpu.VMEM)] * 2,
        out_shape=[jax.ShapeDtypeStruct((tiles, VOX), jnp.float32)] * 2,
        scratch_shapes=[pltpu.VMEM(array.shape, array.dtype) for array in arrays]
        + [
            pltpu.SemaphoreType.DMA((positions // POSITIONS + 1, 4)),
            pltpu.VMEM((frames, 2, 2, 8 * POSITIONS, LANES), jnp.float32),
        ],
        compiler_params=pltpu.CompilerParams(vmem_limit_bytes=TILE_LIMIT),
        cost_estimate=pl.CostEstimate(
            flops=4 * tiles * pixels * pixels * VOX,
            bytes_accessed=sum(array.size * 2 for array in arrays),
            transcendentals=0,
        ),
        name="tile_sums",
    )(*arrays)


def payload_kernel(plan, angles, lorentz, owner, box, value, weight, value_out, weight_out):
    tiles = value.shape[0]
    frames = angles.shape[1]
    table = lorentz[...].reshape(1, -1)
    entry = lax.broadcasted_iota(jnp.int32, table.shape, 1)
    factors = [
        jnp.sum(jnp.where(entry == angles[:, f : f + 1], table, 0.0), axis=1, keepdims=True) for f in range(frames)
    ]
    across = lax.broadcasted_iota(jnp.int32, (tiles, tiles), 1)
    down = lax.broadcasted_iota(jnp.int32, (tiles, tiles), 0)
    flips = masked(plan.upper(owner[...]), FLIP_VOX)
    flips = jnp.sum(jnp.where(across == down, flips, 0), axis=1, keepdims=True)
    ids = destination(plan, owner[...], box[...])
    for out in (value_out, weight_out):
        out[tiles : tiles + 8, :] = jnp.zeros((8, VOX), jnp.float32)
        out[tiles : tiles + 8, :tiles] = jnp.broadcast_to(ids.astype(jnp.float32), (8, tiles))
    lanes = lax.broadcasted_iota(jnp.int32, (8, LANES), 1)
    for start in range(0, tiles, 8):
        span = slice(start, start + 8)
        mask = jnp.broadcast_to(flips[span, :], (8, LANES))
        index = lanes ^ (mask & (LANES - 1))
        swap = (mask & LANES) != 0
        factor = factors[start // (tiles // frames)]
        for ref, out, scale in ((value, value_out, factor), (weight, weight_out, 1.0)):
            low, high = ref[span, :LANES], ref[span, LANES:]
            out[span, :LANES] = lane_gather(jnp.where(swap, high, low), index) * scale
            out[span, LANES:] = lane_gather(jnp.where(swap, low, high), index) * scale


def labelled(plan, angles, lorentz, owner, box, value, weight):
    shape = (value.shape[0] + 8, VOX)
    return pl.pallas_call(
        functools.partial(payload_kernel, plan),
        out_shape=[jax.ShapeDtypeStruct(shape, jnp.float32)] * 2,
        compiler_params=pltpu.CompilerParams(vmem_limit_bytes=VMEM_LIMIT),
        cost_estimate=pl.CostEstimate(flops=1, bytes_accessed=1, transcendentals=0),
        name="payload",
    )(angles.reshape(1, -1), lorentz, owner, box, value, weight)


def scatter_kernel(plan, olds, outs, payload, *refs):
    before, after = refs[:olds], refs[len(refs) - outs :]
    tiles = LANES
    half = payload.shape[0] // 2
    ids = [payload[start + tiles : start + tiles + 1, :tiles] for start in (0, half)]
    ids = plan.box_row(jnp.concatenate(ids, axis=1).astype(jnp.int32) ^ (plan.here() * plan.share))
    values = jnp.concatenate([payload[:tiles, :], payload[half : half + tiles, :]], axis=0)
    high = values.astype(jnp.bfloat16)
    low = (values - high.astype(jnp.float32)).astype(jnp.bfloat16)
    for number, out in enumerate(after):
        boxes = lax.broadcasted_iota(jnp.int32, (out.shape[0], ids.shape[1]), 0) + number * out.shape[0]
        pick = (boxes == ids).astype(jnp.float32).astype(jnp.bfloat16)
        total = jnp.dot(pick, high, preferred_element_type=jnp.float32)
        total = total + jnp.dot(pick, low, preferred_element_type=jnp.float32)
        out[...] = total + before[number][...] if olds else total


def join_kernel(first, second, *rest):
    half, out = first.shape[0], rest[-1]
    out[:half, :] = first[...]
    out[half:, :] = second[...]


def add_kernel(count, *refs):
    inputs, outs = refs[:count], refs[count:]
    start = 0
    for out in outs:
        span = slice(start, start + out.shape[0])
        total = inputs[0][span, :]
        for ref in inputs[1:]:
            total = total + ref[span, :]
        out[...] = total
        start += out.shape[0]


def intensity_kernel(value, *refs):
    inputs, out = refs[:-1], refs[-1]
    weight = inputs[0][...]
    for ref in inputs[1:]:
        weight = weight + ref[...]
    out[...] = value[...] * 0.125 / jnp.maximum(weight * 0.125, 1.0)


def unfold(plan, ref, number, write):
    upper = plan.upper(plan.here())
    local = masked(upper, plan.flip_local)
    mask = masked(upper, FLIP_VOX)
    index = lax.broadcasted_iota(jnp.int32, (8, LANES), 1) ^ (mask & (LANES - 1))
    turn = lax.broadcasted_iota(jnp.int32, (8, LANES), 0) ^ (local & 7)
    swap = (mask & LANES) != 0
    odd = (lax.axis_index("by") & 1) != 0
    codes = (number, SWAPPED[number])
    far = (number & 2) != 0
    relative = jnp.where(odd, codes[1 - far], codes[far])
    base = ((relative ^ masked(upper, (4, 2, 1))) * plan.share) ^ (local & ~(plan.share - 1))
    for group in range(0, plan.share, 8):
        rows = ref[group : group + 8, :]
        low, high = rows[:, :LANES], rows[:, LANES:]
        place = group ^ (local & (plan.share - 1) & ~7)
        for at, item in enumerate((jnp.where(swap, high, low), jnp.where(swap, low, high))):
            item = jnp.take_along_axis(item, turn, axis=0, mode="promise_in_bounds")
            write(base, place, slice(at * LANES, (at + 1) * LANES), lane_gather(item, index))
    return base


def unfold_kernel(plan, *refs):
    inputs, out = refs[:-1], refs[-1]

    def write(base, place, lanes, item):
        out[pl.ds(pl.multiple_of(base + place, 8), 8), lanes] = item

    for number, ref in enumerate(inputs):
        unfold(plan, ref, number, write)


def last_kernel(plan, number, ref, before, out, held, sem):
    def write(base, place, lanes, item):
        held[pl.ds(pl.multiple_of(place, 8), 8), lanes] = item

    base = unfold(plan, ref, number, write)
    copy = pltpu.make_async_copy(held, out.at[pl.ds(pl.multiple_of(base, 8), plan.share)], sem)
    copy.start()
    copy.wait()


def small_call(kernel, shapes, name, *arrays, flops=1):
    return pl.pallas_call(
        kernel,
        out_shape=[jax.ShapeDtypeStruct(shape, jnp.float32) for shape in shapes],
        compiler_params=pltpu.CompilerParams(vmem_limit_bytes=VMEM_LIMIT),
        cost_estimate=pl.CostEstimate(flops=flops, bytes_accessed=1, transcendentals=0),
        name=name,
    )(*arrays)


def shards(plan, counts, row_split, col_split, efficiency, lorentz, angles, tile_owner, tile_box):
    def swap(array, even, odd=None):
        odd = even if odd is None else odd
        pairs = [(i, i ^ (odd if i // plan.sz % 2 else even)) for i in range(plan.devices)]
        return lax.ppermute(array, AXES, pairs)

    def join(first, second, *order):
        rows, width = first.shape
        return small_call(join_kernel, [(2 * rows, width)], "join", first, second, *order)[0]

    gather_steps, reduce_steps = plan.steps()
    owner = tile_owner.reshape(1, -1)
    box = tile_box.reshape(1, -1)
    own = accumulate(counts, row_split, col_split, efficiency)
    own = labelled(plan, angles, lorentz, owner, box, *own)
    arrived = [swap(array, *gather_steps) for array in own]
    near = [join(own[0], arrived[0])]
    near.append(join(own[1], arrived[1], near[0]))
    far = [swap(array, *gather_steps[::-1]) for array in near]
    def box_sums(payload, olds, *waits, flops=1):
        kernel = functools.partial(scatter_kernel, plan, len(olds), plan.sy)
        shapes = [(4 * plan.share, VOX)] * plan.sy
        return small_call(kernel, shapes, "box_sums", payload, *olds, *waits, flops=flops)

    def added(arrays, pieces, flops=1):
        shape = (arrays[0].shape[0] // pieces, VOX)
        kernel = functools.partial(add_kernel, len(arrays))
        return small_call(kernel, [shape] * pieces, "added", *arrays, flops=flops)

    sums = [box_sums(near[0], []), box_sums(near[1], [], flops=LARGE)]
    pairs, waits = [], [sums[1][0]]
    for kind in range(2):
        parts = box_sums(far[kind], sums[kind], *waits, flops=LARGE if kind else 1)
        waits = [parts[0]]
        parts = [parts[0]] + [swap(parts[i], i * plan.sz) for i in range(1, plan.sy)]
        for even, odd in (reduce_steps, reduce_steps[::-1]):
            keep, give = added(parts, 2)
            parts = [keep, swap(give, even, odd)]
        pairs.append(parts)
    (value,) = added(pairs[0], 1, flops=LARGE)
    (own,) = small_call(intensity_kernel, [(plan.share, VOX)], "intensity", value, *pairs[1])
    flip_x, flip_y, flip_z = plan.flip_dev
    near = [own, swap(own, flip_z, flip_x), swap(own, flip_x, flip_z)]
    near.append(swap(near[1], flip_x, flip_z))
    far = [swap(array, flip_y) for array in near]
    ordered = [near[0], near[1], far[0], far[1], near[2], near[3], far[2], far[3]]
    shape = jax.ShapeDtypeStruct((plan.boxes, VOX), jnp.float32)
    (result,) = small_call(functools.partial(unfold_kernel, plan), [shape.shape], "unfold", *ordered[:-1], flops=LARGE)
    result = pl.pallas_call(
        functools.partial(last_kernel, plan, len(ordered) - 1),
        in_specs=[pl.BlockSpec(memory_space=pltpu.VMEM), pl.BlockSpec(memory_space=pl.ANY)],
        out_specs=pl.BlockSpec(memory_space=pl.ANY),
        out_shape=shape,
        scratch_shapes=[pltpu.VMEM((plan.share, VOX), jnp.float32), pltpu.SemaphoreType.DMA(())],
        input_output_aliases={1: 0},
        compiler_params=pltpu.CompilerParams(vmem_limit_bytes=VMEM_LIMIT),
        name="last",
    )(ordered[-1], result)
    return result.reshape(GX // plan.sx, GY // plan.sy, GZ // plan.sz, BOX_BRICK, VOX)


def solution(mesh):
    return jax.shard_map(
        functools.partial(shards, Plan(mesh)),
        mesh=mesh,
        in_specs=(
            P(AXES, None, None, None),
            P(AXES, None, None, None),
            P(AXES, None, None, None),
            P(),
            P(),
            P(AXES),
            P(AXES, None),
            P(AXES),
        ),
        out_specs=P("bx", "by", "bz", None, None),
        check_vma=False,
    )
```
